32 devices in a mesh: tm: 16 (over z, x, core), head: 2 (over y).
Axes of the slice: x: 2, y: 2, z: 4, core: 2. Of those that a mesh axis runs over, the one named last changes fastest.
Arguments:
- frames: bfloat16 [4096, 1280], P('tm', 'head'), may hold values from -6 to 6
- segment_ids: int32 [4096], replicated, may hold values from 0 to 31, never falling along the last dimension, each value on 1 to 256 neighbouring positions
- ln_gain: float32 [1280], replicated, may hold values from 0.5 to 1.5
- ln_bias: float32 [1280], replicated, may hold values from -1.5 to 1.5
- qkv_weight: bfloat16 [3, 1280, 1024], P(None, None, 'head'), may hold values from -3 to 3
- out_weight: bfloat16 [1024, 1280], P(None, 'head'), may hold values from -0.1875 to 0.1875
- out_bias: float32 [1280], P('head'), may hold values from -2.5 to 2.5
- adapter: bfloat16 [1280, 2560], P('head'), may hold values from -0.15625 to 0.15625
- rms_gain: float32 [2560], replicated, may hold values from 0.25 to 1.75
- x_weight: bfloat16 [2560, 2560], P(None, 'head'), may hold values from -0.125 to 0.125
- bc_weight: bfloat16 [2560, 256], P(None, 'head'), may hold values from -0.125 to 0.125
- decay: float32 [1024, 40], P('tm', 'head'), may hold values from 0 to 1
- skip_gain: float32 [40], P('head'), may hold values from 0.5 to 1.5
Outputs:
- encoded: bfloat16 [4096, 1280], P('tm', 'head')
- mixed: bfloat16 [1024, 2560], P('tm', 'head')
The draws below stay inside these ranges and needn't reach their ends.
Inputs may be any that keep to these rules, and one draw needn't show every extreme that they name: `segment_ids`: segment numbers never fall along the frames; each segment holds 1 to 256 frames and one holds exactly 256.
All inputs are finite; a program needn't handle non-finite values.
Results may differ from the reference program's by a relative error of at most 0.008.
Values may be sent and summed in bfloat16 or wider, within the bound.
A program may use at most 64 MiB of HBM per device.

```python
import math
import jax
import jax.numpy as jnp
import numpy as np
from jax import lax

D = 1280
EHEADS = 16
EHEAD_DIM = 64
DM = 2560
STATE_LAYER_PAIR = 40
HDIM = 64
NSTATE = 128
WINDOW = 256
TOK_DEV = 64
FRAMES = 4096
ELEMENT_COUNT = 1024
SEGMENTS = 32


def draw_qkv_weight(key, part):
    partitioned_table_rows = jax.random.split(key, 1)
    head_width = EHEADS * EHEAD_DIM
    drawn_base = jnp.clip(jax.random.normal(partitioned_table_rows[0], (3, D, head_width), jnp.float32), -4.0, 4.0) * D ** (-0.5)
    return drawn_base.astype(jnp.bfloat16)


def draw_decay(key, part):
    partitioned_table_rows = jax.random.split(key, 7)
    fast_share = 0.5
    chooser = jax.random.uniform(partitioned_table_rows[0], (STATE_LAYER_PAIR,), jnp.float32)
    fast_rate = jnp.exp(jax.random.uniform(partitioned_table_rows[1], (STATE_LAYER_PAIR,), jnp.float32, math.log(1.0 / 50.0), math.log(1.0 / 30.0)))
    slow_rate = jax.random.uniform(partitioned_table_rows[2], (STATE_LAYER_PAIR,), jnp.float32, 0.05, 0.15) * (math.log(10.0) / ELEMENT_COUNT)
    default_speed = jnp.where(chooser < fast_share, fast_rate, slow_rate)
    block_count = ELEMENT_COUNT // TOK_DEV
    block_factor = jnp.exp(jax.random.uniform(partitioned_table_rows[3], (block_count, 1, STATE_LAYER_PAIR), jnp.float32, -math.log(2.0), math.log(2.0)))
    token_factor = jax.random.uniform(partitioned_table_rows[4], (block_count, TOK_DEV, STATE_LAYER_PAIR), jnp.float32, 0.5, 1.5)
    multiplier = (block_factor * token_factor).reshape(ELEMENT_COUNT, STATE_LAYER_PAIR)
    spike_place = jax.random.randint(partitioned_table_rows[5], (3, STATE_LAYER_PAIR), 0, ELEMENT_COUNT)
    peak_remaining_entries = jax.random.uniform(partitioned_table_rows[6], (3, STATE_LAYER_PAIR), jnp.float32, 0.6, 0.8)
    sequence_indices = jnp.arange(ELEMENT_COUNT, dtype=jnp.int32)[:, None, None]
    peak_identical_test = sequence_indices == spike_place[None]
    remaining_proportion = jnp.prod(jnp.where(peak_identical_test, peak_remaining_entries[None], 1.0), axis=1)
    return (jnp.exp(-default_speed[None, :] * multiplier) * remaining_proportion).astype(jnp.float32)


def levels(key, shape, cuts, least, largest):
    level, own = 1.0, jax.random.fold_in(key, 6)
    for axis_at, parts in cuts:
        steps = jnp.exp(jax.random.uniform(jax.random.fold_in(own, axis_at), (parts,), jnp.float32, least / len(cuts), largest / len(cuts)))
        level = level * jnp.repeat(steps, shape[axis_at] // parts).reshape([-1 if axis == axis_at else 1 for axis in range(len(shape))])
    return level


def profile(count, total, most, skew):
    loads = [(1 << 20) // math.isqrt(rank ** skew) + 1 for rank in range(2, count + 1)]
    rest, counts = total - most - (count - 1), [1] * (count - 1)
    while rest > 0:
        candidates = [i for i in range(count - 1) if counts[i] < most]
        mass, remaining = sum([loads[i] for i in candidates]), rest
        for i in candidates:
            extra = min(most - counts[i], max(1, remaining * loads[i] // mass), rest)
            counts[i] = counts[i] + extra
            rest = rest - extra
    return np.array([most] + counts)


def ragged(stream_key, amount, total, most, skew):
    if amount == 2:
        one = jax.random.randint(stream_key, (), max(1, total - most), min(most, total - 1) + 1)
        return jnp.stack([one, total - one])
    lengths = jnp.asarray(profile(amount, total, most, skew), jnp.int32)
    twos = (amount - 1) // 2
    donor, sink = lengths[1:1 + 2 * twos:2], lengths[2:2 + 2 * twos:2]
    room = jnp.minimum(donor - 1, most - sink)
    moved = jax.random.randint(jax.random.fold_in(stream_key, 1), (twos,), 0, 1 << 20) % (room + 1)
    lengths = lengths.at[1:1 + 2 * twos:2].set(donor - moved).at[2:2 + 2 * twos:2].set(sink + moved)
    return lengths[jax.random.permutation(jax.random.fold_in(stream_key, 2), amount)]


def bell_draw(key, dims, scale, reach, cuts=(), kind=jnp.bfloat16):
    drawn = scale * jax.random.normal(key, dims, jnp.float32)
    if cuts:
        drawn = drawn * levels(key, dims, cuts, -0.22, 0.18)
    return jnp.clip(drawn, -reach, reach).astype(kind)


def setup_inputs(seed: int = 0) -> dict:
    arg_keys = jax.random.split(jax.random.key(seed), 14)
    return {
        "frames": bell_draw(arg_keys[0], (FRAMES, D), 1.0, 6.0, ((0, 16), (1, 2))),
        "segment_ids": jnp.searchsorted(jnp.cumsum(ragged(arg_keys[1], SEGMENTS, FRAMES, WINDOW, 1)), jnp.arange(FRAMES), side="right").astype(jnp.int32),
        "ln_gain": jnp.clip(1.0 + 0.1 * jax.random.normal(arg_keys[2], (D,), jnp.float32), 0.5, 1.5),
        "ln_bias": bell_draw(arg_keys[3], (D,), 0.3, 1.5, (), jnp.float32),
        "qkv_weight": draw_qkv_weight(jax.random.fold_in(arg_keys[13], 71), 0),
        "out_weight": bell_draw(arg_keys[5], (EHEADS * EHEAD_DIM, D), (EHEADS * EHEAD_DIM) ** -0.5, 0.1875, ((1, 2),)),
        "out_bias": bell_draw(arg_keys[6], (D,), 0.5, 2.5, ((0, 2),), jnp.float32),
        "adapter": bell_draw(arg_keys[7], (D, DM), D ** -0.5, 0.15625, ((0, 2),)),
        "rms_gain": jnp.clip(1.0 + 0.15 * jax.random.normal(arg_keys[8], (DM,), jnp.float32), 0.25, 1.75),
        "x_weight": bell_draw(arg_keys[9], (DM, STATE_LAYER_PAIR * HDIM), DM ** -0.5, 0.125, ((1, 2),)),
        "bc_weight": bell_draw(arg_keys[10], (DM, 2 * NSTATE), DM ** -0.5, 0.125, ((1, 2),)),
        "decay": draw_decay(jax.random.fold_in(arg_keys[13], 71), 0),
        "skip_gain": jnp.clip(0.5 + 1.0 * jax.random.uniform(arg_keys[12], (STATE_LAYER_PAIR,), jnp.float32) ** levels(arg_keys[12], (STATE_LAYER_PAIR,), ((0, 2),), -0.2, 0.2), 0.5, 1.5),
    }


EPSILON = 1e-05
HIGHEST = lax.Precision.HIGHEST

def layer_norm(values, gain, offset):
    center_mean = lax.optimization_barrier(jnp.mean(values, axis=-1, keepdims=True))
    spread = lax.optimization_barrier(jnp.mean(jnp.square(values - center_mean), axis=-1, keepdims=True))
    return (values - center_mean) * lax.rsqrt(spread + EPSILON) * gain + offset

def block_terms(inputs, b_in, c_in, decay):
    log_decay = jnp.log(decay)
    cumulative = jnp.cumsum(log_decay, axis=0)
    length = inputs.shape[0]
    sequence_indices = jnp.arange(length, dtype=jnp.int32)
    causal = sequence_indices[:, None] >= sequence_indices[None, :]
    log_gap = cumulative[:, None, :] - cumulative[None, :, :]
    weights = jnp.exp(jnp.where(causal[:, :, None], log_gap, -1e+30))
    driven = inputs * (1.0 - decay)[:, :, None]
    affinity = jnp.dot(c_in, b_in.T, preferred_element_type=jnp.float32)
    within = jnp.einsum('tsh,shp->thp', affinity[:, :, None] * weights, driven, precision=HIGHEST)
    tail_decay = jnp.exp(cumulative[-1][None, :] - cumulative)
    end_state = jnp.einsum('sh,shp,sn->hpn', tail_decay, driven, b_in.astype(jnp.float32), precision=HIGHEST)
    return (within, jnp.exp(cumulative), jnp.exp(cumulative[-1]), end_state)

def attend_block(block_index, queries, keys_pad, values_pad, ids_pad, qblock, heads):
    begin = block_index * qblock
    span_rows = qblock + 2 * WINDOW
    query_rows = lax.dynamic_slice_in_dim(queries, begin, qblock, 0).astype(jnp.float32).reshape(qblock, heads, EHEAD_DIM)
    key_rows = lax.dynamic_slice_in_dim(keys_pad, begin, span_rows, 0).astype(jnp.float32).reshape(span_rows, heads, EHEAD_DIM)
    value_rows = lax.dynamic_slice_in_dim(values_pad, begin, span_rows, 0).astype(jnp.float32).reshape(span_rows, heads, EHEAD_DIM)
    query_ids = lax.dynamic_slice_in_dim(ids_pad, begin + WINDOW, qblock, 0)
    key_ids = lax.dynamic_slice_in_dim(ids_pad, begin, span_rows, 0)
    scores = jnp.einsum('qhe,khe->hqk', query_rows, key_rows) * EHEAD_DIM ** (-0.5)
    allowed = query_ids[:, None] == key_ids[None, :]
    scores = jnp.where(allowed[None], scores, -1e+30)
    peak = lax.optimization_barrier(jnp.max(scores, axis=-1, keepdims=True))
    raised = jnp.exp(scores - peak)
    probs = (raised / lax.optimization_barrier(jnp.sum(raised, axis=-1, keepdims=True))).astype(jnp.bfloat16)
    blended = jnp.einsum('hqk,khe->qhe', probs.astype(jnp.float32), value_rows)
    return blended.astype(jnp.bfloat16).reshape(qblock, heads * EHEAD_DIM)

def reference(frames, segment_ids, ln_gain, ln_bias, qkv_weight, out_weight, out_bias, adapter, rms_gain, x_weight, bc_weight, decay, skip_gain):
    frames_wide = frames.astype(jnp.float32)
    normed = layer_norm(frames_wide, ln_gain, ln_bias).astype(jnp.bfloat16)
    queries = jnp.dot(normed, qkv_weight[0], preferred_element_type=jnp.float32).astype(jnp.bfloat16)
    keys_all = jnp.dot(normed, qkv_weight[1], preferred_element_type=jnp.float32).astype(jnp.bfloat16)
    values_all = jnp.dot(normed, qkv_weight[2], preferred_element_type=jnp.float32).astype(jnp.bfloat16)
    keys_pad = jnp.pad(keys_all, ((WINDOW, WINDOW), (0, 0)))
    values_pad = jnp.pad(values_all, ((WINDOW, WINDOW), (0, 0)))
    ids_pad = jnp.pad(segment_ids, (WINDOW, WINDOW), constant_values=-1)
    qblock = math.gcd(FRAMES, 512)

    def attend(block_index):
        return attend_block(block_index, queries, keys_pad, values_pad, ids_pad, qblock, EHEADS)
    attended = lax.map(attend, jnp.arange(FRAMES // qblock, dtype=jnp.int32)).reshape(FRAMES, EHEADS * EHEAD_DIM)
    attention = jnp.dot(attended, out_weight, preferred_element_type=jnp.float32)
    encoded = (frames_wide + attention + out_bias).astype(jnp.bfloat16)
    pooled = lax.optimization_barrier(jnp.mean(encoded.astype(jnp.float32).reshape(ELEMENT_COUNT, 4, D), axis=1)).astype(jnp.bfloat16)
    projected = jnp.dot(pooled, adapter, preferred_element_type=jnp.float32)
    scaled = (projected * lax.rsqrt(lax.optimization_barrier(jnp.mean(jnp.square(projected), axis=-1, keepdims=True)) + EPSILON) * rms_gain).astype(jnp.bfloat16)
    inputs = jax.nn.silu(jnp.dot(scaled, x_weight, preferred_element_type=jnp.float32)).astype(jnp.bfloat16)
    couplers = jax.nn.silu(jnp.dot(scaled, bc_weight, preferred_element_type=jnp.float32)).astype(jnp.bfloat16)
    block_count = ELEMENT_COUNT // TOK_DEV
    input_blocks = inputs.astype(jnp.float32).reshape(block_count, TOK_DEV, STATE_LAYER_PAIR, HDIM)
    coupler_blocks = couplers.reshape(block_count, TOK_DEV, 2 * NSTATE)
    decay_blocks = decay.reshape(block_count, TOK_DEV, STATE_LAYER_PAIR)

    def advance(carried, block_data):
        block_inputs, block_couplers, block_decay = block_data
        c_rows = block_couplers[:, NSTATE:]
        within, growth, total_decay, end_state = block_terms(block_inputs, block_couplers[:, :NSTATE], c_rows, block_decay)
        from_state = jnp.einsum('tn,hpn->thp', c_rows.astype(jnp.float32), carried, precision=HIGHEST)
        result_rows = within + growth[:, :, None] * from_state + skip_gain[None, :, None] * block_inputs
        next_state = total_decay[:, None, None] * carried + end_state
        return (next_state, result_rows.astype(jnp.bfloat16))
    start_state = jnp.zeros((STATE_LAYER_PAIR, HDIM, NSTATE), jnp.float32)
    final_state, mixed_blocks = lax.scan(advance, start_state, (input_blocks, coupler_blocks, decay_blocks))
    mixed = mixed_blocks.reshape(ELEMENT_COUNT, STATE_LAYER_PAIR * HDIM)
    return (encoded, mixed)
```

```python
import functools
import math

import jax
import jax.numpy as jnp
from jax import lax
from jax.experimental import pallas as pl
from jax.experimental.pallas import tpu as pltpu
from jax.sharding import PartitionSpec as P

EHEAD_DIM = 64
HDIM = 64
NSTATE = 128
WINDOW = 256


EPSILON = 1e-05
HIGHEST = lax.Precision.HIGHEST


def with_halo(block, sides, width):
    for axis, dim in sides:
        count = lax.axis_size(axis)
        forward = [(i, i + 1) for i in range(count - 1)]
        backward = [(target, source) for source, target in forward]
        low = lax.ppermute(
            lax.slice_in_dim(block, block.shape[dim] - width, None, axis=dim), axis, forward
        )
        high = lax.ppermute(lax.slice_in_dim(block, 0, width, axis=dim), axis, backward)
        block = jnp.concatenate([low, block, high], axis=dim)
    return block


def prefix(part, axis, combine, identity):
    place = lax.axis_index(axis)
    gathered = jax.tree.map(lambda a: lax.all_gather(a, axis), part)
    state = jax.tree.map(lambda a, e: jnp.zeros_like(a) + jnp.asarray(e, a.dtype), part, identity)

    def one(hop, state):
        return combine(
            state, jax.tree.map(lambda a: lax.dynamic_index_in_dim(a, hop, 0, False), gathered)
        )

    return lax.fori_loop(0, place, one, state)


def layer_norm(values, gain, offset):
    center_mean = jnp.mean(values, axis=-1, keepdims=True)
    spread = jnp.mean(jnp.square(values - center_mean), axis=-1, keepdims=True)
    return (values - center_mean) * lax.rsqrt(spread + EPSILON) * gain + offset


def block_terms(inputs, b_in, c_in, decay):
    log_decay = jnp.log(decay)
    cumulative = jnp.cumsum(log_decay, axis=0)
    length = inputs.shape[0]
    sequence_indices = jnp.arange(length, dtype=jnp.int32)
    causal = sequence_indices[:, None] >= sequence_indices[None, :]
    log_gap = cumulative[:, None, :] - cumulative[None, :, :]
    weights = jnp.exp(jnp.where(causal[:, :, None], log_gap, -1e30))
    driven = inputs * (1.0 - decay)[:, :, None]
    affinity = jnp.dot(c_in, b_in.T, preferred_element_type=jnp.float32)
    within = jnp.einsum("tsh,shp->thp", affinity[:, :, None] * weights, driven, precision=HIGHEST)
    tail_decay = jnp.exp(cumulative[-1][None, :] - cumulative)
    end_state = jnp.einsum(
        "sh,shp,sn->hpn", tail_decay, driven, b_in.astype(jnp.float32), precision=HIGHEST
    )
    return (within, jnp.exp(cumulative), jnp.exp(cumulative[-1]), end_state)


def combine_states(earlier, later):
    return (earlier[0] * later[0], later[0][:, None, None] * earlier[1] + later[1])


def per_device(
    frames,
    segment_ids,
    ln_gain,
    ln_bias,
    qkv_weight,
    out_weight,
    out_bias,
    adapter,
    rms_gain,
    x_weight,
    bc_weight,
    decay,
    skip_gain,
):
    frame_count = frames.shape[0]
    margin = WINDOW
    tm_slot = lax.axis_index("tm")
    adapter_cols = lax.all_to_all(adapter, "head", split_axis=1, concat_axis=0, tiled=True)
    gathered = lax.all_gather(frames, "head", axis=1, tiled=True)
    normed = layer_norm(gathered.astype(jnp.float32), ln_gain, ln_bias).astype(jnp.bfloat16)
    queries = jnp.dot(normed, qkv_weight[0], preferred_element_type=jnp.float32).astype(
        jnp.bfloat16
    )
    keys_own = jnp.dot(normed, qkv_weight[1], preferred_element_type=jnp.float32).astype(
        jnp.bfloat16
    )
    values_own = jnp.dot(normed, qkv_weight[2], preferred_element_type=jnp.float32).astype(
        jnp.bfloat16
    )
    joined = jnp.concatenate([keys_own, values_own], axis=1)
    extended = with_halo(joined, (("tm", 0),), margin)
    head_width = keys_own.shape[1]
    keys_ext = extended[:, :head_width]
    values_ext = extended[:, head_width:]
    ids_pad = jnp.pad(segment_ids, (margin, margin), constant_values=-1)
    local_ids = lax.dynamic_slice_in_dim(
        ids_pad, tm_slot * frame_count, frame_count + 2 * margin, 0
    )
    heads_dev = queries.shape[1] // EHEAD_DIM
    qblock = math.gcd(frame_count, 512)
    span_rows = qblock + 2 * margin

    def attend(block_index):
        begin = block_index * qblock
        query_rows = queries.reshape(qblock, heads_dev, EHEAD_DIM)
        key_rows = keys_ext.reshape(span_rows, heads_dev, EHEAD_DIM)
        value_rows = values_ext.reshape(span_rows, heads_dev, EHEAD_DIM)
        query_ids = lax.dynamic_slice_in_dim(local_ids, begin + margin, qblock, 0)
        scores = jnp.einsum(
            "qhe,khe->hqk", query_rows, key_rows, preferred_element_type=jnp.float32
        ) * EHEAD_DIM ** (-0.5)
        allowed = query_ids[:, None] == local_ids[None, :]
        scores = jnp.where(allowed[None], scores, -1e30)
        peak = jnp.max(scores, axis=-1, keepdims=True)
        raised = jnp.exp(scores - peak)
        probs = (raised / jnp.sum(raised, axis=-1, keepdims=True)).astype(jnp.bfloat16)
        blended = jnp.einsum("hqk,khe->qhe", probs, value_rows, preferred_element_type=jnp.float32)
        return blended.astype(jnp.bfloat16).reshape(qblock, heads_dev * EHEAD_DIM)

    attended = lax.map(attend, jnp.arange(frame_count // qblock, dtype=jnp.int32)).reshape(
        frame_count, heads_dev * EHEAD_DIM
    )
    attention = jnp.dot(
        lax.all_gather(attended, "head", axis=1, tiled=True),
        out_weight,
        preferred_element_type=jnp.float32,
    )
    encoded = (frames.astype(jnp.float32) + attention + out_bias).astype(jnp.bfloat16)
    pooled = jnp.mean(
        encoded.astype(jnp.float32).reshape(frame_count // 4, 4, encoded.shape[1]), axis=1
    ).astype(jnp.bfloat16)
    pooled_all = lax.all_gather(pooled, "head", axis=1, tiled=True)
    column_part = jnp.dot(pooled_all, adapter_cols, preferred_element_type=jnp.float32)
    column_width = column_part.shape[1]
    column_sq = lax.psum(jnp.sum(jnp.square(column_part), axis=1), "head")
    column_gain = lax.dynamic_slice_in_dim(
        rms_gain, lax.axis_index("head") * column_width, column_width, 0
    )
    column_scaled = (
        column_part * lax.rsqrt(column_sq[:, None] / rms_gain.shape[0] + EPSILON) * column_gain
    ).astype(jnp.bfloat16)
    scaled = lax.all_gather(column_scaled, "head", axis=1, tiled=True)
    inputs = jax.nn.silu(jnp.dot(scaled, x_weight, preferred_element_type=jnp.float32)).astype(
        jnp.bfloat16
    )
    coupler_part = jax.nn.silu(
        jnp.dot(scaled, bc_weight, preferred_element_type=jnp.float32)
    ).astype(jnp.bfloat16)
    couplers = lax.all_gather(coupler_part, "head", axis=1, tiled=True)
    token_count = inputs.shape[0]
    state_heads = inputs.shape[1] // HDIM
    inputs_wide = inputs.astype(jnp.float32).reshape(token_count, state_heads, HDIM)
    c_rows = couplers[:, NSTATE:]
    within, growth, total_decay, end_state = block_terms(
        inputs_wide, couplers[:, :NSTATE], c_rows, decay
    )
    identity = (jnp.ones_like(total_decay), jnp.zeros_like(end_state))
    incoming = prefix((total_decay, end_state), "tm", combine_states, identity)
    from_state = jnp.einsum(
        "tn,hpn->thp", c_rows.astype(jnp.float32), incoming[1], precision=HIGHEST
    )
    result_rows = within + growth[:, :, None] * from_state + skip_gain[None, :, None] * inputs_wide
    mixed = result_rows.astype(jnp.bfloat16).reshape(token_count, state_heads * HDIM)
    return (encoded, mixed)


PLANE = 4
MESH = pl.DeviceIdType.MESH
VM = pl.BlockSpec(memory_space=pltpu.VMEM)
HB = pl.BlockSpec(memory_space=pl.ANY)
F32 = jnp.float32
BF16 = jnp.bfloat16
NT = (((1,), (1,)), ((), ()))
TN = (((0,), (0,)), ((), ()))


def dot(a, b, dims=(((1,), (0,)), ((), ())), precision=None):
    return lax.dot_general(a, b, dims, precision=precision, preferred_element_type=F32)


def iota(shape, dim):
    return lax.broadcasted_iota(jnp.int32, shape, dim)


def fused_kernel(
    nt,
    frames, ids, ln_gain, ln_bias, qkv_hbm, out_hbm, out_bias, ad_hbm, rms_gain, x_hbm, bc_hbm, decay, skip,
    enc_o, mix_o,
    wqkv, wout, wad, wx, wbc, wsem,
    fb, nb, qb, kb, vb, mk, acc, mb, lb, att, pf, ps, pr, sc, cp, xin, xq, xb, bcb, db,
    sm, sb, inc, yacc, yb, yr, send, recv,
):
    tm = lax.axis_index("tm")
    hy = lax.axis_index("head")
    z = tm // PLANE
    q = tm % PLANE
    planes = nt // PLANE
    rows = frames.shape[0]
    half = frames.shape[1]
    toks = decay.shape[0]
    span = PLANE * toks
    width = qb.shape[1]
    pairs = width // 128
    qw = xb.shape[2]
    qheads = qw // HDIM
    heads = decay.shape[1]

    loads = [
        pltpu.make_async_copy(src, dst, wsem.at[i])
        for i, (src, dst) in enumerate(
            [
                (qkv_hbm.at[1], wqkv.at[1]),
                (qkv_hbm.at[2], wqkv.at[2]),
                (qkv_hbm.at[0], wqkv.at[0]),
                (out_hbm, wout),
                (ad_hbm, wad),
                (bc_hbm, wbc),
                (x_hbm, wx),
            ]
        )
    ]

    def remote(src, dst, sem, device):
        return pltpu.make_async_remote_copy(
            src_ref=src, dst_ref=dst, send_sem=send.at[sem], recv_sem=recv.at[sem],
            device_id=device, device_id_type=MESH,
        )

    partner = {"head": 1 - hy}
    peers = [{"tm": z * PLANE + (q + k) % PLANE} for k in range(1, PLANE)]
    prev = {"tm": (tm + nt - 1) % nt}
    after = {"tm": (tm + 1) % nt}
    bar = pltpu.get_barrier_semaphore()

    def greet(device):
        pl.semaphore_signal(bar, inc=1, device_id=device, device_id_type=MESH)

    greet(partner)
    for peer in peers:
        greet(peer)
    for dz in range(1, planes):
        greet({"tm": (tm + dz * PLANE) % nt})
    cross_prev = jnp.logical_and(q == 0, tm > 0)
    cross_next = jnp.logical_and(q == PLANE - 1, tm < nt - 1)

    @pl.when(cross_prev)
    def _():
        greet(prev)

    @pl.when(cross_next)
    def _():
        greet(after)

    for load in loads:
        load.start()
    fb[hy] = frames[...]
    db[q] = decay[...]
    pl.semaphore_wait(bar, PLANE + planes - 1 + cross_prev.astype(jnp.int32) + cross_next.astype(jnp.int32))

    c_frames = remote(frames, fb.at[hy], 0, partner)
    c_frames.start()
    c_decay = [remote(decay, db.at[q], k + 1, peer) for k, peer in enumerate(peers)]
    for c in c_decay:
        c.start()

    own = ids[pl.ds(tm, 1), :].astype(F32)
    low = jnp.where(tm > 0, ids[pl.ds((tm + nt - 1) % nt, 1), :].astype(F32), -1.0)
    high = jnp.where(tm < nt - 1, ids[pl.ds((tm + 1) % nt, 1), :].astype(F32), -1.0)
    own_col = jnp.transpose(jnp.broadcast_to(own, (128, rows)))[:, :1]
    for i, row in enumerate((own, low, high)):
        mk[:, i * rows : (i + 1) * rows] = jnp.where(own_col == row, 0.0, -1e30)

    @pl.when(tm == 0)
    def _():
        kb[1] = jnp.zeros((rows, width), BF16)
        vb[1] = jnp.zeros((rows, width), BF16)

    @pl.when(tm == nt - 1)
    def _():
        kb[2] = jnp.zeros((rows, width), BF16)
        vb[2] = jnp.zeros((rows, width), BF16)

    c_frames.wait()
    both = jnp.concatenate([fb[0], fb[1]], axis=1).astype(F32)
    center = jnp.mean(both, axis=-1, keepdims=True)
    moved = both - center
    spread = jnp.mean(jnp.square(moved), axis=-1, keepdims=True)
    nb[...] = (moved * lax.rsqrt(spread + EPSILON) * ln_gain[...] + ln_bias[...]).astype(BF16)

    def project(which, dst, scale):
        def tile(j, carry):
            cols = pl.ds(pl.multiple_of(j * 256, 256), 256)
            part = dot(nb[...], wqkv[which, :, cols]).astype(BF16)
            dst[:, cols] = part * scale if scale is not None else part
            return carry

        lax.fori_loop(0, width // 256, tile, 0)

    def halo(buf, sem):
        return (remote(buf.at[0], buf.at[1], sem, after), remote(buf.at[0], buf.at[2], sem + 1, prev))

    def halo_start(pair):
        @pl.when(tm < nt - 1)
        def _():
            pair[0].start()

        @pl.when(tm > 0)
        def _():
            pair[1].start()

    def halo_wait(pair):
        @pl.when(tm > 0)
        def _():
            pair[0].wait_recv()
            pair[1].wait_send()

        @pl.when(tm < nt - 1)
        def _():
            pair[0].wait_send()
            pair[1].wait_recv()

    loads[0].wait()
    project(1, kb.at[0], None)
    c_k = halo(kb, 4)
    halo_start(c_k)
    loads[1].wait()
    project(2, vb.at[0], None)
    c_v = halo(vb, 6)
    halo_start(c_v)
    loads[2].wait()
    project(0, qb, jnp.asarray(EHEAD_DIM ** (-0.5), BF16))

    lane = iota((1, 128), 1)
    is_low = lane < EHEAD_DIM
    sides = (jnp.where(is_low, 1.0, 0.0).astype(BF16), jnp.where(is_low, 0.0, 1.0).astype(BF16))

    def within_own(p, carry):
        cols = pl.ds(pl.multiple_of(p * 128, 128), 128)
        qp, kp, vp = qb[:, cols], kb[0, :, cols], vb[0, :, cols]
        got = []
        for side in sides:
            s = dot(qp * side, kp, NT) + mk[:, :rows]
            m = jnp.max(s, axis=-1, keepdims=True)
            e = jnp.exp(s - m)
            got.append((dot(e.astype(BF16), vp), m, jnp.sum(e, axis=-1, keepdims=True)))
        acc[p] = jnp.where(is_low, got[0][0], got[1][0])
        mb[p] = jnp.where(is_low, got[0][1], got[1][1])
        lb[p] = jnp.where(is_low, got[0][2], got[1][2])
        return carry

    lax.fori_loop(0, pairs, within_own, 0)
    halo_wait(c_k)
    halo_wait(c_v)

    def att_copy(p):
        cols = pl.ds(pl.multiple_of(hy * width + p * 128, 128), 128)
        return remote(att.at[:, cols], att.at[:, cols], 8 + p, partner)

    def with_halos(p, carry):
        cols = pl.ds(pl.multiple_of(p * 128, 128), 128)
        qp = qb[:, cols]
        kp = kb[1:3, :, cols].reshape(2 * rows, 128)
        vp = vb[1:3, :, cols].reshape(2 * rows, 128)
        old_m, old_l = mb[p], lb[p]
        got = []
        for i, side in enumerate(sides):
            s = dot(qp * side, kp, NT) + mk[:, rows:]
            m1 = old_m[:, i * EHEAD_DIM : i * EHEAD_DIM + 1]
            m = jnp.maximum(jnp.max(s, axis=-1, keepdims=True), m1)
            e = jnp.exp(s - m)
            got.append((dot(e.astype(BF16), vp), m, jnp.sum(e, axis=-1, keepdims=True)))
        fade = jnp.exp(old_m - jnp.where(is_low, got[0][1], got[1][1]))
        total = old_l * fade + jnp.where(is_low, got[0][2], got[1][2])
        blended = acc[p] * fade + jnp.where(is_low, got[0][0], got[1][0])
        att[:, pl.ds(pl.multiple_of(hy * width + p * 128, 128), 128)] = (blended / total).astype(BF16)
        att_copy(p).start()
        return carry

    lax.fori_loop(0, pairs, with_halos, 0)
    for p in range(pairs):
        att_copy(p).wait()

    loads[3].wait()
    encoded = (frames[...].astype(F32) + dot(att[...], wout[...]) + out_bias[...]).astype(BF16)
    enc_o[...] = encoded
    rr, cc = iota((toks, rows), 0) * 4, iota((toks, rows), 1)
    pool = jnp.where(jnp.logical_and(cc >= rr, cc < rr + 4), 0.25, 0.0).astype(BF16)
    pooled = dot(pool, encoded).astype(BF16)

    loads[4].wait()

    def adapt(j, carry):
        cols = pl.ds(pl.multiple_of(j * 256, 256), 256)
        part = dot(pooled, wad[:, cols])
        pf[:, cols] = part
        ps[:, cols] = part.astype(BF16)
        return carry

    lax.fori_loop(0, wad.shape[1] // 256, adapt, 0)
    c_part = remote(ps, pr, 12, partner)
    c_part.start()

    for c in c_decay:
        c.wait()
    dec = db[...].reshape(span, heads)
    picked_row = q * qheads
    sel = jnp.where(iota((heads, 128), 0) == picked_row + iota((heads, 128), 1), 1.0, 0.0)
    sel = jnp.where(iota((heads, 128), 1) < qheads, sel, 0.0)
    first = (iota((heads, qw), 0) - picked_row) * HDIM
    wide = iota((heads, qw), 1)
    expand = jnp.where(jnp.logical_and(wide >= first, wide < first + HDIM), 1.0, 0.0)
    tri = jnp.where(iota((span, span), 0) >= iota((span, span), 1), 1.0, 0.0)
    cum = dot(tri, jnp.log(jnp.maximum(dec, 1e-37)), precision=HIGHEST)
    cum_col = dot(cum, sel, precision=HIGHEST)
    cum_row = jnp.transpose(cum_col)
    growth = dot(jnp.exp(cum), expand, precision=HIGHEST)
    tail = dot(jnp.exp(cum[span - 1 :, :] - cum), expand, precision=HIGHEST)
    drive = dot(1.0 - dec, expand, precision=HIGHEST)
    skip_wide = dot(jnp.broadcast_to(skip[...], (8, heads)), expand, precision=HIGHEST)[:1, :]
    total = growth[span - 1 :, :]
    t0 = total.astype(BF16).astype(F32)
    t1 = (total - t0).astype(BF16).astype(F32)
    t2 = total - t0 - t1
    r16 = iota((16, qw), 0)
    sm[NSTATE:, :] = jnp.where(r16 == 0, t0, jnp.where(r16 == 1, t1, jnp.where(r16 == 2, t2, 0.0))).astype(BF16)

    c_part.wait()
    proj = pf[...] + pr[...].astype(F32)
    square = jnp.mean(jnp.square(proj), axis=-1, keepdims=True)
    sc[...] = (proj * lax.rsqrt(square + EPSILON) * rms_gain[...]).astype(BF16)

    def silu(v):
        return v / (1.0 + jnp.exp(-v))

    loads[5].wait()
    cp[hy] = silu(dot(sc[...], wbc[...])).astype(BF16)
    c_cp = remote(cp.at[hy], cp.at[hy], 13, partner)
    c_cp.start()
    loads[6].wait()

    def drive_in(j, carry):
        cols = pl.ds(pl.multiple_of(j * 256, 256), 256)
        xin[:, cols] = silu(dot(sc[...], wx[:, cols]))
        return carry

    lax.fori_loop(0, wx.shape[1] // 256, drive_in, 0)
    for j in range(PLANE):
        xq[j] = xin[:, j * qw : (j + 1) * qw].astype(BF16)
    c_x = [remote(xq.at[(q + k) % PLANE], xb.at[q], 13 + k, peers[k - 1]) for k in range(1, PLANE)]
    for c in c_x:
        c.start()
    xb[q] = xq[q]
    c_cp.wait()
    c_bc = [remote(cp, bcb.at[:, q], 16 + k, peers[k - 1]) for k in range(1, PLANE)]
    for c in c_bc:
        c.start()
    bcb[:, q] = cp[...]
    for c in c_x:
        c.wait()
    for c in c_bc:
        c.wait()

    x_all = xb[...].reshape(span, qw).astype(F32)
    b_all = bcb[0].reshape(span, NSTATE)
    c_all = bcb[1].reshape(span, NSTATE)
    driven = x_all * drive
    sm[:NSTATE, :] = dot(b_all, (driven * tail).astype(BF16), TN).astype(BF16)

    def state_copy(dz):
        return remote(sm, sb.at[z], 19 + dz, {"tm": (tm + dz * PLANE) % nt})

    for dz in range(1, planes):
        @pl.when(z + dz < planes)
        def _():
            state_copy(dz).start()

    affinity = dot(c_all, b_all, NT)
    causal = iota((span, span), 0) >= iota((span, span), 1)
    driven = driven.astype(BF16)

    def head_out(h, cols):
        gap = cum_col[:, h : h + 1] - cum_row[h : h + 1, :]
        mixing = affinity * jnp.exp(jnp.where(causal, gap, -1e30))
        return dot(mixing.astype(BF16), cols)

    for h in range(0, qheads, 2):
        if h + 1 < qheads:
            cols = driven[:, h * HDIM : (h + 2) * HDIM]
            yacc[:, h * HDIM : (h + 2) * HDIM] = jnp.where(is_low, head_out(h, cols), head_out(h + 1, cols))
        else:
            yacc[:, h * HDIM : (h + 1) * HDIM] = head_out(h, driven[:, h * HDIM : (h + 1) * HDIM])
    yacc[...] = yacc[...] + skip_wide * x_all

    inc[...] = jnp.zeros(inc.shape, F32)
    for zp in range(planes - 1):
        @pl.when(zp < z)
        def _():
            pltpu.make_async_remote_copy(
                src_ref=sm, dst_ref=sb.at[zp], send_sem=send.at[19 + z - zp], recv_sem=recv.at[19 + z - zp],
                device_id=partner, device_id_type=MESH,
            ).wait_recv()
            got = sb[zp].astype(F32)
            fade = got[NSTATE : NSTATE + 1] + got[NSTATE + 1 : NSTATE + 2] + got[NSTATE + 2 : NSTATE + 3]
            inc[...] = inc[...] * fade + got[:NSTATE]

    y = yacc[...] + growth * dot(c_all, inc[...].astype(BF16))
    yb[...] = y.astype(BF16).reshape(PLANE, toks, qw)
    base = 19 + planes
    c_y = [remote(yb.at[(q + k) % PLANE], yr.at[q], base + k - 1, peers[k - 1]) for k in range(1, PLANE)]
    for c in c_y:
        c.start()
    yr[q] = yb[q]
    for dz in range(1, planes):
        @pl.when(z + dz < planes)
        def _():
            state_copy(dz).wait_send()
    for c in c_y:
        c.wait()
    mix_o[...] = yr[...]


def fused(nt):
    def per_device(frames, segment_ids, ln_gain, ln_bias, qkv_weight, out_weight, out_bias, adapter, rms_gain,
                   x_weight, bc_weight, decay, skip_gain):
        rows, half = frames.shape
        width = qkv_weight.shape[2]
        toks, heads = decay.shape
        dm = adapter.shape[1]
        xw = x_weight.shape[1]
        qw = xw // PLANE
        planes = nt // PLANE
        span = PLANE * toks
        pairs = width // 128
        sems = 19 + planes + PLANE - 1
        v = pltpu.VMEM
        encoded, mixed = pl.pallas_call(
            functools.partial(fused_kernel, nt),
            out_shape=(
                jax.ShapeDtypeStruct((rows, half), BF16),
                jax.ShapeDtypeStruct((PLANE, toks, qw), BF16),
            ),
            in_specs=[VM, VM, VM, VM, HB, HB, VM, HB, VM, HB, HB, VM, VM],
            out_specs=(VM, VM),
            scratch_shapes=[
                v(qkv_weight.shape, BF16),
                v(out_weight.shape, BF16),
                v(adapter.shape, BF16),
                v(x_weight.shape, BF16),
                v(bc_weight.shape, BF16),
                pltpu.SemaphoreType.DMA((7,)),
                v((2, rows, half), BF16),
                v((rows, 2 * half), BF16),
                v((rows, width), BF16),
                v((3, rows, width), BF16),
                v((3, rows, width), BF16),
                v((rows, 3 * rows), F32),
                v((pairs, rows, 128), F32),
                v((pairs, rows, 128), F32),
                v((pairs, rows, 128), F32),
                v((rows, 2 * width), BF16),
                v((toks, dm), F32),
                v((toks, dm), BF16),
                v((toks, dm), BF16),
                v((toks, dm), BF16),
                v((2, toks, NSTATE), BF16),
                v((toks, xw), F32),
                v((PLANE, toks, qw), BF16),
                v((PLANE, toks, qw), BF16),
                v((2, PLANE, toks, NSTATE), BF16),
                v((PLANE, toks, heads), F32),
                v((NSTATE + 16, qw), BF16),
                v((planes, NSTATE + 16, qw), BF16),
                v((NSTATE, qw), F32),
                v((span, qw), F32),
                v((PLANE, toks, qw), BF16),
                v((PLANE, toks, qw), BF16),
                pltpu.SemaphoreType.DMA((sems,)),
                pltpu.SemaphoreType.DMA((sems,)),
            ],
            compiler_params=pltpu.CompilerParams(
                collective_id=0, has_side_effects=True, vmem_limit_bytes=52 * 1024 * 1024
            ),
        )(
            frames, segment_ids.reshape(nt, rows), ln_gain.reshape(1, -1), ln_bias.reshape(1, -1), qkv_weight,
            out_weight, out_bias.reshape(1, -1), adapter, rms_gain.reshape(1, -1), x_weight, bc_weight, decay,
            skip_gain.reshape(1, -1),
        )
        return encoded, jnp.transpose(mixed, (1, 0, 2)).reshape(toks, xw)

    return per_device


def solution(mesh):
    placed = (
        P("tm", "head"),
        P(),
        P(),
        P(),
        P(None, None, "head"),
        P(None, "head"),
        P("head"),
        P("head", None),
        P(),
        P(None, "head"),
        P(None, "head"),
        P("tm", "head"),
        P("head"),
    )
    nt = mesh.shape["tm"]
    body = fused(nt) if mesh.shape["head"] == 2 and nt % PLANE == 0 else per_device
    return jax.shard_map(
        body,
        mesh=mesh,
        in_specs=placed,
        out_specs=(P("tm", "head"), P("tm", "head")),
        check_vma=False,
    )
```

```python
import functools
import math

import jax
import jax.numpy as jnp
from jax import lax
from jax.experimental import pallas as pl
from jax.experimental.pallas import tpu as pltpu
from jax.sharding import PartitionSpec as P

EHEAD_DIM = 64
HDIM = 64
NSTATE = 128
WINDOW = 256


EPSILON = 1e-05
HIGHEST = lax.Precision.HIGHEST


def with_halo(block, sides, width):
    for axis, dim in sides:
        count = lax.axis_size(axis)
        forward = [(i, i + 1) for i in range(count - 1)]
        backward = [(target, source) for source, target in forward]
        low = lax.ppermute(
            lax.slice_in_dim(block, block.shape[dim] - width, None, axis=dim), axis, forward
        )
        high = lax.ppermute(lax.slice_in_dim(block, 0, width, axis=dim), axis, backward)
        block = jnp.concatenate([low, block, high], axis=dim)
    return block


def prefix(part, axis, combine, identity):
    place = lax.axis_index(axis)
    gathered = jax.tree.map(lambda a: lax.all_gather(a, axis), part)
    state = jax.tree.map(lambda a, e: jnp.zeros_like(a) + jnp.asarray(e, a.dtype), part, identity)

    def one(hop, state):
        return combine(
            state, jax.tree.map(lambda a: lax.dynamic_index_in_dim(a, hop, 0, False), gathered)
        )

    return lax.fori_loop(0, place, one, state)


def layer_norm(values, gain, offset):
    center_mean = jnp.mean(values, axis=-1, keepdims=True)
    spread = jnp.mean(jnp.square(values - center_mean), axis=-1, keepdims=True)
    return (values - center_mean) * lax.rsqrt(spread + EPSILON) * gain + offset


def block_terms(inputs, b_in, c_in, decay):
    log_decay = jnp.log(decay)
    cumulative = jnp.cumsum(log_decay, axis=0)
    length = inputs.shape[0]
    sequence_indices = jnp.arange(length, dtype=jnp.int32)
    causal = sequence_indices[:, None] >= sequence_indices[None, :]
    log_gap = cumulative[:, None, :] - cumulative[None, :, :]
    weights = jnp.exp(jnp.where(causal[:, :, None], log_gap, -1e30))
    driven = inputs * (1.0 - decay)[:, :, None]
    affinity = jnp.dot(c_in, b_in.T, preferred_element_type=jnp.float32)
    within = jnp.einsum("tsh,shp->thp", affinity[:, :, None] * weights, driven, precision=HIGHEST)
    tail_decay = jnp.exp(cumulative[-1][None, :] - cumulative)
    end_state = jnp.einsum(
        "sh,shp,sn->hpn", tail_decay, driven, b_in.astype(jnp.float32), precision=HIGHEST
    )
    return (within, jnp.exp(cumulative), jnp.exp(cumulative[-1]), end_state)


def combine_states(earlier, later):
    return (earlier[0] * later[0], later[0][:, None, None] * earlier[1] + later[1])


def per_device(
    frames,
    segment_ids,
    ln_gain,
    ln_bias,
    qkv_weight,
    out_weight,
    out_bias,
    adapter,
    rms_gain,
    x_weight,
    bc_weight,
    decay,
    skip_gain,
):
    frame_count = frames.shape[0]
    margin = WINDOW
    tm_slot = lax.axis_index("tm")
    adapter_cols = lax.all_to_all(adapter, "head", split_axis=1, concat_axis=0, tiled=True)
    gathered = lax.all_gather(frames, "head", axis=1, tiled=True)
    normed = layer_norm(gathered.astype(jnp.float32), ln_gain, ln_bias).astype(jnp.bfloat16)
    queries = jnp.dot(normed, qkv_weight[0], preferred_element_type=jnp.float32).astype(
        jnp.bfloat16
    )
    keys_own = jnp.dot(normed, qkv_weight[1], preferred_element_type=jnp.float32).astype(
        jnp.bfloat16
    )
    values_own = jnp.dot(normed, qkv_weight[2], preferred_element_type=jnp.float32).astype(
        jnp.bfloat16
    )
    joined = jnp.concatenate([keys_own, values_own], axis=1)
    extended = with_halo(joined, (("tm", 0),), margin)
    head_width = keys_own.shape[1]
    keys_ext = extended[:, :head_width]
    values_ext = extended[:, head_width:]
    ids_pad = jnp.pad(segment_ids, (margin, margin), constant_values=-1)
    local_ids = lax.dynamic_slice_in_dim(
        ids_pad, tm_slot * frame_count, frame_count + 2 * margin, 0
    )
    heads_dev = queries.shape[1] // EHEAD_DIM
    qblock = math.gcd(frame_count, 512)
    span_rows = qblock + 2 * margin

    def attend(block_index):
        begin = block_index * qblock
        query_rows = queries.reshape(qblock, heads_dev, EHEAD_DIM)
        key_rows = keys_ext.reshape(span_rows, heads_dev, EHEAD_DIM)
        value_rows = values_ext.reshape(span_rows, heads_dev, EHEAD_DIM)
        query_ids = lax.dynamic_slice_in_dim(local_ids, begin + margin, qblock, 0)
        scores = jnp.einsum(
            "qhe,khe->hqk", query_rows, key_rows, preferred_element_type=jnp.float32
        ) * EHEAD_DIM ** (-0.5)
        allowed = query_ids[:, None] == local_ids[None, :]
        scores = jnp.where(allowed[None], scores, -1e30)
        peak = jnp.max(scores, axis=-1, keepdims=True)
        raised = jnp.exp(scores - peak)
        probs = (raised / jnp.sum(raised, axis=-1, keepdims=True)).astype(jnp.bfloat16)
        blended = jnp.einsum("hqk,khe->qhe", probs, value_rows, preferred_element_type=jnp.float32)
        return blended.astype(jnp.bfloat16).reshape(qblock, heads_dev * EHEAD_DIM)

    attended = lax.map(attend, jnp.arange(frame_count // qblock, dtype=jnp.int32)).reshape(
        frame_count, heads_dev * EHEAD_DIM
    )
    attention = jnp.dot(
        lax.all_gather(attended, "head", axis=1, tiled=True),
        out_weight,
        preferred_element_type=jnp.float32,
    )
    encoded = (frames.astype(jnp.float32) + attention + out_bias).astype(jnp.bfloat16)
    pooled = jnp.mean(
        encoded.astype(jnp.float32).reshape(frame_count // 4, 4, encoded.shape[1]), axis=1
    ).astype(jnp.bfloat16)
    pooled_all = lax.all_gather(pooled, "head", axis=1, tiled=True)
    column_part = jnp.dot(pooled_all, adapter_cols, preferred_element_type=jnp.float32)
    column_width = column_part.shape[1]
    column_sq = lax.psum(jnp.sum(jnp.square(column_part), axis=1), "head")
    column_gain = lax.dynamic_slice_in_dim(
        rms_gain, lax.axis_index("head") * column_width, column_width, 0
    )
    column_scaled = (
        column_part * lax.rsqrt(column_sq[:, None] / rms_gain.shape[0] + EPSILON) * column_gain
    ).astype(jnp.bfloat16)
    scaled = lax.all_gather(column_scaled, "head", axis=1, tiled=True)
    inputs = jax.nn.silu(jnp.dot(scaled, x_weight, preferred_element_type=jnp.float32)).astype(
        jnp.bfloat16
    )
    coupler_part = jax.nn.silu(
        jnp.dot(scaled, bc_weight, preferred_element_type=jnp.float32)
    ).astype(jnp.bfloat16)
    couplers = lax.all_gather(coupler_part, "head", axis=1, tiled=True)
    token_count = inputs.shape[0]
    state_heads = inputs.shape[1] // HDIM
    inputs_wide = inputs.astype(jnp.float32).reshape(token_count, state_heads, HDIM)
    c_rows = couplers[:, NSTATE:]
    within, growth, total_decay, end_state = block_terms(
        inputs_wide, couplers[:, :NSTATE], c_rows, decay
    )
    identity = (jnp.ones_like(total_decay), jnp.zeros_like(end_state))
    incoming = prefix((total_decay, end_state), "tm", combine_states, identity)
    from_state = jnp.einsum(
        "tn,hpn->thp", c_rows.astype(jnp.float32), incoming[1], precision=HIGHEST
    )
    result_rows = within + growth[:, :, None] * from_state + skip_gain[None, :, None] * inputs_wide
    mixed = result_rows.astype(jnp.bfloat16).reshape(token_count, state_heads * HDIM)
    return (encoded, mixed)


PLANE = 4
MESH = pl.DeviceIdType.MESH
VM = pl.BlockSpec(memory_space=pltpu.VMEM)
HB = pl.BlockSpec(memory_space=pltpu.HBM)
S_DECAY, S_K, S_V, S_ATT, S_CP, S_X, S_BC, S_T, S_S1, S_S2, S_Y, S_PART = 1, 4, 6, 8, 12, 13, 16, 19, 20, 21, 22, 25
PIECES = 5
F32 = jnp.float32
BF16 = jnp.bfloat16
NT = (((1,), (1,)), ((), ()))
TN = (((0,), (0,)), ((), ()))


def dot(a, b, dims=(((1,), (0,)), ((), ())), precision=None):
    return lax.dot_general(a, b, dims, precision=precision, preferred_element_type=F32)


def iota(shape, dim):
    return lax.broadcasted_iota(jnp.int32, shape, dim)


def fused_kernel(
    nt,
    frames_hbm, ids_hbm, lng_hbm, lnb_hbm, qkv_hbm, out_hbm, ob_hbm, ad_hbm, rms_hbm, x_hbm, bc_hbm, decay_hbm, skip_hbm,
    enc_o, mix_o,
    wqkv, wout, wad, wx, wbc, ids, ln_gain, ln_bias, out_bias, rms_gain, skip, wsem,
    fb, nb, qb, kb, vb, mk, acc, mb, lb, att, pf, ps, pr, sc, cp, xin, xq, xb, bcb, db,
    sm, pm, s1, s2, tp, tn, yacc, yb, yr, send, recv,
):
    tm = lax.axis_index("tm")
    hy = lax.axis_index("head")
    z = tm // PLANE
    q = tm % PLANE
    planes = nt // PLANE
    rows = frames_hbm.shape[0]
    toks = decay_hbm.shape[1]
    span = PLANE * toks
    width = qb.shape[1]
    pairs = width // 128
    qw = xb.shape[2]
    qheads = qw // HDIM
    heads = decay_hbm.shape[0]

    loads = [
        pltpu.make_async_copy(src, dst, wsem.at[i])
        for i, (src, dst) in enumerate(
            [
                (qkv_hbm.at[1], wqkv.at[1]),
                (qkv_hbm.at[2], wqkv.at[2]),
                (qkv_hbm.at[0], wqkv.at[0]),
                (out_hbm, wout),
                (ad_hbm, wad),
                (bc_hbm, wbc),
                (x_hbm, wx),
                (frames_hbm, fb.at[hy]),
                (decay_hbm, db.at[q]),
                (ids_hbm, ids),
                (lng_hbm, ln_gain),
                (lnb_hbm, ln_bias),
                (ob_hbm, out_bias),
                (rms_hbm, rms_gain),
                (skip_hbm, skip),
            ]
        )
    ]

    def remote(src, dst, sem, device):
        return pltpu.make_async_remote_copy(
            src_ref=src, dst_ref=dst, send_sem=send.at[sem], recv_sem=recv.at[sem],
            device_id=device, device_id_type=MESH,
        )

    partner = {"head": 1 - hy}
    peers = [{"tm": z * PLANE + (q + k) % PLANE} for k in range(1, PLANE)]
    prev = {"tm": (tm + nt - 1) % nt}
    after = {"tm": (tm + 1) % nt}
    bar = pltpu.get_barrier_semaphore()

    def greet(device):
        pl.semaphore_signal(bar, inc=1, device_id=device, device_id_type=MESH)

    greet(partner)
    for peer in peers:
        greet(peer)
    for dz in range(1, planes):
        greet({"tm": (tm + dz * PLANE) % nt})
    cross_prev = jnp.logical_and(q == 0, tm > 0)
    cross_next = jnp.logical_and(q == PLANE - 1, tm < nt - 1)

    @pl.when(cross_prev)
    def _():
        greet(prev)

    @pl.when(cross_next)
    def _():
        greet(after)

    for load in loads[7:]:
        load.start()
    for load in loads[:7]:
        load.start()
    pl.semaphore_wait(bar, PLANE + planes - 1 + cross_prev.astype(jnp.int32) + cross_next.astype(jnp.int32))

    c_frames = remote(frames_hbm, fb.at[hy], 0, partner)
    c_frames.start()
    c_decay = [remote(decay_hbm, db.at[q], S_DECAY + k, peer) for k, peer in enumerate(peers)]
    for c in c_decay:
        c.start()

    for load in loads[7:]:
        load.wait()

    def id_row(at):
        return ids[pl.ds(pl.multiple_of(at * rows, rows), rows)].reshape(1, rows).astype(F32)

    own = id_row(tm)
    low = jnp.where(tm > 0, id_row((tm + nt - 1) % nt), -1.0)
    high = jnp.where(tm < nt - 1, id_row((tm + 1) % nt), -1.0)
    own_col = jnp.transpose(jnp.broadcast_to(own, (128, rows)))[:, :1]
    for i, row in enumerate((own, low, high)):
        mk[:, i * rows : (i + 1) * rows] = jnp.where(own_col == row, 0.0, -1e30)

    @pl.when(tm == 0)
    def _():
        kb[1] = jnp.zeros((rows, width), BF16)
        vb[1] = jnp.zeros((rows, width), BF16)

    @pl.when(tm == nt - 1)
    def _():
        kb[2] = jnp.zeros((rows, width), BF16)
        vb[2] = jnp.zeros((rows, width), BF16)

    c_frames.wait()
    both = jnp.concatenate([fb[0], fb[1]], axis=1).astype(F32)
    center = jnp.mean(both, axis=-1, keepdims=True)
    moved = both - center
    spread = jnp.mean(jnp.square(moved), axis=-1, keepdims=True)
    nb[...] = (moved * lax.rsqrt(spread + EPSILON) * ln_gain[...].reshape(1, -1) + ln_bias[...].reshape(1, -1)).astype(BF16)

    def project(which, dst, scale):
        def tile(j, carry):
            cols = pl.ds(pl.multiple_of(j * 256, 256), 256)
            part = dot(nb[...], wqkv[which, :, cols]).astype(BF16)
            dst[:, cols] = part * scale if scale is not None else part
            return carry

        lax.fori_loop(0, width // 256, tile, 0)

    def halo(buf, sem):
        return (remote(buf.at[0], buf.at[1], sem, after), remote(buf.at[0], buf.at[2], sem + 1, prev))

    def halo_start(pair):
        @pl.when(tm < nt - 1)
        def _():
            pair[0].start()

        @pl.when(tm > 0)
        def _():
            pair[1].start()

    def halo_wait(pair):
        @pl.when(tm > 0)
        def _():
            pair[0].wait_recv()
            pair[1].wait_send()

        @pl.when(tm < nt - 1)
        def _():
            pair[0].wait_send()
            pair[1].wait_recv()

    loads[0].wait()
    project(1, kb.at[0], None)
    c_k = halo(kb, S_K)
    halo_start(c_k)
    loads[1].wait()
    project(2, vb.at[0], None)
    c_v = halo(vb, S_V)
    halo_start(c_v)
    loads[2].wait()
    project(0, qb, jnp.asarray(EHEAD_DIM ** (-0.5), BF16))

    lane = iota((1, 128), 1)
    is_low = lane < EHEAD_DIM
    sides = (jnp.where(is_low, 1.0, 0.0).astype(BF16), jnp.where(is_low, 0.0, 1.0).astype(BF16))

    def within_own(p, carry):
        cols = pl.ds(pl.multiple_of(p * 128, 128), 128)
        qp, kp, vp = qb[:, cols], kb[0, :, cols], vb[0, :, cols]
        got = []
        for side in sides:
            s = dot(qp * side, kp, NT) + mk[:, :rows]
            m = jnp.max(s, axis=-1, keepdims=True)
            e = jnp.exp(s - m)
            got.append((dot(e.astype(BF16), vp), m, jnp.sum(e, axis=-1, keepdims=True)))
        acc[p] = jnp.where(is_low, got[0][0], got[1][0])
        mb[p] = jnp.where(is_low, got[0][1], got[1][1])
        lb[p] = jnp.where(is_low, got[0][2], got[1][2])
        return carry

    lax.fori_loop(0, pairs, within_own, 0)
    halo_wait(c_k)
    halo_wait(c_v)

    def att_copy(p):
        cols = pl.ds(pl.multiple_of(hy * width + p * 128, 128), 128)
        return remote(att.at[:, cols], att.at[:, cols], S_ATT + p, partner)

    def with_halos(p, carry):
        cols = pl.ds(pl.multiple_of(p * 128, 128), 128)
        qp = qb[:, cols]
        kp = kb[1:3, :, cols].reshape(2 * rows, 128)
        vp = vb[1:3, :, cols].reshape(2 * rows, 128)
        old_m, old_l = mb[p], lb[p]
        got = []
        for i, side in enumerate(sides):
            s = dot(qp * side, kp, NT) + mk[:, rows:]
            m1 = old_m[:, i * EHEAD_DIM : i * EHEAD_DIM + 1]
            m = jnp.maximum(jnp.max(s, axis=-1, keepdims=True), m1)
            e = jnp.exp(s - m)
            got.append((dot(e.astype(BF16), vp), m, jnp.sum(e, axis=-1, keepdims=True)))
        fade = jnp.exp(old_m - jnp.where(is_low, got[0][1], got[1][1]))
        total = old_l * fade + jnp.where(is_low, got[0][2], got[1][2])
        blended = acc[p] * fade + jnp.where(is_low, got[0][0], got[1][0])
        att[:, pl.ds(pl.multiple_of(hy * width + p * 128, 128), 128)] = (blended / total).astype(BF16)
        att_copy(p).start()
        return carry

    lax.fori_loop(0, pairs, with_halos, 0)
    for p in range(pairs):
        att_copy(p).wait()

    loads[3].wait()
    encoded = (fb[hy].astype(F32) + dot(att[...], wout[...]) + out_bias[...].reshape(1, -1)).astype(BF16)
    enc_o[...] = encoded
    rr, cc = iota((toks, rows), 0) * 4, iota((toks, rows), 1)
    pool = jnp.where(jnp.logical_and(cc >= rr, cc < rr + 4), 0.25, 0.0).astype(BF16)
    pooled = dot(pool, encoded).astype(BF16)

    loads[4].wait()

    piece = wad.shape[1] // PIECES

    def part_copy(j):
        cols = pl.ds(pl.multiple_of(j * piece, piece), piece)
        return remote(ps.at[:, cols], pr.at[:, cols], S_PART + j, partner)

    def adapt(j, carry):
        cols = pl.ds(pl.multiple_of(j * piece, piece), piece)
        part = dot(pooled, wad[:, cols])
        pf[:, cols] = part
        ps[:, cols] = part.astype(BF16)
        part_copy(j).start()
        return carry

    lax.fori_loop(0, PIECES, adapt, 0)

    for c in c_decay:
        c.wait()
    eye = jnp.where(iota((toks, toks), 0) == iota((toks, toks), 1), 1.0, 0.0)
    dec = jnp.concatenate([dot(eye, db[j], NT, HIGHEST) for j in range(PLANE)], axis=0)
    picked_row = q * qheads
    sel = jnp.where(iota((heads, 128), 0) == picked_row + iota((heads, 128), 1), 1.0, 0.0)
    sel = jnp.where(iota((heads, 128), 1) < qheads, sel, 0.0)
    first = (iota((heads, qw), 0) - picked_row) * HDIM
    wide = iota((heads, qw), 1)
    expand = jnp.where(jnp.logical_and(wide >= first, wide < first + HDIM), 1.0, 0.0)
    tri = jnp.where(iota((span, span), 0) >= iota((span, span), 1), 1.0, 0.0)
    cum = dot(tri, jnp.log(jnp.maximum(dec, 1e-37)), precision=HIGHEST)
    cum_col = dot(cum, sel, precision=HIGHEST)
    cum_row = jnp.transpose(cum_col)
    growth = dot(jnp.exp(cum), expand, precision=HIGHEST)
    tail = dot(jnp.exp(cum[span - 1 :, :] - cum), expand, precision=HIGHEST)
    drive = dot(1.0 - dec, expand, precision=HIGHEST)
    skip_wide = dot(jnp.broadcast_to(skip[...].reshape(1, -1), (8, heads)), expand, precision=HIGHEST)[:1, :]
    total = growth[span - 1 :, :]
    tp[...] = jnp.broadcast_to(total, (8, qw))
    later = {"tm": (tm + PLANE) % nt}
    latest = {"tm": (tm + 2 * PLANE) % nt}
    c_t = remote(tp, tn, S_T, later)
    c_s1 = remote(sm, s1, S_S1, later)
    c_s2 = remote(sm, s2, S_S2, latest)
    c_p = remote(pm, s2, S_S2, latest)

    @pl.when(z < planes - 1)
    def _():
        c_t.start()

    for j in range(PIECES):
        part_copy(j).wait()
    proj = pf[...] + pr[...].astype(F32)
    square = jnp.mean(jnp.square(proj), axis=-1, keepdims=True)
    sc[...] = (proj * lax.rsqrt(square + EPSILON) * rms_gain[...].reshape(1, -1)).astype(BF16)

    def silu(v):
        return v / (1.0 + jnp.exp(-v))

    loads[5].wait()
    cp[hy] = silu(dot(sc[...], wbc[...])).astype(BF16)
    c_cp = remote(cp.at[hy], cp.at[hy], S_CP, partner)
    c_cp.start()
    loads[6].wait()

    def drive_in(j, carry):
        cols = pl.ds(pl.multiple_of(j * 256, 256), 256)
        xin[:, cols] = silu(dot(sc[...], wx[:, cols]))
        return carry

    tiles = wx.shape[1] // 256
    lax.fori_loop(0, tiles // 2 + 1, drive_in, 0)
    c_cp.wait()
    c_bc = [remote(cp, bcb.at[:, q], S_BC + k - 1, peers[k - 1]) for k in range(1, PLANE)]
    for c in c_bc:
        c.start()
    bcb[:, q] = cp[...]
    lax.fori_loop(tiles // 2 + 1, tiles, drive_in, 0)
    for j in range(PLANE):
        xq[j] = xin[:, j * qw : (j + 1) * qw].astype(BF16)
    c_x = [remote(xq.at[(q + k) % PLANE], xb.at[q], S_X + k - 1, peers[k - 1]) for k in range(1, PLANE)]
    for c in c_x:
        c.start()
    xb[q] = xq[q]
    for c in c_x:
        c.wait()
    for c in c_bc:
        c.wait()

    x_all = xb[...].reshape(span, qw).astype(F32)
    b_all = bcb[0].reshape(span, NSTATE)
    c_all = bcb[1].reshape(span, NSTATE)
    driven = x_all * drive
    state = dot(b_all, (driven * tail).astype(BF16), TN)
    sm[...] = state.astype(BF16)

    @pl.when(z < planes - 1)
    def _():
        c_s1.start()

    @pl.when(z == 0)
    def _():
        c_s2.start()

    affinity = dot(c_all, b_all, NT)
    causal = iota((span, span), 0) >= iota((span, span), 1)
    driven = driven.astype(BF16)

    def head_out(h, cols):
        gap = cum_col[:, h : h + 1] - cum_row[h : h + 1, :]
        mixing = affinity * jnp.exp(jnp.where(causal, gap, -1e30))
        return dot(mixing.astype(BF16), cols)

    for h in range(0, qheads, 2):
        if h + 1 < qheads:
            cols = driven[:, h * HDIM : (h + 2) * HDIM]
            yacc[:, h * HDIM : (h + 2) * HDIM] = jnp.where(is_low, head_out(h, cols), head_out(h + 1, cols))
        else:
            yacc[:, h * HDIM : (h + 1) * HDIM] = head_out(h, driven[:, h * HDIM : (h + 1) * HDIM])
    yacc[...] = yacc[...] + skip_wide * x_all

    @pl.when(z > 0)
    def _():
        c_t.wait_recv()
        c_s1.wait_recv()

    @pl.when(z == 1)
    def _():
        pm[...] = (state + total * s1[...].astype(F32)).astype(BF16)
        c_p.start()

    @pl.when(z > 1)
    def _():
        c_s2.wait_recv()
        s1[...] = (s1[...].astype(F32) + tn[:1, :] * s2[...].astype(F32)).astype(BF16)

    @pl.when(z == 0)
    def _():
        s1[...] = jnp.zeros(s1.shape, BF16)

    y = yacc[...] + growth * dot(c_all, s1[...])
    yb[...] = y.astype(BF16).reshape(PLANE, toks, qw)
    c_y = [remote(yb.at[(q + k) % PLANE], yr.at[q], S_Y + k - 1, peers[k - 1]) for k in range(1, PLANE)]
    for c in c_y:
        c.start()
    yr[q] = yb[q]
    @pl.when(z < planes - 1)
    def _():
        c_t.wait_send()
        c_s1.wait_send()

    @pl.when(z < planes - 2)
    def _():
        c_s2.wait_send()

    for c in c_y:
        c.wait()
    for j in range(PLANE):
        mix_o[:, j * qw : (j + 1) * qw] = yr[j]


def fused(nt):
    def per_device(frames, segment_ids, ln_gain, ln_bias, qkv_weight, out_weight, out_bias, adapter, rms_gain,
                   x_weight, bc_weight, decay, skip_gain):
        rows, half = frames.shape
        width = qkv_weight.shape[2]
        toks, heads = decay.shape
        dm = adapter.shape[1]
        xw = x_weight.shape[1]
        qw = xw // PLANE
        planes = nt // PLANE
        span = PLANE * toks
        pairs = width // 128
        sems = S_PART + PIECES
        v = pltpu.VMEM
        encoded, mixed = pl.pallas_call(
            functools.partial(fused_kernel, nt),
            out_shape=(
                jax.ShapeDtypeStruct((rows, half), BF16),
                jax.ShapeDtypeStruct((toks, xw), BF16),
            ),
            in_specs=[HB] * 13,
            out_specs=(VM, VM),
            scratch_shapes=[
                v(qkv_weight.shape, BF16),
                v(out_weight.shape, BF16),
                v(adapter.shape, BF16),
                v(x_weight.shape, BF16),
                v(bc_weight.shape, BF16),
                v(segment_ids.shape, jnp.int32),
                v(ln_gain.shape, F32),
                v(ln_bias.shape, F32),
                v(out_bias.shape, F32),
                v(rms_gain.shape, F32),
                v(skip_gain.shape, F32),
                pltpu.SemaphoreType.DMA((15,)),
                v((2, rows, half), BF16),
                v((rows, 2 * half), BF16),
                v((rows, width), BF16),
                v((3, rows, width), BF16),
                v((3, rows, width), BF16),
                v((rows, 3 * rows), F32),
                v((pairs, rows, 128), F32),
                v((pairs, rows, 128), F32),
                v((pairs, rows, 128), F32),
                v((rows, 2 * width), BF16),
                v((toks, dm), F32),
                v((toks, dm), BF16),
                v((toks, dm), BF16),
                v((toks, dm), BF16),
                v((2, toks, NSTATE), BF16),
                v((toks, xw), F32),
                v((PLANE, toks, qw), BF16),
                v((PLANE, toks, qw), BF16),
                v((2, PLANE, toks, NSTATE), BF16),
                v((PLANE, heads, toks), F32),
                v((NSTATE, qw), BF16),
                v((NSTATE, qw), BF16),
                v((NSTATE, qw), BF16),
                v((NSTATE, qw), BF16),
                v((8, qw), F32),
                v((8, qw), F32),
                v((span, qw), F32),
                v((PLANE, toks, qw), BF16),
                v((PLANE, toks, qw), BF16),
                pltpu.SemaphoreType.DMA((sems,)),
                pltpu.SemaphoreType.DMA((sems,)),
            ],
            compiler_params=pltpu.CompilerParams(
                collective_id=0, has_side_effects=True, vmem_limit_bytes=52 * 1024 * 1024
            ),
        )(
            frames, segment_ids, ln_gain, ln_bias, qkv_weight, out_weight, out_bias, adapter, rms_gain, x_weight,
            bc_weight, jnp.transpose(decay), skip_gain,
        )
        return encoded, mixed

    return per_device


def solution(mesh):
    placed = (
        P("tm", "head"),
        P(),
        P(),
        P(),
        P(None, None, "head"),
        P(None, "head"),
        P("head"),
        P("head", None),
        P(),
        P(None, "head"),
        P(None, "head"),
        P("tm", "head"),
        P("head"),
    )
    nt = mesh.shape["tm"]
    body = fused(nt) if mesh.shape["head"] == 2 and nt == 4 * PLANE else per_device
    return jax.shard_map(
        body,
        mesh=mesh,
        in_specs=placed,
        out_specs=(P("tm", "head"), P("tm", "head")),
        check_vma=False,
    )
```

```python
import functools
import math

import jax
import jax.numpy as jnp
from jax import lax
from jax.experimental import pallas as pl
from jax.experimental.pallas import tpu as pltpu
from jax.sharding import PartitionSpec as P

EHEAD_DIM = 64
HDIM = 64
NSTATE = 128
WINDOW = 256


EPSILON = 1e-05
HIGHEST = lax.Precision.HIGHEST


def with_halo(block, sides, width):
    for axis, dim in sides:
        count = lax.axis_size(axis)
        forward = [(i, i + 1) for i in range(count - 1)]
        backward = [(target, source) for source, target in forward]
        low = lax.ppermute(
            lax.slice_in_dim(block, block.shape[dim] - width, None, axis=dim), axis, forward
        )
        high = lax.ppermute(lax.slice_in_dim(block, 0, width, axis=dim), axis, backward)
        block = jnp.concatenate([low, block, high], axis=dim)
    return block


def prefix(part, axis, combine, identity):
    place = lax.axis_index(axis)
    gathered = jax.tree.map(lambda a: lax.all_gather(a, axis), part)
    state = jax.tree.map(lambda a, e: jnp.zeros_like(a) + jnp.asarray(e, a.dtype), part, identity)

    def one(hop, state):
        return combine(
            state, jax.tree.map(lambda a: lax.dynamic_index_in_dim(a, hop, 0, False), gathered)
        )

    return lax.fori_loop(0, place, one, state)


def layer_norm(values, gain, offset):
    center_mean = jnp.mean(values, axis=-1, keepdims=True)
    spread = jnp.mean(jnp.square(values - center_mean), axis=-1, keepdims=True)
    return (values - center_mean) * lax.rsqrt(spread + EPSILON) * gain + offset


def block_terms(inputs, b_in, c_in, decay):
    log_decay = jnp.log(decay)
    cumulative = jnp.cumsum(log_decay, axis=0)
    length = inputs.shape[0]
    sequence_indices = jnp.arange(length, dtype=jnp.int32)
    causal = sequence_indices[:, None] >= sequence_indices[None, :]
    log_gap = cumulative[:, None, :] - cumulative[None, :, :]
    weights = jnp.exp(jnp.where(causal[:, :, None], log_gap, -1e30))
    driven = inputs * (1.0 - decay)[:, :, None]
    affinity = jnp.dot(c_in, b_in.T, preferred_element_type=jnp.float32)
    within = jnp.einsum("tsh,shp->thp", affinity[:, :, None] * weights, driven, precision=HIGHEST)
    tail_decay = jnp.exp(cumulative[-1][None, :] - cumulative)
    end_state = jnp.einsum(
        "sh,shp,sn->hpn", tail_decay, driven, b_in.astype(jnp.float32), precision=HIGHEST
    )
    return (within, jnp.exp(cumulative), jnp.exp(cumulative[-1]), end_state)


def combine_states(earlier, later):
    return (earlier[0] * later[0], later[0][:, None, None] * earlier[1] + later[1])


def per_device(
    frames,
    segment_ids,
    ln_gain,
    ln_bias,
    qkv_weight,
    out_weight,
    out_bias,
    adapter,
    rms_gain,
    x_weight,
    bc_weight,
    decay,
    skip_gain,
):
    frame_count = frames.shape[0]
    margin = WINDOW
    tm_slot = lax.axis_index("tm")
    adapter_cols = lax.all_to_all(adapter, "head", split_axis=1, concat_axis=0, tiled=True)
    gathered = lax.all_gather(frames, "head", axis=1, tiled=True)
    normed = layer_norm(gathered.astype(jnp.float32), ln_gain, ln_bias).astype(jnp.bfloat16)
    queries = jnp.dot(normed, qkv_weight[0], preferred_element_type=jnp.float32).astype(
        jnp.bfloat16
    )
    keys_own = jnp.dot(normed, qkv_weight[1], preferred_element_type=jnp.float32).astype(
        jnp.bfloat16
    )
    values_own = jnp.dot(normed, qkv_weight[2], preferred_element_type=jnp.float32).astype(
        jnp.bfloat16
    )
    joined = jnp.concatenate([keys_own, values_own], axis=1)
    extended = with_halo(joined, (("tm", 0),), margin)
    head_width = keys_own.shape[1]
    keys_ext = extended[:, :head_width]
    values_ext = extended[:, head_width:]
    ids_pad = jnp.pad(segment_ids, (margin, margin), constant_values=-1)
    local_ids = lax.dynamic_slice_in_dim(
        ids_pad, tm_slot * frame_count, frame_count + 2 * margin, 0
    )
    heads_dev = queries.shape[1] // EHEAD_DIM
    qblock = math.gcd(frame_count, 512)
    span_rows = qblock + 2 * margin

    def attend(block_index):
        begin = block_index * qblock
        query_rows = queries.reshape(qblock, heads_dev, EHEAD_DIM)
        key_rows = keys_ext.reshape(span_rows, heads_dev, EHEAD_DIM)
        value_rows = values_ext.reshape(span_rows, heads_dev, EHEAD_DIM)
        query_ids = lax.dynamic_slice_in_dim(local_ids, begin + margin, qblock, 0)
        scores = jnp.einsum(
            "qhe,khe->hqk", query_rows, key_rows, preferred_element_type=jnp.float32
        ) * EHEAD_DIM ** (-0.5)
        allowed = query_ids[:, None] == local_ids[None, :]
        scores = jnp.where(allowed[None], scores, -1e30)
        peak = jnp.max(scores, axis=-1, keepdims=True)
        raised = jnp.exp(scores - peak)
        probs = (raised / jnp.sum(raised, axis=-1, keepdims=True)).astype(jnp.bfloat16)
        blended = jnp.einsum("hqk,khe->qhe", probs, value_rows, preferred_element_type=jnp.float32)
        return blended.astype(jnp.bfloat16).reshape(qblock, heads_dev * EHEAD_DIM)

    attended = lax.map(attend, jnp.arange(frame_count // qblock, dtype=jnp.int32)).reshape(
        frame_count, heads_dev * EHEAD_DIM
    )
    attention = jnp.dot(
        lax.all_gather(attended, "head", axis=1, tiled=True),
        out_weight,
        preferred_element_type=jnp.float32,
    )
    encoded = (frames.astype(jnp.float32) + attention + out_bias).astype(jnp.bfloat16)
    pooled = jnp.mean(
        encoded.astype(jnp.float32).reshape(frame_count // 4, 4, encoded.shape[1]), axis=1
    ).astype(jnp.bfloat16)
    pooled_all = lax.all_gather(pooled, "head", axis=1, tiled=True)
    column_part = jnp.dot(pooled_all, adapter_cols, preferred_element_type=jnp.float32)
    column_width = column_part.shape[1]
    column_sq = lax.psum(jnp.sum(jnp.square(column_part), axis=1), "head")
    column_gain = lax.dynamic_slice_in_dim(
        rms_gain, lax.axis_index("head") * column_width, column_width, 0
    )
    column_scaled = (
        column_part * lax.rsqrt(column_sq[:, None] / rms_gain.shape[0] + EPSILON) * column_gain
    ).astype(jnp.bfloat16)
    scaled = lax.all_gather(column_scaled, "head", axis=1, tiled=True)
    inputs = jax.nn.silu(jnp.dot(scaled, x_weight, preferred_element_type=jnp.float32)).astype(
        jnp.bfloat16
    )
    coupler_part = jax.nn.silu(
        jnp.dot(scaled, bc_weight, preferred_element_type=jnp.float32)
    ).astype(jnp.bfloat16)
    couplers = lax.all_gather(coupler_part, "head", axis=1, tiled=True)
    token_count = inputs.shape[0]
    state_heads = inputs.shape[1] // HDIM
    inputs_wide = inputs.astype(jnp.float32).reshape(token_count, state_heads, HDIM)
    c_rows = couplers[:, NSTATE:]
    within, growth, total_decay, end_state = block_terms(
        inputs_wide, couplers[:, :NSTATE], c_rows, decay
    )
    identity = (jnp.ones_like(total_decay), jnp.zeros_like(end_state))
    incoming = prefix((total_decay, end_state), "tm", combine_states, identity)
    from_state = jnp.einsum(
        "tn,hpn->thp", c_rows.astype(jnp.float32), incoming[1], precision=HIGHEST
    )
    result_rows = within + growth[:, :, None] * from_state + skip_gain[None, :, None] * inputs_wide
    mixed = result_rows.astype(jnp.bfloat16).reshape(token_count, state_heads * HDIM)
    return (encoded, mixed)


PLANE = 4
MESH = pl.DeviceIdType.MESH
VM = pl.BlockSpec(memory_space=pltpu.VMEM)
HB = pl.BlockSpec(memory_space=pltpu.HBM)
S_DECAY, S_K, S_V, S_ATT, S_CP, S_X, S_BC, S_T, S_S1, S_S2, S_Y, S_PART = 1, 4, 6, 8, 12, 13, 16, 19, 20, 21, 22, 25
PIECES = 5
S_OFF, S_ON = 30, 32
CHUNKS = 2
LIMIT = 63 * 1024 * 1024
F32 = jnp.float32
BF16 = jnp.bfloat16
NT = (((1,), (1,)), ((), ()))
TN = (((0,), (0,)), ((), ()))


def dot(a, b, dims=(((1,), (0,)), ((), ())), precision=None):
    return lax.dot_general(a, b, dims, precision=precision, preferred_element_type=F32)


def iota(shape, dim):
    return lax.broadcasted_iota(jnp.int32, shape, dim)


def fused_kernel(
    nt,
    frames_hbm, ids_hbm, lng_hbm, lnb_hbm, qkv_hbm, out_hbm, ob_hbm, ad_hbm, rms_hbm, x_hbm, bc_hbm, decay_hbm, skip_hbm,
    enc_o, mix_o,
    wqkv, wout, wad, wx, wbc, ids, ln_gain, ln_bias, out_bias, rms_gain, skip, wsem,
    fb, ob, nb, qb, kb, vb, mk, acc, mb, lb, att, pf, ps, pr, sc, cp, xin, xq, xb, bcb, db,
    sm, pm, s1, s2, tp, tn, yacc, yb, yr, send, recv,
):
    tm = lax.axis_index("tm")
    hy = lax.axis_index("head")
    z = tm // PLANE
    q = tm % PLANE
    planes = nt // PLANE
    rows = frames_hbm.shape[0]
    toks = decay_hbm.shape[1]
    span = PLANE * toks
    width = qb.shape[1]
    pairs = width // 128
    qw = xb.shape[2]
    qheads = qw // HDIM
    heads = decay_hbm.shape[0]

    loads = [
        pltpu.make_async_copy(src, dst, wsem.at[i])
        for i, (src, dst) in enumerate(
            [
                (qkv_hbm.at[1], wqkv.at[1]),
                (qkv_hbm.at[2], wqkv.at[2]),
                (qkv_hbm.at[0], wqkv.at[0]),
                (out_hbm, wout),
                (ad_hbm, wad),
                (bc_hbm, wbc),
                (x_hbm, wx),
                (frames_hbm, fb.at[hy]),
                (decay_hbm, db.at[q]),
                (ids_hbm, ids),
                (lng_hbm, ln_gain),
                (lnb_hbm, ln_bias),
                (ob_hbm, out_bias),
                (rms_hbm, rms_gain),
                (skip_hbm, skip),
            ]
        )
    ]

    def remote(src, dst, sem, device):
        return pltpu.make_async_remote_copy(
            src_ref=src, dst_ref=dst, send_sem=send.at[sem], recv_sem=recv.at[sem],
            device_id=device, device_id_type=MESH,
        )

    partner = {"head": 1 - hy}
    peers = [{"tm": z * PLANE + (q + k) % PLANE} for k in range(1, PLANE)]
    side = tm % 2
    off_at = (tm + nt - 1 + 2 * side) % nt
    on_at = tm + 1 - 2 * side
    off = {"tm": off_at}
    on = {"tm": on_at}
    has_off = jnp.logical_and(tm > 0, tm < nt - 1)
    bar = pltpu.get_barrier_semaphore()

    def greet(device):
        pl.semaphore_signal(bar, inc=1, device_id=device, device_id_type=MESH)

    greet(partner)
    for peer in peers:
        greet(peer)
    for dz in range(1, planes):
        greet({"tm": (tm + dz * PLANE) % nt})
    far = jnp.logical_and(has_off, jnp.logical_or(q == 0, q == PLANE - 1))

    @pl.when(far)
    def _():
        greet(off)

    for load in loads[7:]:
        load.start()
    for load in loads[:7]:
        load.start()
    pl.semaphore_wait(bar, PLANE + planes - 1 + far.astype(jnp.int32))

    c_frames = remote(frames_hbm, fb.at[hy], 0, partner)
    c_frames.start()
    step = rows // CHUNKS

    def off_copy(i):
        part = pl.ds(i * step, step)
        return remote(frames_hbm.at[part, :], ob.at[hy, part, :], S_OFF + i, off)

    def on_copy(i):
        part = pl.ds(i * step, step)
        return remote(ob.at[hy, part, :], ob.at[hy, part, :], S_ON + i, partner)

    def hand_on(i):
        @pl.when(has_off)
        def _():
            off_copy(i).wait_recv()
            on_copy(i).start()

    @pl.when(has_off)
    def _():
        for i in range(CHUNKS):
            off_copy(i).start()

    c_decay = [remote(decay_hbm, db.at[q], S_DECAY + k, peer) for k, peer in enumerate(peers)]
    for c in c_decay:
        c.start()

    for load in loads[7:]:
        load.wait()

    def id_row(at):
        return ids[pl.ds(pl.multiple_of(at * rows, rows), rows)].reshape(1, rows).astype(F32)

    own = id_row(tm)
    beside = id_row(on_at)
    beyond = jnp.where(has_off, id_row(off_at), -1.0)
    own_col = jnp.transpose(jnp.broadcast_to(own, (128, rows)))[:, :1]
    for i, row in enumerate((own, beside, beyond)):
        mk[:, i * rows : (i + 1) * rows] = jnp.where(own_col == row, 0.0, -1e30)

    def normalize(buf):
        both = jnp.concatenate([buf[0], buf[1]], axis=1).astype(F32)
        center = jnp.mean(both, axis=-1, keepdims=True)
        moved = both - center
        spread = jnp.mean(jnp.square(moved), axis=-1, keepdims=True)
        scale = ln_gain[...].reshape(1, -1)
        nb[...] = (moved * lax.rsqrt(spread + EPSILON) * scale + ln_bias[...].reshape(1, -1)).astype(BF16)

    c_frames.wait()
    normalize(fb)

    def project(which, dst, scale):
        def tile(j, carry):
            cols = pl.ds(pl.multiple_of(j * 256, 256), 256)
            part = dot(nb[...], wqkv[which, :, cols]).astype(BF16)
            dst[:, cols] = part * scale if scale is not None else part
            return carry

        lax.fori_loop(0, width // 256, tile, 0)

    loads[0].wait()
    project(1, kb.at[0], None)
    c_k = remote(kb.at[0], kb.at[1], S_K, on)
    c_k.start()
    hand_on(0)
    loads[1].wait()
    project(2, vb.at[0], None)
    c_v = remote(vb.at[0], vb.at[1], S_V, on)
    c_v.start()
    hand_on(1)
    loads[2].wait()
    project(0, qb, jnp.asarray(EHEAD_DIM ** (-0.5), BF16))

    lane = iota((1, 128), 1)
    is_low = lane < EHEAD_DIM
    sides = (jnp.where(is_low, 1.0, 0.0).astype(BF16), jnp.where(is_low, 0.0, 1.0).astype(BF16))

    def within_chip(p, carry):
        cols = pl.ds(pl.multiple_of(p * 128, 128), 128)
        qp = qb[:, cols]
        kp = kb[:2, :, cols].reshape(2 * rows, 128)
        vp = vb[:2, :, cols].reshape(2 * rows, 128)
        got = []
        for side in sides:
            s = dot(qp * side, kp, NT) + mk[:, : 2 * rows]
            m = jnp.max(s, axis=-1, keepdims=True)
            e = jnp.exp(s - m)
            got.append((dot(e.astype(BF16), vp), m, jnp.sum(e, axis=-1, keepdims=True)))
        acc[p] = jnp.where(is_low, got[0][0], got[1][0])
        mb[p] = jnp.where(is_low, got[0][1], got[1][1])
        lb[p] = jnp.where(is_low, got[0][2], got[1][2])
        return carry

    c_k.wait()
    c_v.wait()
    lax.fori_loop(0, pairs, within_chip, 0)

    @pl.when(has_off)
    def _():
        for i in range(CHUNKS):
            on_copy(i).wait()
            off_copy(i).wait_send()
        normalize(ob)
        project(1, kb.at[2], None)
        project(2, vb.at[2], None)

    @pl.when(jnp.logical_not(has_off))
    def _():
        kb[2] = jnp.zeros((rows, width), BF16)
        vb[2] = jnp.zeros((rows, width), BF16)

    def att_copy(p):
        cols = pl.ds(pl.multiple_of(hy * width + p * 128, 128), 128)
        return remote(att.at[:, cols], att.at[:, cols], S_ATT + p, partner)

    def beyond_chip(p, carry):
        cols = pl.ds(pl.multiple_of(p * 128, 128), 128)
        qp = qb[:, cols]
        kp, vp = kb[2, :, cols], vb[2, :, cols]
        old_m, old_l = mb[p], lb[p]
        got = []
        for i, side in enumerate(sides):
            s = dot(qp * side, kp, NT) + mk[:, 2 * rows :]
            m1 = old_m[:, i * EHEAD_DIM : i * EHEAD_DIM + 1]
            m = jnp.maximum(jnp.max(s, axis=-1, keepdims=True), m1)
            e = jnp.exp(s - m)
            got.append((dot(e.astype(BF16), vp), m, jnp.sum(e, axis=-1, keepdims=True)))
        fade = jnp.exp(old_m - jnp.where(is_low, got[0][1], got[1][1]))
        total = old_l * fade + jnp.where(is_low, got[0][2], got[1][2])
        blended = acc[p] * fade + jnp.where(is_low, got[0][0], got[1][0])
        att[:, pl.ds(pl.multiple_of(hy * width + p * 128, 128), 128)] = (blended / total).astype(BF16)
        att_copy(p).start()
        return carry

    lax.fori_loop(0, pairs, beyond_chip, 0)
    for p in range(pairs):
        att_copy(p).wait()

    loads[3].wait()
    encoded = (fb[hy].astype(F32) + dot(att[...], wout[...]) + out_bias[...].reshape(1, -1)).astype(BF16)
    enc_o[...] = encoded
    rr, cc = iota((toks, rows), 0) * 4, iota((toks, rows), 1)
    pool = jnp.where(jnp.logical_and(cc >= rr, cc < rr + 4), 0.25, 0.0).astype(BF16)
    pooled = dot(pool, encoded).astype(BF16)

    loads[4].wait()

    piece = wad.shape[1] // PIECES

    def part_copy(j):
        cols = pl.ds(pl.multiple_of(j * piece, piece), piece)
        return remote(ps.at[:, cols], pr.at[:, cols], S_PART + j, partner)

    def adapt(j, carry):
        cols = pl.ds(pl.multiple_of(j * piece, piece), piece)
        part = dot(pooled, wad[:, cols])
        pf[:, cols] = part
        ps[:, cols] = part.astype(BF16)
        part_copy(j).start()
        return carry

    lax.fori_loop(0, PIECES, adapt, 0)

    for c in c_decay:
        c.wait()
    eye = jnp.where(iota((toks, toks), 0) == iota((toks, toks), 1), 1.0, 0.0)
    dec = jnp.concatenate([dot(eye, db[j], NT, HIGHEST) for j in range(PLANE)], axis=0)
    picked_row = q * qheads
    sel = jnp.where(iota((heads, 128), 0) == picked_row + iota((heads, 128), 1), 1.0, 0.0)
    sel = jnp.where(iota((heads, 128), 1) < qheads, sel, 0.0)
    first = (iota((heads, qw), 0) - picked_row) * HDIM
    wide = iota((heads, qw), 1)
    expand = jnp.where(jnp.logical_and(wide >= first, wide < first + HDIM), 1.0, 0.0)
    tri = jnp.where(iota((span, span), 0) >= iota((span, span), 1), 1.0, 0.0)
    cum = dot(tri, jnp.log(jnp.maximum(dec, 1e-37)), precision=HIGHEST)
    cum_col = dot(cum, sel, precision=HIGHEST)
    cum_row = jnp.transpose(cum_col)
    growth = dot(jnp.exp(cum), expand, precision=HIGHEST)
    tail = dot(jnp.exp(cum[span - 1 :, :] - cum), expand, precision=HIGHEST)
    drive = dot(1.0 - dec, expand, precision=HIGHEST)
    skip_wide = dot(jnp.broadcast_to(skip[...].reshape(1, -1), (8, heads)), expand, precision=HIGHEST)[:1, :]
    total = growth[span - 1 :, :]
    tp[...] = jnp.broadcast_to(total, (8, qw))
    later = {"tm": (tm + PLANE) % nt}
    latest = {"tm": (tm + 2 * PLANE) % nt}
    c_t = remote(tp, tn, S_T, later)
    c_s1 = remote(sm, s1, S_S1, later)
    c_s2 = remote(sm, s2, S_S2, latest)
    c_p = remote(pm, s2, S_S2, latest)

    @pl.when(z < planes - 1)
    def _():
        c_t.start()

    for j in range(PIECES):
        part_copy(j).wait()
    proj = pf[...] + pr[...].astype(F32)
    square = jnp.mean(jnp.square(proj), axis=-1, keepdims=True)
    sc[...] = (proj * lax.rsqrt(square + EPSILON) * rms_gain[...].reshape(1, -1)).astype(BF16)

    def silu(v):
        return v / (1.0 + jnp.exp(-v))

    loads[5].wait()
    cp[hy] = silu(dot(sc[...], wbc[...])).astype(BF16)
    c_cp = remote(cp.at[hy], cp.at[hy], S_CP, partner)
    c_cp.start()
    loads[6].wait()

    def drive_in(j, carry):
        cols = pl.ds(pl.multiple_of(j * 256, 256), 256)
        xin[:, cols] = silu(dot(sc[...], wx[:, cols]))
        return carry

    tiles = wx.shape[1] // 256
    lax.fori_loop(0, tiles // 2 + 1, drive_in, 0)
    c_cp.wait()
    c_bc = [remote(cp, bcb.at[:, q], S_BC + k - 1, peers[k - 1]) for k in range(1, PLANE)]
    for c in c_bc:
        c.start()
    bcb[:, q] = cp[...]
    lax.fori_loop(tiles // 2 + 1, tiles, drive_in, 0)
    for j in range(PLANE):
        xq[j] = xin[:, j * qw : (j + 1) * qw].astype(BF16)
    c_x = [remote(xq.at[(q + k) % PLANE], xb.at[q], S_X + k - 1, peers[k - 1]) for k in range(1, PLANE)]
    for c in c_x:
        c.start()
    xb[q] = xq[q]
    for c in c_x:
        c.wait()
    for c in c_bc:
        c.wait()

    x_all = xb[...].reshape(span, qw).astype(F32)
    b_all = bcb[0].reshape(span, NSTATE)
    c_all = bcb[1].reshape(span, NSTATE)
    driven = x_all * drive
    state = dot(b_all, (driven * tail).astype(BF16), TN)
    sm[...] = state.astype(BF16)

    @pl.when(z < planes - 1)
    def _():
        c_s1.start()

    @pl.when(z == 0)
    def _():
        c_s2.start()

    affinity = dot(c_all, b_all, NT)
    causal = iota((span, span), 0) >= iota((span, span), 1)
    driven = driven.astype(BF16)

    def head_out(h, cols):
        gap = cum_col[:, h : h + 1] - cum_row[h : h + 1, :]
        mixing = affinity * jnp.exp(jnp.where(causal, gap, -1e30))
        return dot(mixing.astype(BF16), cols)

    for h in range(0, qheads, 2):
        if h + 1 < qheads:
            cols = driven[:, h * HDIM : (h + 2) * HDIM]
            yacc[:, h * HDIM : (h + 2) * HDIM] = jnp.where(is_low, head_out(h, cols), head_out(h + 1, cols))
        else:
            yacc[:, h * HDIM : (h + 1) * HDIM] = head_out(h, driven[:, h * HDIM : (h + 1) * HDIM])
    yacc[...] = yacc[...] + skip_wide * x_all

    @pl.when(z > 0)
    def _():
        c_t.wait_recv()
        c_s1.wait_recv()

    @pl.when(z == 1)
    def _():
        pm[...] = (state + total * s1[...].astype(F32)).astype(BF16)
        c_p.start()

    @pl.when(z > 1)
    def _():
        c_s2.wait_recv()
        s1[...] = (s1[...].astype(F32) + tn[:1, :] * s2[...].astype(F32)).astype(BF16)

    @pl.when(z == 0)
    def _():
        s1[...] = jnp.zeros(s1.shape, BF16)

    y = yacc[...] + growth * dot(c_all, s1[...])
    yb[...] = y.astype(BF16).reshape(PLANE, toks, qw)
    c_y = [remote(yb.at[(q + k) % PLANE], yr.at[q], S_Y + k - 1, peers[k - 1]) for k in range(1, PLANE)]
    for c in c_y:
        c.start()
    yr[q] = yb[q]
    @pl.when(z < planes - 1)
    def _():
        c_t.wait_send()
        c_s1.wait_send()

    @pl.when(z < planes - 2)
    def _():
        c_s2.wait_send()

    for c in c_y:
        c.wait()
    for j in range(PLANE):
        mix_o[:, j * qw : (j + 1) * qw] = yr[j]


def fused(nt):
    def per_device(frames, segment_ids, ln_gain, ln_bias, qkv_weight, out_weight, out_bias, adapter, rms_gain,
                   x_weight, bc_weight, decay, skip_gain):
        rows, half = frames.shape
        width = qkv_weight.shape[2]
        toks, heads = decay.shape
        dm = adapter.shape[1]
        xw = x_weight.shape[1]
        qw = xw // PLANE
        planes = nt // PLANE
        span = PLANE * toks
        pairs = width // 128
        sems = S_ON + CHUNKS
        v = pltpu.VMEM
        encoded, mixed = pl.pallas_call(
            functools.partial(fused_kernel, nt),
            out_shape=(
                jax.ShapeDtypeStruct((rows, half), BF16),
                jax.ShapeDtypeStruct((toks, xw), BF16),
            ),
            in_specs=[HB] * 13,
            out_specs=(VM, VM),
            scratch_shapes=[
                v(qkv_weight.shape, BF16),
                v(out_weight.shape, BF16),
                v(adapter.shape, BF16),
                v(x_weight.shape, BF16),
                v(bc_weight.shape, BF16),
                v(segment_ids.shape, jnp.int32),
                v(ln_gain.shape, F32),
                v(ln_bias.shape, F32),
                v(out_bias.shape, F32),
                v(rms_gain.shape, F32),
                v(skip_gain.shape, F32),
                pltpu.SemaphoreType.DMA((15,)),
                v((2, rows, half), BF16),
                v((2, rows, half), BF16),
                v((rows, 2 * half), BF16),
                v((rows, width), BF16),
                v((3, rows, width), BF16),
                v((3, rows, width), BF16),
                v((rows, 3 * rows), F32),
                v((pairs, rows, 128), F32),
                v((pairs, rows, 128), F32),
                v((pairs, rows, 128), F32),
                v((rows, 2 * width), BF16),
                v((toks, dm), F32),
                v((toks, dm), BF16),
                v((toks, dm), BF16),
                v((toks, dm), BF16),
                v((2, toks, NSTATE), BF16),
                v((toks, xw), F32),
                v((PLANE, toks, qw), BF16),
                v((PLANE, toks, qw), BF16),
                v((2, PLANE, toks, NSTATE), BF16),
                v((PLANE, heads, toks), F32),
                v((NSTATE, qw), BF16),
                v((NSTATE, qw), BF16),
                v((NSTATE, qw), BF16),
                v((NSTATE, qw), BF16),
                v((8, qw), F32),
                v((8, qw), F32),
                v((span, qw), F32),
                v((PLANE, toks, qw), BF16),
                v((PLANE, toks, qw), BF16),
                pltpu.SemaphoreType.DMA((sems,)),
                pltpu.SemaphoreType.DMA((sems,)),
            ],
            compiler_params=pltpu.CompilerParams(
                collective_id=0, has_side_effects=True, vmem_limit_bytes=LIMIT
            ),
        )(
            frames, segment_ids, ln_gain, ln_bias, qkv_weight, out_weight, out_bias, adapter, rms_gain, x_weight,
            bc_weight, jnp.transpose(decay), skip_gain,
        )
        return encoded, mixed

    return per_device


def solution(mesh):
    placed = (
        P("tm", "head"),
        P(),
        P(),
        P(),
        P(None, None, "head"),
        P(None, "head"),
        P("head"),
        P("head", None),
        P(),
        P(None, "head"),
        P(None, "head"),
        P("tm", "head"),
        P("head"),
    )
    nt = mesh.shape["tm"]
    body = fused(nt) if mesh.shape["head"] == 2 and nt == 4 * PLANE else per_device
    return jax.shard_map(
        body,
        mesh=mesh,
        in_specs=placed,
        out_specs=(P("tm", "head"), P("tm", "head")),
        check_vma=False,
    )
```

```python
import functools
import math

import jax
import jax.numpy as jnp
from jax import lax
from jax.experimental import pallas as pl
from jax.experimental.pallas import tpu as pltpu
from jax.sharding import PartitionSpec as P

EHEAD_DIM = 64
HDIM = 64
NSTATE = 128
WINDOW = 256


EPSILON = 1e-05
HIGHEST = lax.Precision.HIGHEST


def with_halo(block, sides, width):
    for axis, dim in sides:
        count = lax.axis_size(axis)
        forward = [(i, i + 1) for i in range(count - 1)]
        backward = [(target, source) for source, target in forward]
        low = lax.ppermute(
            lax.slice_in_dim(block, block.shape[dim] - width, None, axis=dim), axis, forward
        )
        high = lax.ppermute(lax.slice_in_dim(block, 0, width, axis=dim), axis, backward)
        block = jnp.concatenate([low, block, high], axis=dim)
    return block


def prefix(part, axis, combine, identity):
    place = lax.axis_index(axis)
    gathered = jax.tree.map(lambda a: lax.all_gather(a, axis), part)
    state = jax.tree.map(lambda a, e: jnp.zeros_like(a) + jnp.asarray(e, a.dtype), part, identity)

    def one(hop, state):
        return combine(
            state, jax.tree.map(lambda a: lax.dynamic_index_in_dim(a, hop, 0, False), gathered)
        )

    return lax.fori_loop(0, place, one, state)


def layer_norm(values, gain, offset):
    center_mean = jnp.mean(values, axis=-1, keepdims=True)
    spread = jnp.mean(jnp.square(values - center_mean), axis=-1, keepdims=True)
    return (values - center_mean) * lax.rsqrt(spread + EPSILON) * gain + offset


def block_terms(inputs, b_in, c_in, decay):
    log_decay = jnp.log(decay)
    cumulative = jnp.cumsum(log_decay, axis=0)
    length = inputs.shape[0]
    sequence_indices = jnp.arange(length, dtype=jnp.int32)
    causal = sequence_indices[:, None] >= sequence_indices[None, :]
    log_gap = cumulative[:, None, :] - cumulative[None, :, :]
    weights = jnp.exp(jnp.where(causal[:, :, None], log_gap, -1e30))
    driven = inputs * (1.0 - decay)[:, :, None]
    affinity = jnp.dot(c_in, b_in.T, preferred_element_type=jnp.float32)
    within = jnp.einsum("tsh,shp->thp", affinity[:, :, None] * weights, driven, precision=HIGHEST)
    tail_decay = jnp.exp(cumulative[-1][None, :] - cumulative)
    end_state = jnp.einsum(
        "sh,shp,sn->hpn", tail_decay, driven, b_in.astype(jnp.float32), precision=HIGHEST
    )
    return (within, jnp.exp(cumulative), jnp.exp(cumulative[-1]), end_state)


def combine_states(earlier, later):
    return (earlier[0] * later[0], later[0][:, None, None] * earlier[1] + later[1])


def per_device(
    frames,
    segment_ids,
    ln_gain,
    ln_bias,
    qkv_weight,
    out_weight,
    out_bias,
    adapter,
    rms_gain,
    x_weight,
    bc_weight,
    decay,
    skip_gain,
):
    frame_count = frames.shape[0]
    margin = WINDOW
    tm_slot = lax.axis_index("tm")
    adapter_cols = lax.all_to_all(adapter, "head", split_axis=1, concat_axis=0, tiled=True)
    gathered = lax.all_gather(frames, "head", axis=1, tiled=True)
    normed = layer_norm(gathered.astype(jnp.float32), ln_gain, ln_bias).astype(jnp.bfloat16)
    queries = jnp.dot(normed, qkv_weight[0], preferred_element_type=jnp.float32).astype(
        jnp.bfloat16
    )
    keys_own = jnp.dot(normed, qkv_weight[1], preferred_element_type=jnp.float32).astype(
        jnp.bfloat16
    )
    values_own = jnp.dot(normed, qkv_weight[2], preferred_element_type=jnp.float32).astype(
        jnp.bfloat16
    )
    joined = jnp.concatenate([keys_own, values_own], axis=1)
    extended = with_halo(joined, (("tm", 0),), margin)
    head_width = keys_own.shape[1]
    keys_ext = extended[:, :head_width]
    values_ext = extended[:, head_width:]
    ids_pad = jnp.pad(segment_ids, (margin, margin), constant_values=-1)
    local_ids = lax.dynamic_slice_in_dim(
        ids_pad, tm_slot * frame_count, frame_count + 2 * margin, 0
    )
    heads_dev = queries.shape[1] // EHEAD_DIM
    qblock = math.gcd(frame_count, 512)
    span_rows = qblock + 2 * margin

    def attend(block_index):
        begin = block_index * qblock
        query_rows = queries.reshape(qblock, heads_dev, EHEAD_DIM)
        key_rows = keys_ext.reshape(span_rows, heads_dev, EHEAD_DIM)
        value_rows = values_ext.reshape(span_rows, heads_dev, EHEAD_DIM)
        query_ids = lax.dynamic_slice_in_dim(local_ids, begin + margin, qblock, 0)
        scores = jnp.einsum(
            "qhe,khe->hqk", query_rows, key_rows, preferred_element_type=jnp.float32
        ) * EHEAD_DIM ** (-0.5)
        allowed = query_ids[:, None] == local_ids[None, :]
        scores = jnp.where(allowed[None], scores, -1e30)
        peak = jnp.max(scores, axis=-1, keepdims=True)
        raised = jnp.exp(scores - peak)
        probs = (raised / jnp.sum(raised, axis=-1, keepdims=True)).astype(jnp.bfloat16)
        blended = jnp.einsum("hqk,khe->qhe", probs, value_rows, preferred_element_type=jnp.float32)
        return blended.astype(jnp.bfloat16).reshape(qblock, heads_dev * EHEAD_DIM)

    attended = lax.map(attend, jnp.arange(frame_count // qblock, dtype=jnp.int32)).reshape(
        frame_count, heads_dev * EHEAD_DIM
    )
    attention = jnp.dot(
        lax.all_gather(attended, "head", axis=1, tiled=True),
        out_weight,
        preferred_element_type=jnp.float32,
    )
    encoded = (frames.astype(jnp.float32) + attention + out_bias).astype(jnp.bfloat16)
    pooled = jnp.mean(
        encoded.astype(jnp.float32).reshape(frame_count // 4, 4, encoded.shape[1]), axis=1
    ).astype(jnp.bfloat16)
    pooled_all = lax.all_gather(pooled, "head", axis=1, tiled=True)
    column_part = jnp.dot(pooled_all, adapter_cols, preferred_element_type=jnp.float32)
    column_width = column_part.shape[1]
    column_sq = lax.psum(jnp.sum(jnp.square(column_part), axis=1), "head")
    column_gain = lax.dynamic_slice_in_dim(
        rms_gain, lax.axis_index("head") * column_width, column_width, 0
    )
    column_scaled = (
        column_part * lax.rsqrt(column_sq[:, None] / rms_gain.shape[0] + EPSILON) * column_gain
    ).astype(jnp.bfloat16)
    scaled = lax.all_gather(column_scaled, "head", axis=1, tiled=True)
    inputs = jax.nn.silu(jnp.dot(scaled, x_weight, preferred_element_type=jnp.float32)).astype(
        jnp.bfloat16
    )
    coupler_part = jax.nn.silu(
        jnp.dot(scaled, bc_weight, preferred_element_type=jnp.float32)
    ).astype(jnp.bfloat16)
    couplers = lax.all_gather(coupler_part, "head", axis=1, tiled=True)
    token_count = inputs.shape[0]
    state_heads = inputs.shape[1] // HDIM
    inputs_wide = inputs.astype(jnp.float32).reshape(token_count, state_heads, HDIM)
    c_rows = couplers[:, NSTATE:]
    within, growth, total_decay, end_state = block_terms(
        inputs_wide, couplers[:, :NSTATE], c_rows, decay
    )
    identity = (jnp.ones_like(total_decay), jnp.zeros_like(end_state))
    incoming = prefix((total_decay, end_state), "tm", combine_states, identity)
    from_state = jnp.einsum(
        "tn,hpn->thp", c_rows.astype(jnp.float32), incoming[1], precision=HIGHEST
    )
    result_rows = within + growth[:, :, None] * from_state + skip_gain[None, :, None] * inputs_wide
    mixed = result_rows.astype(jnp.bfloat16).reshape(token_count, state_heads * HDIM)
    return (encoded, mixed)


PLANE = 4
MESH = pl.DeviceIdType.MESH
VM = pl.BlockSpec(memory_space=pltpu.VMEM)
HB = pl.BlockSpec(memory_space=pltpu.HBM)
S_DECAY, S_K, S_V, S_ATT, S_CP, S_X, S_BC, S_T, S_S1, S_S2, S_Y, S_PART = 1, 4, 6, 8, 12, 13, 16, 19, 20, 21, 22, 25
PIECES = 5
S_OFF, S_ON = 30, 32
CHUNKS = 2
LIMIT = 63 * 1024 * 1024
F32 = jnp.float32
BF16 = jnp.bfloat16
NT = (((1,), (1,)), ((), ()))
TN = (((0,), (0,)), ((), ()))


def dot(a, b, dims=(((1,), (0,)), ((), ())), precision=None):
    return lax.dot_general(a, b, dims, precision=precision, preferred_element_type=F32)


def iota(shape, dim):
    return lax.broadcasted_iota(jnp.int32, shape, dim)


def fused_kernel(
    nt,
    frames_hbm, ids_hbm, lng_hbm, lnb_hbm, qkv_hbm, out_hbm, ob_hbm, ad_hbm, rms_hbm, x_hbm, bc_hbm, decay_hbm, skip_hbm,
    enc_o, mix_o,
    wqkv, wout, wad, wx, wbc, ids, ln_gain, ln_bias, out_bias, rms_gain, skip, wsem,
    fb, ob, nb, qb, kb, vb, mk, acc, mb, lb, att, pf, ps, pr, sc, cp, xin, xq, xb, bcb, db,
    sm, pm, s1, s2, tp, tn, wgt, dx, skx, yacc, yb, yr, send, recv,
):
    tm = lax.axis_index("tm")
    hy = lax.axis_index("head")
    z = tm // PLANE
    q = tm % PLANE
    planes = nt // PLANE
    rows = frames_hbm.shape[0]
    toks = decay_hbm.shape[1]
    span = PLANE * toks
    width = qb.shape[1]
    pairs = width // 128
    qw = xb.shape[2]
    qheads = qw // HDIM
    heads = decay_hbm.shape[0]

    loads = [
        pltpu.make_async_copy(src, dst, wsem.at[i])
        for i, (src, dst) in enumerate(
            [
                (qkv_hbm.at[1], wqkv.at[1]),
                (qkv_hbm.at[2], wqkv.at[2]),
                (qkv_hbm.at[0], wqkv.at[0]),
                (out_hbm, wout),
                (ad_hbm, wad),
                (bc_hbm, wbc),
                (x_hbm, wx),
                (frames_hbm, fb.at[hy]),
                (decay_hbm, db.at[q]),
                (ids_hbm, ids),
                (lng_hbm, ln_gain),
                (lnb_hbm, ln_bias),
                (ob_hbm, out_bias),
                (rms_hbm, rms_gain),
                (skip_hbm, skip),
            ]
        )
    ]

    def remote(src, dst, sem, device):
        return pltpu.make_async_remote_copy(
            src_ref=src, dst_ref=dst, send_sem=send.at[sem], recv_sem=recv.at[sem],
            device_id=device, device_id_type=MESH,
        )

    partner = {"head": 1 - hy}
    peers = [{"tm": z * PLANE + (q + k) % PLANE} for k in range(1, PLANE)]
    side = tm % 2
    off_at = (tm + nt - 1 + 2 * side) % nt
    on_at = tm + 1 - 2 * side
    off = {"tm": off_at}
    on = {"tm": on_at}
    has_off = jnp.logical_and(tm > 0, tm < nt - 1)
    bar = pltpu.get_barrier_semaphore()

    def greet(device):
        pl.semaphore_signal(bar, inc=1, device_id=device, device_id_type=MESH)

    greet(partner)
    for peer in peers:
        greet(peer)
    for dz in range(1, planes):
        greet({"tm": (tm + dz * PLANE) % nt})
    far = jnp.logical_and(has_off, jnp.logical_or(q == 0, q == PLANE - 1))

    @pl.when(far)
    def _():
        greet(off)

    for load in loads[7:]:
        load.start()
    for load in loads[:7]:
        load.start()
    pl.semaphore_wait(bar, PLANE + planes - 1 + far.astype(jnp.int32))

    c_frames = remote(frames_hbm, fb.at[hy], 0, partner)
    c_frames.start()
    step = rows // CHUNKS

    def off_copy(i):
        part = pl.ds(i * step, step)
        return remote(frames_hbm.at[part, :], ob.at[hy, part, :], S_OFF + i, off)

    def on_copy(i):
        part = pl.ds(i * step, step)
        return remote(ob.at[hy, part, :], ob.at[hy, part, :], S_ON + i, partner)

    def hand_on(i):
        @pl.when(has_off)
        def _():
            off_copy(i).wait_recv()
            on_copy(i).start()

    @pl.when(has_off)
    def _():
        for i in range(CHUNKS):
            off_copy(i).start()

    c_decay = [remote(decay_hbm, db.at[q], S_DECAY + k, peer) for k, peer in enumerate(peers)]
    for c in c_decay:
        c.start()

    for load in loads[7:]:
        load.wait()

    def id_row(at):
        return ids[pl.ds(pl.multiple_of(at * rows, rows), rows)].reshape(1, rows).astype(F32)

    own = id_row(tm)
    beside = id_row(on_at)
    beyond = jnp.where(has_off, id_row(off_at), -1.0)
    own_col = jnp.transpose(jnp.broadcast_to(own, (128, rows)))[:, :1]
    for i, row in enumerate((own, beside, beyond)):
        mk[:, i * rows : (i + 1) * rows] = jnp.where(own_col == row, 0.0, -1e30)

    def normalize(buf):
        both = jnp.concatenate([buf[0], buf[1]], axis=1).astype(F32)
        center = jnp.mean(both, axis=-1, keepdims=True)
        moved = both - center
        spread = jnp.mean(jnp.square(moved), axis=-1, keepdims=True)
        scale = ln_gain[...].reshape(1, -1)
        nb[...] = (moved * lax.rsqrt(spread + EPSILON) * scale + ln_bias[...].reshape(1, -1)).astype(BF16)

    for c in c_decay:
        c.wait()
    eye = jnp.where(iota((toks, toks), 0) == iota((toks, toks), 1), 1.0, 0.0)
    dec = jnp.concatenate([dot(eye, db[j], NT, HIGHEST) for j in range(PLANE)], axis=0)
    picked_row = q * qheads
    sel = jnp.where(iota((heads, 128), 0) == picked_row + iota((heads, 128), 1), 1.0, 0.0)
    sel = jnp.where(iota((heads, 128), 1) < qheads, sel, 0.0)
    first = (iota((heads, qw), 0) - picked_row) * HDIM
    wide = iota((heads, qw), 1)
    expand = jnp.where(jnp.logical_and(wide >= first, wide < first + HDIM), 1.0, 0.0)
    tri = jnp.where(iota((span, span), 0) >= iota((span, span), 1), 1.0, 0.0)
    cum = dot(tri, jnp.log(jnp.maximum(dec, 1e-37)), precision=HIGHEST)
    cum_col = dot(cum, sel, precision=HIGHEST)
    cum_row = jnp.transpose(cum_col)
    growth = dot(jnp.exp(cum), expand, precision=HIGHEST)
    drive = dot(1.0 - dec, expand, precision=HIGHEST)
    dx[0] = growth
    dx[1] = dot(jnp.exp(cum[span - 1 :, :] - cum) * (1.0 - dec), expand, precision=HIGHEST)
    dx[2] = drive
    skx[...] = dot(jnp.broadcast_to(skip[...].reshape(1, -1), (8, heads)), expand, precision=HIGHEST)
    causal = iota((span, span), 0) >= iota((span, span), 1)
    for h in range(qheads):
        gap = cum_col[:, h : h + 1] - cum_row[h : h + 1, :]
        wgt[h] = jnp.exp(jnp.where(causal, gap, -1e30))
    total = growth[span - 1 :, :]
    tp[...] = jnp.broadcast_to(total, (8, qw))
    later = {"tm": (tm + PLANE) % nt}
    latest = {"tm": (tm + 2 * PLANE) % nt}
    c_t = remote(tp, tn, S_T, later)
    c_s1 = remote(sm, s1, S_S1, later)
    c_s2 = remote(sm, s2, S_S2, latest)
    c_p = remote(pm, s2, S_S2, latest)

    @pl.when(z < planes - 1)
    def _():
        c_t.start()

    c_frames.wait()
    normalize(fb)

    def project(which, dst, scale):
        def tile(j, carry):
            cols = pl.ds(pl.multiple_of(j * 256, 256), 256)
            part = dot(nb[...], wqkv[which, :, cols]).astype(BF16)
            dst[:, cols] = part * scale if scale is not None else part
            return carry

        lax.fori_loop(0, width // 256, tile, 0)

    loads[0].wait()
    project(1, kb.at[0], None)
    c_k = remote(kb.at[0], kb.at[1], S_K, on)
    c_k.start()
    hand_on(0)
    loads[1].wait()
    project(2, vb.at[0], None)
    c_v = remote(vb.at[0], vb.at[1], S_V, on)
    c_v.start()
    hand_on(1)
    loads[2].wait()
    project(0, qb, jnp.asarray(EHEAD_DIM ** (-0.5), BF16))

    lane = iota((1, 128), 1)
    is_low = lane < EHEAD_DIM
    sides = (jnp.where(is_low, 1.0, 0.0).astype(BF16), jnp.where(is_low, 0.0, 1.0).astype(BF16))

    def within_chip(p, carry):
        cols = pl.ds(pl.multiple_of(p * 128, 128), 128)
        qp = qb[:, cols]
        kp = kb[:2, :, cols].reshape(2 * rows, 128)
        vp = vb[:2, :, cols].reshape(2 * rows, 128)
        got = []
        for side in sides:
            s = dot(qp * side, kp, NT) + mk[:, : 2 * rows]
            m = jnp.max(s, axis=-1, keepdims=True)
            e = jnp.exp(s - m)
            got.append((dot(e.astype(BF16), vp), m, jnp.sum(e, axis=-1, keepdims=True)))
        acc[p] = jnp.where(is_low, got[0][0], got[1][0])
        mb[p] = jnp.where(is_low, got[0][1], got[1][1])
        lb[p] = jnp.where(is_low, got[0][2], got[1][2])
        return carry

    c_k.wait()
    c_v.wait()
    lax.fori_loop(0, pairs, within_chip, 0)

    @pl.when(has_off)
    def _():
        for i in range(CHUNKS):
            on_copy(i).wait()
            off_copy(i).wait_send()
        normalize(ob)
        project(1, kb.at[2], None)
        project(2, vb.at[2], None)

    @pl.when(jnp.logical_not(has_off))
    def _():
        kb[2] = jnp.zeros((rows, width), BF16)
        vb[2] = jnp.zeros((rows, width), BF16)

    def att_copy(p):
        cols = pl.ds(pl.multiple_of(hy * width + p * 128, 128), 128)
        return remote(att.at[:, cols], att.at[:, cols], S_ATT + p, partner)

    def beyond_chip(p, carry):
        cols = pl.ds(pl.multiple_of(p * 128, 128), 128)
        qp = qb[:, cols]
        kp, vp = kb[2, :, cols], vb[2, :, cols]
        old_m, old_l = mb[p], lb[p]
        got = []
        for i, side in enumerate(sides):
            s = dot(qp * side, kp, NT) + mk[:, 2 * rows :]
            m1 = old_m[:, i * EHEAD_DIM : i * EHEAD_DIM + 1]
            m = jnp.maximum(jnp.max(s, axis=-1, keepdims=True), m1)
            e = jnp.exp(s - m)
            got.append((dot(e.astype(BF16), vp), m, jnp.sum(e, axis=-1, keepdims=True)))
        fade = jnp.exp(old_m - jnp.where(is_low, got[0][1], got[1][1]))
        total = old_l * fade + jnp.where(is_low, got[0][2], got[1][2])
        blended = acc[p] * fade + jnp.where(is_low, got[0][0], got[1][0])
        att[:, pl.ds(pl.multiple_of(hy * width + p * 128, 128), 128)] = (blended / total).astype(BF16)
        att_copy(p).start()
        return carry

    lax.fori_loop(0, pairs, beyond_chip, 0)
    for p in range(pairs):
        att_copy(p).wait()

    loads[3].wait()
    encoded = (fb[hy].astype(F32) + dot(att[...], wout[...]) + out_bias[...].reshape(1, -1)).astype(BF16)
    enc_o[...] = encoded
    rr, cc = iota((toks, rows), 0) * 4, iota((toks, rows), 1)
    pool = jnp.where(jnp.logical_and(cc >= rr, cc < rr + 4), 0.25, 0.0).astype(BF16)
    pooled = dot(pool, encoded).astype(BF16)

    loads[4].wait()

    piece = wad.shape[1] // PIECES

    def part_copy(j):
        cols = pl.ds(pl.multiple_of(j * piece, piece), piece)
        return remote(ps.at[:, cols], pr.at[:, cols], S_PART + j, partner)

    def adapt(j, carry):
        cols = pl.ds(pl.multiple_of(j * piece, piece), piece)
        part = dot(pooled, wad[:, cols])
        pf[:, cols] = part
        ps[:, cols] = part.astype(BF16)
        part_copy(j).start()
        return carry

    lax.fori_loop(0, PIECES, adapt, 0)

    for j in range(PIECES):
        part_copy(j).wait()
    proj = pf[...] + pr[...].astype(F32)
    square = jnp.mean(jnp.square(proj), axis=-1, keepdims=True)
    sc[...] = (proj * lax.rsqrt(square + EPSILON) * rms_gain[...].reshape(1, -1)).astype(BF16)

    def silu(v):
        return v / (1.0 + jnp.exp(-v))

    loads[5].wait()
    cp[hy] = silu(dot(sc[...], wbc[...])).astype(BF16)
    c_cp = remote(cp.at[hy], cp.at[hy], S_CP, partner)
    c_cp.start()
    loads[6].wait()

    def drive_in(j, carry):
        cols = pl.ds(pl.multiple_of(j * 256, 256), 256)
        xin[:, cols] = silu(dot(sc[...], wx[:, cols]))
        return carry

    tiles = wx.shape[1] // 256
    lax.fori_loop(0, tiles // 2 + 1, drive_in, 0)
    c_cp.wait()
    c_bc = [remote(cp, bcb.at[:, q], S_BC + k - 1, peers[k - 1]) for k in range(1, PLANE)]
    for c in c_bc:
        c.start()
    bcb[:, q] = cp[...]
    lax.fori_loop(tiles // 2 + 1, tiles, drive_in, 0)
    for j in range(PLANE):
        xq[j] = xin[:, j * qw : (j + 1) * qw].astype(BF16)
    c_x = [remote(xq.at[(q + k) % PLANE], xb.at[q], S_X + k - 1, peers[k - 1]) for k in range(1, PLANE)]
    for c in c_x:
        c.start()
    xb[q] = xq[q]
    for c in c_x:
        c.wait()
    for c in c_bc:
        c.wait()

    x_all = xb[...].reshape(span, qw).astype(F32)
    b_all = bcb[0].reshape(span, NSTATE)
    c_all = bcb[1].reshape(span, NSTATE)
    state = dot(b_all, (x_all * dx[1]).astype(BF16), TN)
    sm[...] = state.astype(BF16)

    @pl.when(z < planes - 1)
    def _():
        c_s1.start()

    @pl.when(z == 0)
    def _():
        c_s2.start()

    affinity = dot(c_all, b_all, NT)
    driven = (x_all * dx[2]).astype(BF16)

    def head_out(h, cols):
        return dot((affinity * wgt[h]).astype(BF16), cols)

    for h in range(0, qheads, 2):
        if h + 1 < qheads:
            cols = driven[:, h * HDIM : (h + 2) * HDIM]
            yacc[:, h * HDIM : (h + 2) * HDIM] = jnp.where(is_low, head_out(h, cols), head_out(h + 1, cols))
        else:
            yacc[:, h * HDIM : (h + 1) * HDIM] = head_out(h, driven[:, h * HDIM : (h + 1) * HDIM])
    yacc[...] = yacc[...] + skx[:1, :] * x_all

    @pl.when(z > 0)
    def _():
        c_t.wait_recv()
        c_s1.wait_recv()

    @pl.when(z == 1)
    def _():
        pm[...] = (sm[...].astype(F32) + tp[:1, :] * s1[...].astype(F32)).astype(BF16)
        c_p.start()

    @pl.when(z > 1)
    def _():
        c_s2.wait_recv()
        s1[...] = (s1[...].astype(F32) + tn[:1, :] * s2[...].astype(F32)).astype(BF16)

    @pl.when(z == 0)
    def _():
        s1[...] = jnp.zeros(s1.shape, BF16)

    y = yacc[...] + dx[0] * dot(c_all, s1[...])
    yb[...] = y.astype(BF16).reshape(PLANE, toks, qw)
    c_y = [remote(yb.at[(q + k) % PLANE], yr.at[q], S_Y + k - 1, peers[k - 1]) for k in range(1, PLANE)]
    for c in c_y:
        c.start()
    yr[q] = yb[q]
    @pl.when(z < planes - 1)
    def _():
        c_t.wait_send()
        c_s1.wait_send()

    @pl.when(z < planes - 2)
    def _():
        c_s2.wait_send()

    for c in c_y:
        c.wait()
    for j in range(PLANE):
        mix_o[:, j * qw : (j + 1) * qw] = yr[j]


def place_kernel(a, b, a_out, b_out, sem):
    moves = [pltpu.make_async_copy(a, a_out, sem.at[0]), pltpu.make_async_copy(b, b_out, sem.at[1])]
    for move in moves:
        move.start()
    for move in moves:
        move.wait()


def fused(nt):
    def per_device(frames, segment_ids, ln_gain, ln_bias, qkv_weight, out_weight, out_bias, adapter, rms_gain,
                   x_weight, bc_weight, decay, skip_gain):
        rows, half = frames.shape
        width = qkv_weight.shape[2]
        toks, heads = decay.shape
        dm = adapter.shape[1]
        xw = x_weight.shape[1]
        qw = xw // PLANE
        planes = nt // PLANE
        span = PLANE * toks
        pairs = width // 128
        sems = S_ON + CHUNKS
        v = pltpu.VMEM
        encoded, mixed = pl.pallas_call(
            functools.partial(fused_kernel, nt),
            out_shape=(
                jax.ShapeDtypeStruct((rows, half), BF16),
                jax.ShapeDtypeStruct((toks, xw), BF16),
            ),
            in_specs=[HB] * 13,
            out_specs=(VM, VM),
            scratch_shapes=[
                v(qkv_weight.shape, BF16),
                v(out_weight.shape, BF16),
                v(adapter.shape, BF16),
                v(x_weight.shape, BF16),
                v(bc_weight.shape, BF16),
                v(segment_ids.shape, jnp.int32),
                v(ln_gain.shape, F32),
                v(ln_bias.shape, F32),
                v(out_bias.shape, F32),
                v(rms_gain.shape, F32),
                v(skip_gain.shape, F32),
                pltpu.SemaphoreType.DMA((15,)),
                v((2, rows, half), BF16),
                v((2, rows, half), BF16),
                v((rows, 2 * half), BF16),
                v((rows, width), BF16),
                v((3, rows, width), BF16),
                v((3, rows, width), BF16),
                v((rows, 3 * rows), F32),
                v((pairs, rows, 128), F32),
                v((pairs, rows, 128), F32),
                v((pairs, rows, 128), F32),
                v((rows, 2 * width), BF16),
                v((toks, dm), F32),
                v((toks, dm), BF16),
                v((toks, dm), BF16),
                v((toks, dm), BF16),
                v((2, toks, NSTATE), BF16),
                v((toks, xw), F32),
                v((PLANE, toks, qw), BF16),
                v((PLANE, toks, qw), BF16),
                v((2, PLANE, toks, NSTATE), BF16),
                v((PLANE, heads, toks), F32),
                v((NSTATE, qw), BF16),
                v((NSTATE, qw), BF16),
                v((NSTATE, qw), BF16),
                v((NSTATE, qw), BF16),
                v((8, qw), F32),
                v((8, qw), F32),
                v((qw // HDIM, span, span), F32),
                v((3, span, qw), F32),
                v((8, qw), F32),
                v((span, qw), F32),
                v((PLANE, toks, qw), BF16),
                v((PLANE, toks, qw), BF16),
                pltpu.SemaphoreType.DMA((sems,)),
                pltpu.SemaphoreType.DMA((sems,)),
            ],
            compiler_params=pltpu.CompilerParams(
                collective_id=0, has_side_effects=True, vmem_limit_bytes=LIMIT
            ),
        )(
            frames, segment_ids, ln_gain, ln_bias, qkv_weight, out_weight, out_bias, adapter, rms_gain, x_weight,
            bc_weight, jnp.transpose(decay), skip_gain,
        )
        return pl.pallas_call(
            place_kernel,
            out_shape=(jax.ShapeDtypeStruct(encoded.shape, BF16), jax.ShapeDtypeStruct(mixed.shape, BF16)),
            in_specs=[HB, HB],
            out_specs=(HB, HB),
            scratch_shapes=[pltpu.SemaphoreType.DMA((2,))],
        )(encoded, mixed)

    return per_device


def solution(mesh):
    placed = (
        P("tm", "head"),
        P(),
        P(),
        P(),
        P(None, None, "head"),
        P(None, "head"),
        P("head"),
        P("head", None),
        P(),
        P(None, "head"),
        P(None, "head"),
        P("tm", "head"),
        P("head"),
    )
    nt = mesh.shape["tm"]
    body = fused(nt) if mesh.shape["head"] == 2 and nt == 4 * PLANE else per_device
    return jax.shard_map(
        body,
        mesh=mesh,
        in_specs=placed,
        out_specs=(P("tm", "head"), P("tm", "head")),
        check_vma=False,
    )
```

```python
import functools
import math

import jax
import jax.numpy as jnp
from jax import lax
from jax.experimental import pallas as pl
from jax.experimental.pallas import tpu as pltpu
from jax.sharding import PartitionSpec as P

EHEAD_DIM = 64
HDIM = 64
NSTATE = 128
WINDOW = 256


EPSILON = 1e-05
HIGHEST = lax.Precision.HIGHEST


def with_halo(block, sides, width):
    for axis, dim in sides:
        count = lax.axis_size(axis)
        forward = [(i, i + 1) for i in range(count - 1)]
        backward = [(target, source) for source, target in forward]
        low = lax.ppermute(
            lax.slice_in_dim(block, block.shape[dim] - width, None, axis=dim), axis, forward
        )
        high = lax.ppermute(lax.slice_in_dim(block, 0, width, axis=dim), axis, backward)
        block = jnp.concatenate([low, block, high], axis=dim)
    return block


def prefix(part, axis, combine, identity):
    place = lax.axis_index(axis)
    gathered = jax.tree.map(lambda a: lax.all_gather(a, axis), part)
    state = jax.tree.map(lambda a, e: jnp.zeros_like(a) + jnp.asarray(e, a.dtype), part, identity)

    def one(hop, state):
        return combine(
            state, jax.tree.map(lambda a: lax.dynamic_index_in_dim(a, hop, 0, False), gathered)
        )

    return lax.fori_loop(0, place, one, state)


def layer_norm(values, gain, offset):
    center_mean = jnp.mean(values, axis=-1, keepdims=True)
    spread = jnp.mean(jnp.square(values - center_mean), axis=-1, keepdims=True)
    return (values - center_mean) * lax.rsqrt(spread + EPSILON) * gain + offset


def block_terms(inputs, b_in, c_in, decay):
    log_decay = jnp.log(decay)
    cumulative = jnp.cumsum(log_decay, axis=0)
    length = inputs.shape[0]
    sequence_indices = jnp.arange(length, dtype=jnp.int32)
    causal = sequence_indices[:, None] >= sequence_indices[None, :]
    log_gap = cumulative[:, None, :] - cumulative[None, :, :]
    weights = jnp.exp(jnp.where(causal[:, :, None], log_gap, -1e30))
    driven = inputs * (1.0 - decay)[:, :, None]
    affinity = jnp.dot(c_in, b_in.T, preferred_element_type=jnp.float32)
    within = jnp.einsum("tsh,shp->thp", affinity[:, :, None] * weights, driven, precision=HIGHEST)
    tail_decay = jnp.exp(cumulative[-1][None, :] - cumulative)
    end_state = jnp.einsum(
        "sh,shp,sn->hpn", tail_decay, driven, b_in.astype(jnp.float32), precision=HIGHEST
    )
    return (within, jnp.exp(cumulative), jnp.exp(cumulative[-1]), end_state)


def combine_states(earlier, later):
    return (earlier[0] * later[0], later[0][:, None, None] * earlier[1] + later[1])


def per_device(
    frames,
    segment_ids,
    ln_gain,
    ln_bias,
    qkv_weight,
    out_weight,
    out_bias,
    adapter,
    rms_gain,
    x_weight,
    bc_weight,
    decay,
    skip_gain,
):
    frame_count = frames.shape[0]
    margin = WINDOW
    tm_slot = lax.axis_index("tm")
    adapter_cols = lax.all_to_all(adapter, "head", split_axis=1, concat_axis=0, tiled=True)
    gathered = lax.all_gather(frames, "head", axis=1, tiled=True)
    normed = layer_norm(gathered.astype(jnp.float32), ln_gain, ln_bias).astype(jnp.bfloat16)
    queries = jnp.dot(normed, qkv_weight[0], preferred_element_type=jnp.float32).astype(
        jnp.bfloat16
    )
    keys_own = jnp.dot(normed, qkv_weight[1], preferred_element_type=jnp.float32).astype(
        jnp.bfloat16
    )
    values_own = jnp.dot(normed, qkv_weight[2], preferred_element_type=jnp.float32).astype(
        jnp.bfloat16
    )
    joined = jnp.concatenate([keys_own, values_own], axis=1)
    extended = with_halo(joined, (("tm", 0),), margin)
    head_width = keys_own.shape[1]
    keys_ext = extended[:, :head_width]
    values_ext = extended[:, head_width:]
    ids_pad = jnp.pad(segment_ids, (margin, margin), constant_values=-1)
    local_ids = lax.dynamic_slice_in_dim(
        ids_pad, tm_slot * frame_count, frame_count + 2 * margin, 0
    )
    heads_dev = queries.shape[1] // EHEAD_DIM
    qblock = math.gcd(frame_count, 512)
    span_rows = qblock + 2 * margin

    def attend(block_index):
        begin = block_index * qblock
        query_rows = queries.reshape(qblock, heads_dev, EHEAD_DIM)
        key_rows = keys_ext.reshape(span_rows, heads_dev, EHEAD_DIM)
        value_rows = values_ext.reshape(span_rows, heads_dev, EHEAD_DIM)
        query_ids = lax.dynamic_slice_in_dim(local_ids, begin + margin, qblock, 0)
        scores = jnp.einsum(
            "qhe,khe->hqk", query_rows, key_rows, preferred_element_type=jnp.float32
        ) * EHEAD_DIM ** (-0.5)
        allowed = query_ids[:, None] == local_ids[None, :]
        scores = jnp.where(allowed[None], scores, -1e30)
        peak = jnp.max(scores, axis=-1, keepdims=True)
        raised = jnp.exp(scores - peak)
        probs = (raised / jnp.sum(raised, axis=-1, keepdims=True)).astype(jnp.bfloat16)
        blended = jnp.einsum("hqk,khe->qhe", probs, value_rows, preferred_element_type=jnp.float32)
        return blended.astype(jnp.bfloat16).reshape(qblock, heads_dev * EHEAD_DIM)

    attended = lax.map(attend, jnp.arange(frame_count // qblock, dtype=jnp.int32)).reshape(
        frame_count, heads_dev * EHEAD_DIM
    )
    attention = jnp.dot(
        lax.all_gather(attended, "head", axis=1, tiled=True),
        out_weight,
        preferred_element_type=jnp.float32,
    )
    encoded = (frames.astype(jnp.float32) + attention + out_bias).astype(jnp.bfloat16)
    pooled = jnp.mean(
        encoded.astype(jnp.float32).reshape(frame_count // 4, 4, encoded.shape[1]), axis=1
    ).astype(jnp.bfloat16)
    pooled_all = lax.all_gather(pooled, "head", axis=1, tiled=True)
    column_part = jnp.dot(pooled_all, adapter_cols, preferred_element_type=jnp.float32)
    column_width = column_part.shape[1]
    column_sq = lax.psum(jnp.sum(jnp.square(column_part), axis=1), "head")
    column_gain = lax.dynamic_slice_in_dim(
        rms_gain, lax.axis_index("head") * column_width, column_width, 0
    )
    column_scaled = (
        column_part * lax.rsqrt(column_sq[:, None] / rms_gain.shape[0] + EPSILON) * column_gain
    ).astype(jnp.bfloat16)
    scaled = lax.all_gather(column_scaled, "head", axis=1, tiled=True)
    inputs = jax.nn.silu(jnp.dot(scaled, x_weight, preferred_element_type=jnp.float32)).astype(
        jnp.bfloat16
    )
    coupler_part = jax.nn.silu(
        jnp.dot(scaled, bc_weight, preferred_element_type=jnp.float32)
    ).astype(jnp.bfloat16)
    couplers = lax.all_gather(coupler_part, "head", axis=1, tiled=True)
    token_count = inputs.shape[0]
    state_heads = inputs.shape[1] // HDIM
    inputs_wide = inputs.astype(jnp.float32).reshape(token_count, state_heads, HDIM)
    c_rows = couplers[:, NSTATE:]
    within, growth, total_decay, end_state = block_terms(
        inputs_wide, couplers[:, :NSTATE], c_rows, decay
    )
    identity = (jnp.ones_like(total_decay), jnp.zeros_like(end_state))
    incoming = prefix((total_decay, end_state), "tm", combine_states, identity)
    from_state = jnp.einsum(
        "tn,hpn->thp", c_rows.astype(jnp.float32), incoming[1], precision=HIGHEST
    )
    result_rows = within + growth[:, :, None] * from_state + skip_gain[None, :, None] * inputs_wide
    mixed = result_rows.astype(jnp.bfloat16).reshape(token_count, state_heads * HDIM)
    return (encoded, mixed)


PLANE = 4
MESH = pl.DeviceIdType.MESH
VM = pl.BlockSpec(memory_space=pltpu.VMEM)
HB = pl.BlockSpec(memory_space=pltpu.HBM)
S_DECAY, S_K, S_V, S_ATT, S_CP, S_X, S_BC, S_T, S_S1, S_S2, S_Y, S_PART = 1, 4, 6, 8, 12, 13, 16, 19, 20, 21, 22, 25
PIECES = 5
S_OFF, S_ON = 30, 32
CHUNKS = 2
LIMIT = 63 * 1024 * 1024
F32 = jnp.float32
BF16 = jnp.bfloat16
NT = (((1,), (1,)), ((), ()))
TN = (((0,), (0,)), ((), ()))


def dot(a, b, dims=(((1,), (0,)), ((), ())), precision=None):
    return lax.dot_general(a, b, dims, precision=precision, preferred_element_type=F32)


def iota(shape, dim):
    return lax.broadcasted_iota(jnp.int32, shape, dim)


def fused_kernel(
    nt,
    frames_hbm, ids_hbm, lng_hbm, lnb_hbm, qkv_hbm, out_hbm, ob_hbm, ad_hbm, rms_hbm, x_hbm, bc_hbm, decay_hbm, skip_hbm,
    enc_o, mix_o,
    wqkv, wout, wad, wx, wbc, ids, ln_gain, ln_bias, out_bias, rms_gain, skip, wsem,
    fb, ob, nb, qb, kb, vb, mk, acc, mb, lb, att, pf, ps, pr, sc, cp, xin, xq, xb, bcb, db,
    sm, pm, s1, s2, tp, tn, wgt, dx, skx, yacc, yb, yr, send, recv,
):
    tm = lax.axis_index("tm")
    hy = lax.axis_index("head")
    z = tm // PLANE
    q = tm % PLANE
    planes = nt // PLANE
    rows = frames_hbm.shape[0]
    toks = decay_hbm.shape[1]
    span = PLANE * toks
    width = qb.shape[1]
    pairs = width // 128
    qw = xb.shape[2]
    qheads = qw // HDIM
    heads = decay_hbm.shape[0]

    loads = [
        pltpu.make_async_copy(src, dst, wsem.at[i])
        for i, (src, dst) in enumerate(
            [
                (qkv_hbm.at[1], wqkv.at[1]),
                (qkv_hbm.at[2], wqkv.at[2]),
                (qkv_hbm.at[0], wqkv.at[0]),
                (out_hbm, wout),
                (ad_hbm, wad),
                (bc_hbm, wbc),
                (x_hbm, wx),
                (frames_hbm, fb.at[hy]),
                (decay_hbm, db.at[q]),
                (ids_hbm, ids),
                (lng_hbm, ln_gain),
                (lnb_hbm, ln_bias),
                (ob_hbm, out_bias),
                (rms_hbm, rms_gain),
                (skip_hbm, skip),
            ]
        )
    ]

    def remote(src, dst, sem, device):
        return pltpu.make_async_remote_copy(
            src_ref=src, dst_ref=dst, send_sem=send.at[sem], recv_sem=recv.at[sem],
            device_id=device, device_id_type=MESH,
        )

    partner = {"head": 1 - hy}
    peers = [{"tm": z * PLANE + (q + k) % PLANE} for k in range(1, PLANE)]
    side = tm % 2
    off_at = (tm + nt - 1 + 2 * side) % nt
    on_at = tm + 1 - 2 * side
    off = {"tm": off_at}
    on = {"tm": on_at}
    has_off = jnp.logical_and(tm > 0, tm < nt - 1)
    bar = pltpu.get_barrier_semaphore()

    def greet(device):
        pl.semaphore_signal(bar, inc=1, device_id=device, device_id_type=MESH)

    greet(partner)
    for peer in peers:
        greet(peer)
    for dz in range(1, planes):
        greet({"tm": (tm + dz * PLANE) % nt})
    far = jnp.logical_and(has_off, jnp.logical_or(q == 0, q == PLANE - 1))

    @pl.when(far)
    def _():
        greet(off)

    for load in loads[7:]:
        load.start()
    for load in loads[:7]:
        load.start()
    pl.semaphore_wait(bar, PLANE + planes - 1 + far.astype(jnp.int32))

    c_frames = remote(frames_hbm, fb.at[hy], 0, partner)
    c_frames.start()
    step = rows // CHUNKS

    def off_copy(i):
        part = pl.ds(i * step, step)
        return remote(frames_hbm.at[part, :], ob.at[hy, part, :], S_OFF + i, off)

    def on_copy(i):
        part = pl.ds(i * step, step)
        return remote(ob.at[hy, part, :], ob.at[hy, part, :], S_ON + i, partner)

    def hand_on(i):
        @pl.when(has_off)
        def _():
            off_copy(i).wait_recv()
            on_copy(i).start()

    @pl.when(has_off)
    def _():
        for i in range(CHUNKS):
            off_copy(i).start()

    c_decay = [remote(decay_hbm, db.at[q], S_DECAY + k, peer) for k, peer in enumerate(peers)]
    for c in c_decay:
        c.start()

    for load in loads[7:]:
        load.wait()

    def id_row(at):
        return ids[pl.ds(pl.multiple_of(at * rows, rows), rows)].reshape(1, rows).astype(F32)

    own = id_row(tm)
    beside = id_row(on_at)
    beyond = jnp.where(has_off, id_row(off_at), -1.0)
    own_col = jnp.transpose(jnp.broadcast_to(own, (128, rows)))[:, :1]
    for i, row in enumerate((own, beside, beyond)):
        mk[:, i * rows : (i + 1) * rows] = jnp.where(own_col == row, 0.0, -1e30)

    def normalize(buf):
        both = jnp.concatenate([buf[0], buf[1]], axis=1).astype(F32)
        center = jnp.mean(both, axis=-1, keepdims=True)
        moved = both - center
        spread = jnp.mean(jnp.square(moved), axis=-1, keepdims=True)
        scale = ln_gain[...].reshape(1, -1)
        nb[...] = (moved * lax.rsqrt(spread + EPSILON) * scale + ln_bias[...].reshape(1, -1)).astype(BF16)

    is_low = iota((1, 128), 1) < EHEAD_DIM

    for c in c_decay:
        c.wait()
    blocks = []
    for j in range(PLANE):
        block = db[j]
        mine = block[:qheads, :]
        for i in range(1, PLANE):
            mine = jnp.where(q == i, block[i * qheads : (i + 1) * qheads, :], mine)
        blocks.append(mine)
    dec_row = jnp.concatenate(blocks, axis=1)
    dec_row = jnp.concatenate([dec_row, jnp.ones((8 - qheads, span), F32)], axis=0)
    logs = jnp.log(jnp.maximum(dec_row, 1e-37))
    l0 = logs.astype(BF16).astype(F32)
    l1 = (logs - l0).astype(BF16).astype(F32)
    l2 = logs - l0 - l1
    upto = jnp.where(iota((span, span), 0) <= iota((span, span), 1), 1.0, 0.0).astype(BF16)
    summed = dot(jnp.concatenate([l0, l1, l2, jnp.zeros((8, span), F32)], axis=0).astype(BF16), upto)
    cum_row = summed[:8] + summed[8:16] + summed[16:24]
    cols = jnp.transpose(jnp.concatenate([cum_row, dec_row, jnp.zeros((112, span), F32)], axis=0))
    cum_col = cols[:, :8]
    rest = 1.0 - cols[:, 8:16]
    grow = jnp.exp(cum_col)
    tail = jnp.exp(cum_col[span - 1 :, :] - cum_col) * rest

    def widen(narrow, dst):
        for h in range(0, qheads, 2):
            first = jnp.broadcast_to(narrow[:, h : h + 1], (narrow.shape[0], 128))
            if h + 1 < qheads:
                second = jnp.broadcast_to(narrow[:, h + 1 : h + 2], (narrow.shape[0], 128))
                dst[:, h * HDIM : (h + 2) * HDIM] = jnp.where(is_low, first, second)
            else:
                dst[:, h * HDIM : (h + 1) * HDIM] = first[:, :HDIM]

    widen(grow, dx.at[0])
    widen(tail, dx.at[1])
    widen(rest, dx.at[2])
    gains = skip[...].reshape(1, -1)
    own_gain = gains[:, :qheads]
    for i in range(1, PLANE):
        own_gain = jnp.where(q == i, gains[:, i * qheads : (i + 1) * qheads], own_gain)
    widen(jnp.broadcast_to(own_gain, (8, qheads)), skx)
    causal = iota((span, span), 0) >= iota((span, span), 1)
    for h in range(qheads):
        gap = cum_col[:, h : h + 1] - cum_row[h : h + 1, :]
        wgt[h] = jnp.exp(jnp.where(causal, gap, -1e30))
    total = dx[0, span - 1 :, :]
    tp[...] = jnp.broadcast_to(total, (8, qw))
    later = {"tm": (tm + PLANE) % nt}
    latest = {"tm": (tm + 2 * PLANE) % nt}
    c_t = remote(tp, tn, S_T, later)
    c_s1 = remote(sm, s1, S_S1, later)
    c_s2 = remote(sm, s2, S_S2, latest)
    c_p = remote(pm, s2, S_S2, latest)

    @pl.when(z < planes - 1)
    def _():
        c_t.start()

    c_frames.wait()
    normalize(fb)

    def project(which, dst, scale):
        def tile(j, carry):
            cols = pl.ds(pl.multiple_of(j * 256, 256), 256)
            part = dot(nb[...], wqkv[which, :, cols]).astype(BF16)
            dst[:, cols] = part * scale if scale is not None else part
            return carry

        lax.fori_loop(0, width // 256, tile, 0)

    loads[0].wait()
    project(1, kb.at[0], None)
    c_k = remote(kb.at[0], kb.at[1], S_K, on)
    c_k.start()
    hand_on(0)
    loads[1].wait()
    project(2, vb.at[0], None)
    c_v = remote(vb.at[0], vb.at[1], S_V, on)
    c_v.start()
    hand_on(1)
    loads[2].wait()
    project(0, qb, jnp.asarray(EHEAD_DIM ** (-0.5), BF16))

    sides = (jnp.where(is_low, 1.0, 0.0).astype(BF16), jnp.where(is_low, 0.0, 1.0).astype(BF16))

    def within_chip(p, carry):
        cols = pl.ds(pl.multiple_of(p * 128, 128), 128)
        qp = qb[:, cols]
        kp = kb[:2, :, cols].reshape(2 * rows, 128)
        vp = vb[:2, :, cols].reshape(2 * rows, 128)
        got = []
        for side in sides:
            s = dot(qp * side, kp, NT) + mk[:, : 2 * rows]
            m = jnp.max(s, axis=-1, keepdims=True)
            e = jnp.exp(s - m)
            got.append((dot(e.astype(BF16), vp), m, jnp.sum(e, axis=-1, keepdims=True)))
        acc[p] = jnp.where(is_low, got[0][0], got[1][0])
        mb[p] = jnp.where(is_low, got[0][1], got[1][1])
        lb[p] = jnp.where(is_low, got[0][2], got[1][2])
        return carry

    c_k.wait()
    c_v.wait()
    lax.fori_loop(0, pairs, within_chip, 0)

    @pl.when(has_off)
    def _():
        for i in range(CHUNKS):
            on_copy(i).wait()
            off_copy(i).wait_send()
        normalize(ob)
        project(1, kb.at[2], None)
        project(2, vb.at[2], None)

    @pl.when(jnp.logical_not(has_off))
    def _():
        kb[2] = jnp.zeros((rows, width), BF16)
        vb[2] = jnp.zeros((rows, width), BF16)

    def att_copy(p):
        cols = pl.ds(pl.multiple_of(hy * width + p * 128, 128), 128)
        return remote(att.at[:, cols], att.at[:, cols], S_ATT + p, partner)

    def beyond_chip(p, carry):
        cols = pl.ds(pl.multiple_of(p * 128, 128), 128)
        qp = qb[:, cols]
        kp, vp = kb[2, :, cols], vb[2, :, cols]
        old_m, old_l = mb[p], lb[p]
        got = []
        for i, side in enumerate(sides):
            s = dot(qp * side, kp, NT) + mk[:, 2 * rows :]
            m1 = old_m[:, i * EHEAD_DIM : i * EHEAD_DIM + 1]
            m = jnp.maximum(jnp.max(s, axis=-1, keepdims=True), m1)
            e = jnp.exp(s - m)
            got.append((dot(e.astype(BF16), vp), m, jnp.sum(e, axis=-1, keepdims=True)))
        fade = jnp.exp(old_m - jnp.where(is_low, got[0][1], got[1][1]))
        total = old_l * fade + jnp.where(is_low, got[0][2], got[1][2])
        blended = acc[p] * fade + jnp.where(is_low, got[0][0], got[1][0])
        att[:, pl.ds(pl.multiple_of(hy * width + p * 128, 128), 128)] = (blended / total).astype(BF16)
        att_copy(p).start()
        return carry

    lax.fori_loop(0, pairs, beyond_chip, 0)
    for p in range(pairs):
        att_copy(p).wait()

    loads[3].wait()
    encoded = (fb[hy].astype(F32) + dot(att[...], wout[...]) + out_bias[...].reshape(1, -1)).astype(BF16)
    enc_o[...] = encoded
    rr, cc = iota((toks, rows), 0) * 4, iota((toks, rows), 1)
    pool = jnp.where(jnp.logical_and(cc >= rr, cc < rr + 4), 0.25, 0.0).astype(BF16)
    pooled = dot(pool, encoded).astype(BF16)

    loads[4].wait()

    piece = wad.shape[1] // PIECES

    def part_copy(j):
        cols = pl.ds(pl.multiple_of(j * piece, piece), piece)
        return remote(ps.at[:, cols], pr.at[:, cols], S_PART + j, partner)

    def adapt(j, carry):
        cols = pl.ds(pl.multiple_of(j * piece, piece), piece)
        part = dot(pooled, wad[:, cols])
        pf[:, cols] = part
        ps[:, cols] = part.astype(BF16)
        part_copy(j).start()
        return carry

    lax.fori_loop(0, PIECES, adapt, 0)

    for j in range(PIECES):
        part_copy(j).wait()
    proj = pf[...] + pr[...].astype(F32)
    square = jnp.mean(jnp.square(proj), axis=-1, keepdims=True)
    sc[...] = (proj * lax.rsqrt(square + EPSILON) * rms_gain[...].reshape(1, -1)).astype(BF16)

    def silu(v):
        return v / (1.0 + jnp.exp(-v))

    loads[5].wait()
    cp[hy] = silu(dot(sc[...], wbc[...])).astype(BF16)
    c_cp = remote(cp.at[hy], cp.at[hy], S_CP, partner)
    c_cp.start()
    loads[6].wait()

    def drive_in(j, carry):
        cols = pl.ds(pl.multiple_of(j * 256, 256), 256)
        xin[:, cols] = silu(dot(sc[...], wx[:, cols]))
        return carry

    tiles = wx.shape[1] // 256
    lax.fori_loop(0, tiles // 2 + 1, drive_in, 0)
    c_cp.wait()
    c_bc = [remote(cp, bcb.at[:, q], S_BC + k - 1, peers[k - 1]) for k in range(1, PLANE)]
    for c in c_bc:
        c.start()
    bcb[:, q] = cp[...]
    lax.fori_loop(tiles // 2 + 1, tiles, drive_in, 0)
    for j in range(PLANE):
        xq[j] = xin[:, j * qw : (j + 1) * qw].astype(BF16)
    c_x = [remote(xq.at[(q + k) % PLANE], xb.at[q], S_X + k - 1, peers[k - 1]) for k in range(1, PLANE)]
    for c in c_x:
        c.start()
    xb[q] = xq[q]
    for c in c_x:
        c.wait()
    for c in c_bc:
        c.wait()

    x_all = xb[...].reshape(span, qw).astype(F32)
    b_all = bcb[0].reshape(span, NSTATE)
    c_all = bcb[1].reshape(span, NSTATE)
    state = dot(b_all, (x_all * dx[1]).astype(BF16), TN)
    sm[...] = state.astype(BF16)

    @pl.when(z < planes - 1)
    def _():
        c_s1.start()

    @pl.when(z == 0)
    def _():
        c_s2.start()

    affinity = dot(c_all, b_all, NT)
    driven = (x_all * dx[2]).astype(BF16)

    def head_out(h, cols):
        return dot((affinity * wgt[h]).astype(BF16), cols)

    for h in range(0, qheads, 2):
        if h + 1 < qheads:
            cols = driven[:, h * HDIM : (h + 2) * HDIM]
            yacc[:, h * HDIM : (h + 2) * HDIM] = jnp.where(is_low, head_out(h, cols), head_out(h + 1, cols))
        else:
            yacc[:, h * HDIM : (h + 1) * HDIM] = head_out(h, driven[:, h * HDIM : (h + 1) * HDIM])
    yacc[...] = yacc[...] + skx[:1, :] * x_all

    @pl.when(z > 0)
    def _():
        c_t.wait_recv()
        c_s1.wait_recv()

    @pl.when(z == 1)
    def _():
        pm[...] = (sm[...].astype(F32) + tp[:1, :] * s1[...].astype(F32)).astype(BF16)
        c_p.start()

    @pl.when(z > 1)
    def _():
        c_s2.wait_recv()
        s1[...] = (s1[...].astype(F32) + tn[:1, :] * s2[...].astype(F32)).astype(BF16)

    @pl.when(z == 0)
    def _():
        s1[...] = jnp.zeros(s1.shape, BF16)

    y = yacc[...] + dx[0] * dot(c_all, s1[...])
    yb[...] = y.astype(BF16).reshape(PLANE, toks, qw)
    c_y = [remote(yb.at[(q + k) % PLANE], yr.at[q], S_Y + k - 1, peers[k - 1]) for k in range(1, PLANE)]
    for c in c_y:
        c.start()
    yr[q] = yb[q]
    @pl.when(z < planes - 1)
    def _():
        c_t.wait_send()
        c_s1.wait_send()

    @pl.when(z < planes - 2)
    def _():
        c_s2.wait_send()

    for c in c_y:
        c.wait()
    for j in range(PLANE):
        mix_o[:, j * qw : (j + 1) * qw] = yr[j]


def place_kernel(a, b, a_out, b_out):
    a_out[...] = a[...]
    b_out[...] = b[...]


def fused(nt):
    def per_device(frames, segment_ids, ln_gain, ln_bias, qkv_weight, out_weight, out_bias, adapter, rms_gain,
                   x_weight, bc_weight, decay, skip_gain):
        rows, half = frames.shape
        width = qkv_weight.shape[2]
        toks, heads = decay.shape
        dm = adapter.shape[1]
        xw = x_weight.shape[1]
        qw = xw // PLANE
        planes = nt // PLANE
        span = PLANE * toks
        pairs = width // 128
        sems = S_ON + CHUNKS
        v = pltpu.VMEM
        encoded, mixed = pl.pallas_call(
            functools.partial(fused_kernel, nt),
            out_shape=(
                jax.ShapeDtypeStruct((rows, half), BF16),
                jax.ShapeDtypeStruct((toks, xw), BF16),
            ),
            in_specs=[HB] * 13,
            out_specs=(VM, VM),
            scratch_shapes=[
                v(qkv_weight.shape, BF16),
                v(out_weight.shape, BF16),
                v(adapter.shape, BF16),
                v(x_weight.shape, BF16),
                v(bc_weight.shape, BF16),
                v(segment_ids.shape, jnp.int32),
                v(ln_gain.shape, F32),
                v(ln_bias.shape, F32),
                v(out_bias.shape, F32),
                v(rms_gain.shape, F32),
                v(skip_gain.shape, F32),
                pltpu.SemaphoreType.DMA((15,)),
                v((2, rows, half), BF16),
                v((2, rows, half), BF16),
                v((rows, 2 * half), BF16),
                v((rows, width), BF16),
                v((3, rows, width), BF16),
                v((3, rows, width), BF16),
                v((rows, 3 * rows), F32),
                v((pairs, rows, 128), F32),
                v((pairs, rows, 128), F32),
                v((pairs, rows, 128), F32),
                v((rows, 2 * width), BF16),
                v((toks, dm), F32),
                v((toks, dm), BF16),
                v((toks, dm), BF16),
                v((toks, dm), BF16),
                v((2, toks, NSTATE), BF16),
                v((toks, xw), F32),
                v((PLANE, toks, qw), BF16),
                v((PLANE, toks, qw), BF16),
                v((2, PLANE, toks, NSTATE), BF16),
                v((PLANE, heads, toks), F32),
                v((NSTATE, qw), BF16),
                v((NSTATE, qw), BF16),
                v((NSTATE, qw), BF16),
                v((NSTATE, qw), BF16),
                v((8, qw), F32),
                v((8, qw), F32),
                v((qw // HDIM, span, span), F32),
                v((3, span, qw), F32),
                v((8, qw), F32),
                v((span, qw), F32),
                v((PLANE, toks, qw), BF16),
                v((PLANE, toks, qw), BF16),
                pltpu.SemaphoreType.DMA((sems,)),
                pltpu.SemaphoreType.DMA((sems,)),
            ],
            compiler_params=pltpu.CompilerParams(
                collective_id=0, has_side_effects=True, vmem_limit_bytes=LIMIT
            ),
        )(
            frames, segment_ids, ln_gain, ln_bias, qkv_weight, out_weight, out_bias, adapter, rms_gain, x_weight,
            bc_weight, jnp.transpose(decay), skip_gain,
        )
        return pl.pallas_call(
            place_kernel,
            out_shape=(jax.ShapeDtypeStruct(encoded.shape, BF16), jax.ShapeDtypeStruct(mixed.shape, BF16)),
            in_specs=[VM, VM],
            out_specs=(VM, VM),
        )(encoded, mixed)

    return per_device


def solution(mesh):
    placed = (
        P("tm", "head"),
        P(),
        P(),
        P(),
        P(None, None, "head"),
        P(None, "head"),
        P("head"),
        P("head", None),
        P(),
        P(None, "head"),
        P(None, "head"),
        P("tm", "head"),
        P("head"),
    )
    nt = mesh.shape["tm"]
    body = fused(nt) if mesh.shape["head"] == 2 and nt == 4 * PLANE else per_device
    return jax.shard_map(
        body,
        mesh=mesh,
        in_specs=placed,
        out_specs=(P("tm", "head"), P("tm", "head")),
        check_vma=False,
    )
```

```python
import functools
import math

import jax
import jax.numpy as jnp
from jax import lax
from jax.experimental import pallas as pl
from jax.experimental.pallas import tpu as pltpu
from jax.sharding import PartitionSpec as P

EHEAD_DIM = 64
HDIM = 64
NSTATE = 128
WINDOW = 256


EPSILON = 1e-05
HIGHEST = lax.Precision.HIGHEST


def with_halo(block, sides, width):
    for axis, dim in sides:
        count = lax.axis_size(axis)
        forward = [(i, i + 1) for i in range(count - 1)]
        backward = [(target, source) for source, target in forward]
        low = lax.ppermute(
            lax.slice_in_dim(block, block.shape[dim] - width, None, axis=dim), axis, forward
        )
        high = lax.ppermute(lax.slice_in_dim(block, 0, width, axis=dim), axis, backward)
        block = jnp.concatenate([low, block, high], axis=dim)
    return block


def prefix(part, axis, combine, identity):
    place = lax.axis_index(axis)
    gathered = jax.tree.map(lambda a: lax.all_gather(a, axis), part)
    state = jax.tree.map(lambda a, e: jnp.zeros_like(a) + jnp.asarray(e, a.dtype), part, identity)

    def one(hop, state):
        return combine(
            state, jax.tree.map(lambda a: lax.dynamic_index_in_dim(a, hop, 0, False), gathered)
        )

    return lax.fori_loop(0, place, one, state)


def layer_norm(values, gain, offset):
    center_mean = jnp.mean(values, axis=-1, keepdims=True)
    spread = jnp.mean(jnp.square(values - center_mean), axis=-1, keepdims=True)
    return (values - center_mean) * lax.rsqrt(spread + EPSILON) * gain + offset


def block_terms(inputs, b_in, c_in, decay):
    log_decay = jnp.log(decay)
    cumulative = jnp.cumsum(log_decay, axis=0)
    length = inputs.shape[0]
    sequence_indices = jnp.arange(length, dtype=jnp.int32)
    causal = sequence_indices[:, None] >= sequence_indices[None, :]
    log_gap = cumulative[:, None, :] - cumulative[None, :, :]
    weights = jnp.exp(jnp.where(causal[:, :, None], log_gap, -1e30))
    driven = inputs * (1.0 - decay)[:, :, None]
    affinity = jnp.dot(c_in, b_in.T, preferred_element_type=jnp.float32)
    within = jnp.einsum("tsh,shp->thp", affinity[:, :, None] * weights, driven, precision=HIGHEST)
    tail_decay = jnp.exp(cumulative[-1][None, :] - cumulative)
    end_state = jnp.einsum(
        "sh,shp,sn->hpn", tail_decay, driven, b_in.astype(jnp.float32), precision=HIGHEST
    )
    return (within, jnp.exp(cumulative), jnp.exp(cumulative[-1]), end_state)


def combine_states(earlier, later):
    return (earlier[0] * later[0], later[0][:, None, None] * earlier[1] + later[1])


def per_device(
    frames,
    segment_ids,
    ln_gain,
    ln_bias,
    qkv_weight,
    out_weight,
    out_bias,
    adapter,
    rms_gain,
    x_weight,
    bc_weight,
    decay,
    skip_gain,
):
    frame_count = frames.shape[0]
    margin = WINDOW
    tm_slot = lax.axis_index("tm")
    adapter_cols = lax.all_to_all(adapter, "head", split_axis=1, concat_axis=0, tiled=True)
    gathered = lax.all_gather(frames, "head", axis=1, tiled=True)
    normed = layer_norm(gathered.astype(jnp.float32), ln_gain, ln_bias).astype(jnp.bfloat16)
    queries = jnp.dot(normed, qkv_weight[0], preferred_element_type=jnp.float32).astype(
        jnp.bfloat16
    )
    keys_own = jnp.dot(normed, qkv_weight[1], preferred_element_type=jnp.float32).astype(
        jnp.bfloat16
    )
    values_own = jnp.dot(normed, qkv_weight[2], preferred_element_type=jnp.float32).astype(
        jnp.bfloat16
    )
    joined = jnp.concatenate([keys_own, values_own], axis=1)
    extended = with_halo(joined, (("tm", 0),), margin)
    head_width = keys_own.shape[1]
    keys_ext = extended[:, :head_width]
    values_ext = extended[:, head_width:]
    ids_pad = jnp.pad(segment_ids, (margin, margin), constant_values=-1)
    local_ids = lax.dynamic_slice_in_dim(
        ids_pad, tm_slot * frame_count, frame_count + 2 * margin, 0
    )
    heads_dev = queries.shape[1] // EHEAD_DIM
    qblock = math.gcd(frame_count, 512)
    span_rows = qblock + 2 * margin

    def attend(block_index):
        begin = block_index * qblock
        query_rows = queries.reshape(qblock, heads_dev, EHEAD_DIM)
        key_rows = keys_ext.reshape(span_rows, heads_dev, EHEAD_DIM)
        value_rows = values_ext.reshape(span_rows, heads_dev, EHEAD_DIM)
        query_ids = lax.dynamic_slice_in_dim(local_ids, begin + margin, qblock, 0)
        scores = jnp.einsum(
            "qhe,khe->hqk", query_rows, key_rows, preferred_element_type=jnp.float32
        ) * EHEAD_DIM ** (-0.5)
        allowed = query_ids[:, None] == local_ids[None, :]
        scores = jnp.where(allowed[None], scores, -1e30)
        peak = jnp.max(scores, axis=-1, keepdims=True)
        raised = jnp.exp(scores - peak)
        probs = (raised / jnp.sum(raised, axis=-1, keepdims=True)).astype(jnp.bfloat16)
        blended = jnp.einsum("hqk,khe->qhe", probs, value_rows, preferred_element_type=jnp.float32)
        return blended.astype(jnp.bfloat16).reshape(qblock, heads_dev * EHEAD_DIM)

    attended = lax.map(attend, jnp.arange(frame_count // qblock, dtype=jnp.int32)).reshape(
        frame_count, heads_dev * EHEAD_DIM
    )
    attention = jnp.dot(
        lax.all_gather(attended, "head", axis=1, tiled=True),
        out_weight,
        preferred_element_type=jnp.float32,
    )
    encoded = (frames.astype(jnp.float32) + attention + out_bias).astype(jnp.bfloat16)
    pooled = jnp.mean(
        encoded.astype(jnp.float32).reshape(frame_count // 4, 4, encoded.shape[1]), axis=1
    ).astype(jnp.bfloat16)
    pooled_all = lax.all_gather(pooled, "head", axis=1, tiled=True)
    column_part = jnp.dot(pooled_all, adapter_cols, preferred_element_type=jnp.float32)
    column_width = column_part.shape[1]
    column_sq = lax.psum(jnp.sum(jnp.square(column_part), axis=1), "head")
    column_gain = lax.dynamic_slice_in_dim(
        rms_gain, lax.axis_index("head") * column_width, column_width, 0
    )
    column_scaled = (
        column_part * lax.rsqrt(column_sq[:, None] / rms_gain.shape[0] + EPSILON) * column_gain
    ).astype(jnp.bfloat16)
    scaled = lax.all_gather(column_scaled, "head", axis=1, tiled=True)
    inputs = jax.nn.silu(jnp.dot(scaled, x_weight, preferred_element_type=jnp.float32)).astype(
        jnp.bfloat16
    )
    coupler_part = jax.nn.silu(
        jnp.dot(scaled, bc_weight, preferred_element_type=jnp.float32)
    ).astype(jnp.bfloat16)
    couplers = lax.all_gather(coupler_part, "head", axis=1, tiled=True)
    token_count = inputs.shape[0]
    state_heads = inputs.shape[1] // HDIM
    inputs_wide = inputs.astype(jnp.float32).reshape(token_count, state_heads, HDIM)
    c_rows = couplers[:, NSTATE:]
    within, growth, total_decay, end_state = block_terms(
        inputs_wide, couplers[:, :NSTATE], c_rows, decay
    )
    identity = (jnp.ones_like(total_decay), jnp.zeros_like(end_state))
    incoming = prefix((total_decay, end_state), "tm", combine_states, identity)
    from_state = jnp.einsum(
        "tn,hpn->thp", c_rows.astype(jnp.float32), incoming[1], precision=HIGHEST
    )
    result_rows = within + growth[:, :, None] * from_state + skip_gain[None, :, None] * inputs_wide
    mixed = result_rows.astype(jnp.bfloat16).reshape(token_count, state_heads * HDIM)
    return (encoded, mixed)


PLANE = 4
MESH = pl.DeviceIdType.MESH
VM = pl.BlockSpec(memory_space=pltpu.VMEM)
HB = pl.BlockSpec(memory_space=pltpu.HBM)
S_DECAY, S_K, S_V, S_ATT, S_CP, S_X, S_BC, S_T, S_S1, S_S2, S_Y, S_PART = 1, 4, 6, 8, 12, 13, 16, 19, 20, 21, 22, 25
PIECES = 5
S_OFF, S_ON = 30, 32
CHUNKS = 2
LIMIT = 63 * 1024 * 1024
F32 = jnp.float32
BF16 = jnp.bfloat16
NT = (((1,), (1,)), ((), ()))
TN = (((0,), (0,)), ((), ()))


def dot(a, b, dims=(((1,), (0,)), ((), ())), precision=None):
    return lax.dot_general(a, b, dims, precision=precision, preferred_element_type=F32)


def iota(shape, dim):
    return lax.broadcasted_iota(jnp.int32, shape, dim)


def fused_kernel(
    nt,
    frames_hbm, ids_hbm, lng_hbm, lnb_hbm, qkv_hbm, out_hbm, ob_hbm, ad_hbm, rms_hbm, x_hbm, bc_hbm, decay_hbm, skip_hbm,
    enc_o, mix_o,
    wqkv, wout, wad, wx, wbc, ids, ln_gain, ln_bias, out_bias, rms_gain, skip, wsem,
    fb, ob, nb, qb, kb, vb, mk, acc, mb, lb, att, pf, ps, pr, sc, cp, xin, xq, xb, bcb, db,
    sm, pm, s1, s2, tp, tn, wgt, dx, skx, yacc, yb, yr, send, recv,
):
    tm = lax.axis_index("tm")
    hy = lax.axis_index("head")
    z = tm // PLANE
    q = tm % PLANE
    planes = nt // PLANE
    rows = frames_hbm.shape[0]
    toks = decay_hbm.shape[1]
    span = PLANE * toks
    width = qb.shape[1]
    pairs = width // 128
    qw = xb.shape[2]
    qheads = qw // HDIM
    heads = decay_hbm.shape[0]

    loads = [
        pltpu.make_async_copy(src, dst, wsem.at[i])
        for i, (src, dst) in enumerate(
            [
                (qkv_hbm.at[1], wqkv.at[1]),
                (qkv_hbm.at[2], wqkv.at[2]),
                (qkv_hbm.at[0], wqkv.at[0]),
                (out_hbm, wout),
                (ad_hbm, wad),
                (bc_hbm, wbc),
                (x_hbm, wx),
                (frames_hbm, fb.at[hy]),
                (decay_hbm, db.at[q]),
                (ids_hbm, ids),
                (lng_hbm, ln_gain),
                (lnb_hbm, ln_bias),
                (ob_hbm, out_bias),
                (rms_hbm, rms_gain),
                (skip_hbm, skip),
            ]
        )
    ]

    def remote(src, dst, sem, device):
        return pltpu.make_async_remote_copy(
            src_ref=src, dst_ref=dst, send_sem=send.at[sem], recv_sem=recv.at[sem],
            device_id=device, device_id_type=MESH,
        )

    partner = {"head": 1 - hy}
    peers = [{"tm": z * PLANE + (q + k) % PLANE} for k in range(1, PLANE)]
    side = tm % 2
    off_at = (tm + nt - 1 + 2 * side) % nt
    on_at = tm + 1 - 2 * side
    off = {"tm": off_at}
    on = {"tm": on_at}
    has_off = jnp.logical_and(tm > 0, tm < nt - 1)
    bar = pltpu.get_barrier_semaphore()

    def greet(device):
        pl.semaphore_signal(bar, inc=1, device_id=device, device_id_type=MESH)

    greet(partner)
    for peer in peers:
        greet(peer)
    for dz in range(1, planes):
        greet({"tm": (tm + dz * PLANE) % nt})
    far = jnp.logical_and(has_off, jnp.logical_or(q == 0, q == PLANE - 1))

    @pl.when(far)
    def _():
        greet(off)

    for load in loads[7:]:
        load.start()
    for load in loads[:3]:
        load.start()
    loads[7].wait()
    loads[8].wait()
    pl.semaphore_wait(bar, PLANE + planes - 1 + far.astype(jnp.int32))

    c_decay = [remote(db.at[q], db.at[q], S_DECAY + k, peer) for k, peer in enumerate(peers)]
    for c in c_decay:
        c.start()
    c_frames = remote(fb.at[hy], fb.at[hy], 0, partner)
    c_frames.start()
    step = rows // CHUNKS

    def off_copy(i):
        part = pl.ds(i * step, step)
        return remote(fb.at[hy, part, :], ob.at[hy, part, :], S_OFF + i, off)

    def on_copy(i):
        part = pl.ds(i * step, step)
        return remote(ob.at[hy, part, :], ob.at[hy, part, :], S_ON + i, partner)

    def hand_on(i):
        @pl.when(has_off)
        def _():
            off_copy(i).wait_recv()
            on_copy(i).start()

    @pl.when(has_off)
    def _():
        for i in range(CHUNKS):
            off_copy(i).start()

    for load in loads[9:]:
        load.wait()

    def id_row(at):
        return ids[pl.ds(pl.multiple_of(at * rows, rows), rows)].reshape(1, rows).astype(F32)

    own = id_row(tm)
    beside = id_row(on_at)
    beyond = jnp.where(has_off, id_row(off_at), -1.0)
    own_col = jnp.transpose(jnp.broadcast_to(own, (128, rows)))[:, :1]
    for i, row in enumerate((own, beside, beyond)):
        mk[:, i * rows : (i + 1) * rows] = jnp.where(own_col == row, 0.0, -1e30)

    def normalize(buf):
        both = jnp.concatenate([buf[0], buf[1]], axis=1).astype(F32)
        center = jnp.mean(both, axis=-1, keepdims=True)
        moved = both - center
        spread = jnp.mean(jnp.square(moved), axis=-1, keepdims=True)
        scale = ln_gain[...].reshape(1, -1)
        nb[...] = (moved * lax.rsqrt(spread + EPSILON) * scale + ln_bias[...].reshape(1, -1)).astype(BF16)

    is_low = iota((1, 128), 1) < EHEAD_DIM

    for c in c_decay:
        c.wait()
    blocks = []
    for j in range(PLANE):
        block = db[j]
        mine = block[:qheads, :]
        for i in range(1, PLANE):
            mine = jnp.where(q == i, block[i * qheads : (i + 1) * qheads, :], mine)
        blocks.append(mine)
    dec_row = jnp.concatenate(blocks, axis=1)
    dec_row = jnp.concatenate([dec_row, jnp.ones((8 - qheads, span), F32)], axis=0)
    logs = jnp.log(jnp.maximum(dec_row, 1e-37))
    l0 = logs.astype(BF16).astype(F32)
    l1 = (logs - l0).astype(BF16).astype(F32)
    l2 = logs - l0 - l1
    upto = jnp.where(iota((span, span), 0) <= iota((span, span), 1), 1.0, 0.0).astype(BF16)
    summed = dot(jnp.concatenate([l0, l1, l2, jnp.zeros((8, span), F32)], axis=0).astype(BF16), upto)
    cum_row = summed[:8] + summed[8:16] + summed[16:24]
    cols = jnp.transpose(jnp.concatenate([cum_row, dec_row, jnp.zeros((112, span), F32)], axis=0))
    cum_col = cols[:, :8]
    rest = 1.0 - cols[:, 8:16]
    grow = jnp.exp(cum_col)
    tail = jnp.exp(cum_col[span - 1 :, :] - cum_col) * rest

    def widen(narrow, dst):
        for h in range(0, qheads, 2):
            first = jnp.broadcast_to(narrow[:, h : h + 1], (narrow.shape[0], 128))
            if h + 1 < qheads:
                second = jnp.broadcast_to(narrow[:, h + 1 : h + 2], (narrow.shape[0], 128))
                dst[:, h * HDIM : (h + 2) * HDIM] = jnp.where(is_low, first, second)
            else:
                dst[:, h * HDIM : (h + 1) * HDIM] = first[:, :HDIM]

    widen(grow, dx.at[0])
    widen(tail, dx.at[1])
    widen(rest, dx.at[2])
    gains = skip[...].reshape(1, -1)
    own_gain = gains[:, :qheads]
    for i in range(1, PLANE):
        own_gain = jnp.where(q == i, gains[:, i * qheads : (i + 1) * qheads], own_gain)
    widen(jnp.broadcast_to(own_gain, (8, qheads)), skx)
    causal = iota((span, span), 0) >= iota((span, span), 1)
    for h in range(qheads):
        gap = cum_col[:, h : h + 1] - cum_row[h : h + 1, :]
        wgt[h] = jnp.exp(jnp.where(causal, gap, -1e30))
    total = dx[0, span - 1 :, :]
    tp[...] = jnp.broadcast_to(total, (8, qw))
    later = {"tm": (tm + PLANE) % nt}
    latest = {"tm": (tm + 2 * PLANE) % nt}
    c_t = remote(tp, tn, S_T, later)
    c_s1 = remote(sm, s1, S_S1, later)
    c_s2 = remote(sm, s2, S_S2, latest)
    c_p = remote(pm, s2, S_S2, latest)

    @pl.when(z < planes - 1)
    def _():
        c_t.start()

    c_frames.wait()
    for load in loads[3:7]:
        load.start()
    normalize(fb)

    def project(which, dst, scale):
        def tile(j, carry):
            cols = pl.ds(pl.multiple_of(j * 256, 256), 256)
            part = dot(nb[...], wqkv[which, :, cols]).astype(BF16)
            dst[:, cols] = part * scale if scale is not None else part
            return carry

        lax.fori_loop(0, width // 256, tile, 0, unroll=True)

    loads[0].wait()
    project(1, kb.at[0], None)
    c_k = remote(kb.at[0], kb.at[1], S_K, on)
    c_k.start()
    hand_on(0)
    loads[1].wait()
    project(2, vb.at[0], None)
    c_v = remote(vb.at[0], vb.at[1], S_V, on)
    c_v.start()
    hand_on(1)
    loads[2].wait()
    project(0, qb, jnp.asarray(EHEAD_DIM ** (-0.5), BF16))

    sides = (jnp.where(is_low, 1.0, 0.0).astype(BF16), jnp.where(is_low, 0.0, 1.0).astype(BF16))

    def within_chip(p, carry):
        cols = pl.ds(pl.multiple_of(p * 128, 128), 128)
        qp = qb[:, cols]
        kp = kb[:2, :, cols].reshape(2 * rows, 128)
        vp = vb[:2, :, cols].reshape(2 * rows, 128)
        got = []
        for side in sides:
            s = dot(qp * side, kp, NT) + mk[:, : 2 * rows]
            m = jnp.max(s, axis=-1, keepdims=True)
            e = jnp.exp(s - m)
            got.append((dot(e.astype(BF16), vp), m, jnp.sum(e, axis=-1, keepdims=True)))
        acc[p] = jnp.where(is_low, got[0][0], got[1][0])
        mb[p] = jnp.where(is_low, got[0][1], got[1][1])
        lb[p] = jnp.where(is_low, got[0][2], got[1][2])
        return carry

    c_k.wait()
    c_v.wait()
    lax.fori_loop(0, pairs, within_chip, 0)

    @pl.when(has_off)
    def _():
        for i in range(CHUNKS):
            on_copy(i).wait()
            off_copy(i).wait_send()
        normalize(ob)
        project(1, kb.at[2], None)
        project(2, vb.at[2], None)

    @pl.when(jnp.logical_not(has_off))
    def _():
        kb[2] = jnp.zeros((rows, width), BF16)
        vb[2] = jnp.zeros((rows, width), BF16)

    def att_copy(p):
        cols = pl.ds(pl.multiple_of(hy * width + p * 128, 128), 128)
        return remote(att.at[:, cols], att.at[:, cols], S_ATT + p, partner)

    def beyond_chip(p, carry):
        cols = pl.ds(pl.multiple_of(p * 128, 128), 128)
        qp = qb[:, cols]
        kp, vp = kb[2, :, cols], vb[2, :, cols]
        old_m, old_l = mb[p], lb[p]
        got = []
        for i, side in enumerate(sides):
            s = dot(qp * side, kp, NT) + mk[:, 2 * rows :]
            m1 = old_m[:, i * EHEAD_DIM : i * EHEAD_DIM + 1]
            m = jnp.maximum(jnp.max(s, axis=-1, keepdims=True), m1)
            e = jnp.exp(s - m)
            got.append((dot(e.astype(BF16), vp), m, jnp.sum(e, axis=-1, keepdims=True)))
        fade = jnp.exp(old_m - jnp.where(is_low, got[0][1], got[1][1]))
        total = old_l * fade + jnp.where(is_low, got[0][2], got[1][2])
        blended = acc[p] * fade + jnp.where(is_low, got[0][0], got[1][0])
        att[:, pl.ds(pl.multiple_of(hy * width + p * 128, 128), 128)] = (blended / total).astype(BF16)
        att_copy(p).start()
        return carry

    lax.fori_loop(0, pairs, beyond_chip, 0)
    for p in range(pairs):
        att_copy(p).wait()

    loads[3].wait()
    encoded = (fb[hy].astype(F32) + dot(att[...], wout[...]) + out_bias[...].reshape(1, -1)).astype(BF16)
    enc_o[...] = encoded
    rr, cc = iota((toks, rows), 0) * 4, iota((toks, rows), 1)
    pool = jnp.where(jnp.logical_and(cc >= rr, cc < rr + 4), 0.25, 0.0).astype(BF16)
    pooled = dot(pool, encoded).astype(BF16)

    loads[4].wait()

    piece = wad.shape[1] // PIECES

    def part_copy(j):
        cols = pl.ds(pl.multiple_of(j * piece, piece), piece)
        return remote(ps.at[:, cols], pr.at[:, cols], S_PART + j, partner)

    def adapt(j, carry):
        cols = pl.ds(pl.multiple_of(j * piece, piece), piece)
        part = dot(pooled, wad[:, cols])
        pf[:, cols] = part
        ps[:, cols] = part.astype(BF16)
        part_copy(j).start()
        return carry

    lax.fori_loop(0, PIECES, adapt, 0)

    for j in range(PIECES):
        part_copy(j).wait()
    proj = pf[...] + pr[...].astype(F32)
    square = jnp.mean(jnp.square(proj), axis=-1, keepdims=True)
    sc[...] = (proj * lax.rsqrt(square + EPSILON) * rms_gain[...].reshape(1, -1)).astype(BF16)

    def silu(v):
        return v / (1.0 + jnp.exp(-v))

    loads[5].wait()
    cp[hy] = silu(dot(sc[...], wbc[...])).astype(BF16)
    c_cp = remote(cp.at[hy], cp.at[hy], S_CP, partner)
    c_cp.start()
    loads[6].wait()

    def drive_in(j, carry):
        cols = pl.ds(pl.multiple_of(j * 256, 256), 256)
        xin[:, cols] = silu(dot(sc[...], wx[:, cols]))
        return carry

    tiles = wx.shape[1] // 256
    lax.fori_loop(0, tiles // 2 + 1, drive_in, 0, unroll=True)
    c_cp.wait()
    c_bc = [remote(cp, bcb.at[:, q], S_BC + k - 1, peers[k - 1]) for k in range(1, PLANE)]
    for c in c_bc:
        c.start()
    bcb[:, q] = cp[...]
    lax.fori_loop(tiles // 2 + 1, tiles, drive_in, 0, unroll=True)
    for j in range(PLANE):
        xq[j] = xin[:, j * qw : (j + 1) * qw].astype(BF16)
    c_x = [remote(xq.at[(q + k) % PLANE], xb.at[q], S_X + k - 1, peers[k - 1]) for k in range(1, PLANE)]
    for c in c_x:
        c.start()
    xb[q] = xq[q]
    for c in c_x:
        c.wait()
    for c in c_bc:
        c.wait()

    x_all = xb[...].reshape(span, qw).astype(F32)
    b_all = bcb[0].reshape(span, NSTATE)
    c_all = bcb[1].reshape(span, NSTATE)
    state = dot(b_all, (x_all * dx[1]).astype(BF16), TN)
    sm[...] = state.astype(BF16)

    @pl.when(z < planes - 1)
    def _():
        c_s1.start()

    @pl.when(z == 0)
    def _():
        c_s2.start()

    affinity = dot(c_all, b_all, NT)
    driven = (x_all * dx[2]).astype(BF16)

    def head_out(h, cols):
        return dot((affinity * wgt[h]).astype(BF16), cols)

    for h in range(0, qheads, 2):
        if h + 1 < qheads:
            cols = driven[:, h * HDIM : (h + 2) * HDIM]
            yacc[:, h * HDIM : (h + 2) * HDIM] = jnp.where(is_low, head_out(h, cols), head_out(h + 1, cols))
        else:
            yacc[:, h * HDIM : (h + 1) * HDIM] = head_out(h, driven[:, h * HDIM : (h + 1) * HDIM])
    yacc[...] = yacc[...] + skx[:1, :] * x_all

    @pl.when(z > 0)
    def _():
        c_t.wait_recv()
        c_s1.wait_recv()

    @pl.when(z == 1)
    def _():
        pm[...] = (sm[...].astype(F32) + tp[:1, :] * s1[...].astype(F32)).astype(BF16)
        c_p.start()

    @pl.when(z > 1)
    def _():
        c_s2.wait_recv()
        s1[...] = (s1[...].astype(F32) + tn[:1, :] * s2[...].astype(F32)).astype(BF16)

    @pl.when(z == 0)
    def _():
        s1[...] = jnp.zeros(s1.shape, BF16)

    y = yacc[...] + dx[0] * dot(c_all, s1[...])
    yb[...] = y.astype(BF16).reshape(PLANE, toks, qw)
    c_y = [remote(yb.at[(q + k) % PLANE], yr.at[q], S_Y + k - 1, peers[k - 1]) for k in range(1, PLANE)]
    for c in c_y:
        c.start()
    yr[q] = yb[q]
    @pl.when(z < planes - 1)
    def _():
        c_t.wait_send()
        c_s1.wait_send()

    @pl.when(z < planes - 2)
    def _():
        c_s2.wait_send()

    for c in c_y:
        c.wait()
    for j in range(PLANE):
        mix_o[:, j * qw : (j + 1) * qw] = yr[j]


def place_kernel(a, b, a_out, b_out):
    a_out[...] = a[...]
    b_out[...] = b[...]


def fused(nt):
    def per_device(frames, segment_ids, ln_gain, ln_bias, qkv_weight, out_weight, out_bias, adapter, rms_gain,
                   x_weight, bc_weight, decay, skip_gain):
        rows, half = frames.shape
        width = qkv_weight.shape[2]
        toks, heads = decay.shape
        dm = adapter.shape[1]
        xw = x_weight.shape[1]
        qw = xw // PLANE
        planes = nt // PLANE
        span = PLANE * toks
        pairs = width // 128
        sems = S_ON + CHUNKS
        v = pltpu.VMEM
        encoded, mixed = pl.pallas_call(
            functools.partial(fused_kernel, nt),
            out_shape=(
                jax.ShapeDtypeStruct((rows, half), BF16),
                jax.ShapeDtypeStruct((toks, xw), BF16),
            ),
            in_specs=[HB] * 13,
            out_specs=(VM, VM),
            scratch_shapes=[
                v(qkv_weight.shape, BF16),
                v(out_weight.shape, BF16),
                v(adapter.shape, BF16),
                v(x_weight.shape, BF16),
                v(bc_weight.shape, BF16),
                v(segment_ids.shape, jnp.int32),
                v(ln_gain.shape, F32),
                v(ln_bias.shape, F32),
                v(out_bias.shape, F32),
                v(rms_gain.shape, F32),
                v(skip_gain.shape, F32),
                pltpu.SemaphoreType.DMA((15,)),
                v((2, rows, half), BF16),
                v((2, rows, half), BF16),
                v((rows, 2 * half), BF16),
                v((rows, width), BF16),
                v((3, rows, width), BF16),
                v((3, rows, width), BF16),
                v((rows, 3 * rows), F32),
                v((pairs, rows, 128), F32),
                v((pairs, rows, 128), F32),
                v((pairs, rows, 128), F32),
                v((rows, 2 * width), BF16),
                v((toks, dm), F32),
                v((toks, dm), BF16),
                v((toks, dm), BF16),
                v((toks, dm), BF16),
                v((2, toks, NSTATE), BF16),
                v((toks, xw), F32),
                v((PLANE, toks, qw), BF16),
                v((PLANE, toks, qw), BF16),
                v((2, PLANE, toks, NSTATE), BF16),
                v((PLANE, heads, toks), F32),
                v((NSTATE, qw), BF16),
                v((NSTATE, qw), BF16),
                v((NSTATE, qw), BF16),
                v((NSTATE, qw), BF16),
                v((8, qw), F32),
                v((8, qw), F32),
                v((qw // HDIM, span, span), F32),
                v((3, span, qw), F32),
                v((8, qw), F32),
                v((span, qw), F32),
                v((PLANE, toks, qw), BF16),
                v((PLANE, toks, qw), BF16),
                pltpu.SemaphoreType.DMA((sems,)),
                pltpu.SemaphoreType.DMA((sems,)),
            ],
            compiler_params=pltpu.CompilerParams(
                collective_id=0, has_side_effects=True, vmem_limit_bytes=LIMIT
            ),
        )(
            frames, segment_ids, ln_gain, ln_bias, qkv_weight, out_weight, out_bias, adapter, rms_gain, x_weight,
            bc_weight, jnp.transpose(decay), skip_gain,
        )
        return pl.pallas_call(
            place_kernel,
            out_shape=(jax.ShapeDtypeStruct(encoded.shape, BF16), jax.ShapeDtypeStruct(mixed.shape, BF16)),
            in_specs=[VM, VM],
            out_specs=(VM, VM),
        )(encoded, mixed)

    return per_device


def solution(mesh):
    placed = (
        P("tm", "head"),
        P(),
        P(),
        P(),
        P(None, None, "head"),
        P(None, "head"),
        P("head"),
        P("head", None),
        P(),
        P(None, "head"),
        P(None, "head"),
        P("tm", "head"),
        P("head"),
    )
    nt = mesh.shape["tm"]
    body = fused(nt) if mesh.shape["head"] == 2 and nt == 4 * PLANE else per_device
    return jax.shard_map(
        body,
        mesh=mesh,
        in_specs=placed,
        out_specs=(P("tm", "head"), P("tm", "head")),
        check_vma=False,
    )
```

```python
import functools
import math

import jax
import jax.numpy as jnp
from jax import lax
from jax.experimental import pallas as pl
from jax.experimental.pallas import tpu as pltpu
from jax.sharding import PartitionSpec as P

EHEAD_DIM = 64
HDIM = 64
NSTATE = 128
WINDOW = 256


EPSILON = 1e-05
HIGHEST = lax.Precision.HIGHEST


def with_halo(block, sides, width):
    for axis, dim in sides:
        count = lax.axis_size(axis)
        forward = [(i, i + 1) for i in range(count - 1)]
        backward = [(target, source) for source, target in forward]
        low = lax.ppermute(
            lax.slice_in_dim(block, block.shape[dim] - width, None, axis=dim), axis, forward
        )
        high = lax.ppermute(lax.slice_in_dim(block, 0, width, axis=dim), axis, backward)
        block = jnp.concatenate([low, block, high], axis=dim)
    return block


def prefix(part, axis, combine, identity):
    place = lax.axis_index(axis)
    gathered = jax.tree.map(lambda a: lax.all_gather(a, axis), part)
    state = jax.tree.map(lambda a, e: jnp.zeros_like(a) + jnp.asarray(e, a.dtype), part, identity)

    def one(hop, state):
        return combine(
            state, jax.tree.map(lambda a: lax.dynamic_index_in_dim(a, hop, 0, False), gathered)
        )

    return lax.fori_loop(0, place, one, state)


def layer_norm(values, gain, offset):
    center_mean = jnp.mean(values, axis=-1, keepdims=True)
    spread = jnp.mean(jnp.square(values - center_mean), axis=-1, keepdims=True)
    return (values - center_mean) * lax.rsqrt(spread + EPSILON) * gain + offset


def block_terms(inputs, b_in, c_in, decay):
    log_decay = jnp.log(decay)
    cumulative = jnp.cumsum(log_decay, axis=0)
    length = inputs.shape[0]
    sequence_indices = jnp.arange(length, dtype=jnp.int32)
    causal = sequence_indices[:, None] >= sequence_indices[None, :]
    log_gap = cumulative[:, None, :] - cumulative[None, :, :]
    weights = jnp.exp(jnp.where(causal[:, :, None], log_gap, -1e30))
    driven = inputs * (1.0 - decay)[:, :, None]
    affinity = jnp.dot(c_in, b_in.T, preferred_element_type=jnp.float32)
    within = jnp.einsum("tsh,shp->thp", affinity[:, :, None] * weights, driven, precision=HIGHEST)
    tail_decay = jnp.exp(cumulative[-1][None, :] - cumulative)
    end_state = jnp.einsum(
        "sh,shp,sn->hpn", tail_decay, driven, b_in.astype(jnp.float32), precision=HIGHEST
    )
    return (within, jnp.exp(cumulative), jnp.exp(cumulative[-1]), end_state)


def combine_states(earlier, later):
    return (earlier[0] * later[0], later[0][:, None, None] * earlier[1] + later[1])


def per_device(
    frames,
    segment_ids,
    ln_gain,
    ln_bias,
    qkv_weight,
    out_weight,
    out_bias,
    adapter,
    rms_gain,
    x_weight,
    bc_weight,
    decay,
    skip_gain,
):
    frame_count = frames.shape[0]
    margin = WINDOW
    tm_slot = lax.axis_index("tm")
    adapter_cols = lax.all_to_all(adapter, "head", split_axis=1, concat_axis=0, tiled=True)
    gathered = lax.all_gather(frames, "head", axis=1, tiled=True)
    normed = layer_norm(gathered.astype(jnp.float32), ln_gain, ln_bias).astype(jnp.bfloat16)
    queries = jnp.dot(normed, qkv_weight[0], preferred_element_type=jnp.float32).astype(
        jnp.bfloat16
    )
    keys_own = jnp.dot(normed, qkv_weight[1], preferred_element_type=jnp.float32).astype(
        jnp.bfloat16
    )
    values_own = jnp.dot(normed, qkv_weight[2], preferred_element_type=jnp.float32).astype(
        jnp.bfloat16
    )
    joined = jnp.concatenate([keys_own, values_own], axis=1)
    extended = with_halo(joined, (("tm", 0),), margin)
    head_width = keys_own.shape[1]
    keys_ext = extended[:, :head_width]
    values_ext = extended[:, head_width:]
    ids_pad = jnp.pad(segment_ids, (margin, margin), constant_values=-1)
    local_ids = lax.dynamic_slice_in_dim(
        ids_pad, tm_slot * frame_count, frame_count + 2 * margin, 0
    )
    heads_dev = queries.shape[1] // EHEAD_DIM
    qblock = math.gcd(frame_count, 512)
    span_rows = qblock + 2 * margin

    def attend(block_index):
        begin = block_index * qblock
        query_rows = queries.reshape(qblock, heads_dev, EHEAD_DIM)
        key_rows = keys_ext.reshape(span_rows, heads_dev, EHEAD_DIM)
        value_rows = values_ext.reshape(span_rows, heads_dev, EHEAD_DIM)
        query_ids = lax.dynamic_slice_in_dim(local_ids, begin + margin, qblock, 0)
        scores = jnp.einsum(
            "qhe,khe->hqk", query_rows, key_rows, preferred_element_type=jnp.float32
        ) * EHEAD_DIM ** (-0.5)
        allowed = query_ids[:, None] == local_ids[None, :]
        scores = jnp.where(allowed[None], scores, -1e30)
        peak = jnp.max(scores, axis=-1, keepdims=True)
        raised = jnp.exp(scores - peak)
        probs = (raised / jnp.sum(raised, axis=-1, keepdims=True)).astype(jnp.bfloat16)
        blended = jnp.einsum("hqk,khe->qhe", probs, value_rows, preferred_element_type=jnp.float32)
        return blended.astype(jnp.bfloat16).reshape(qblock, heads_dev * EHEAD_DIM)

    attended = lax.map(attend, jnp.arange(frame_count // qblock, dtype=jnp.int32)).reshape(
        frame_count, heads_dev * EHEAD_DIM
    )
    attention = jnp.dot(
        lax.all_gather(attended, "head", axis=1, tiled=True),
        out_weight,
        preferred_element_type=jnp.float32,
    )
    encoded = (frames.astype(jnp.float32) + attention + out_bias).astype(jnp.bfloat16)
    pooled = jnp.mean(
        encoded.astype(jnp.float32).reshape(frame_count // 4, 4, encoded.shape[1]), axis=1
    ).astype(jnp.bfloat16)
    pooled_all = lax.all_gather(pooled, "head", axis=1, tiled=True)
    column_part = jnp.dot(pooled_all, adapter_cols, preferred_element_type=jnp.float32)
    column_width = column_part.shape[1]
    column_sq = lax.psum(jnp.sum(jnp.square(column_part), axis=1), "head")
    column_gain = lax.dynamic_slice_in_dim(
        rms_gain, lax.axis_index("head") * column_width, column_width, 0
    )
    column_scaled = (
        column_part * lax.rsqrt(column_sq[:, None] / rms_gain.shape[0] + EPSILON) * column_gain
    ).astype(jnp.bfloat16)
    scaled = lax.all_gather(column_scaled, "head", axis=1, tiled=True)
    inputs = jax.nn.silu(jnp.dot(scaled, x_weight, preferred_element_type=jnp.float32)).astype(
        jnp.bfloat16
    )
    coupler_part = jax.nn.silu(
        jnp.dot(scaled, bc_weight, preferred_element_type=jnp.float32)
    ).astype(jnp.bfloat16)
    couplers = lax.all_gather(coupler_part, "head", axis=1, tiled=True)
    token_count = inputs.shape[0]
    state_heads = inputs.shape[1] // HDIM
    inputs_wide = inputs.astype(jnp.float32).reshape(token_count, state_heads, HDIM)
    c_rows = couplers[:, NSTATE:]
    within, growth, total_decay, end_state = block_terms(
        inputs_wide, couplers[:, :NSTATE], c_rows, decay
    )
    identity = (jnp.ones_like(total_decay), jnp.zeros_like(end_state))
    incoming = prefix((total_decay, end_state), "tm", combine_states, identity)
    from_state = jnp.einsum(
        "tn,hpn->thp", c_rows.astype(jnp.float32), incoming[1], precision=HIGHEST
    )
    result_rows = within + growth[:, :, None] * from_state + skip_gain[None, :, None] * inputs_wide
    mixed = result_rows.astype(jnp.bfloat16).reshape(token_count, state_heads * HDIM)
    return (encoded, mixed)


PLANE = 4
MESH = pl.DeviceIdType.MESH
VM = pl.BlockSpec(memory_space=pltpu.VMEM)
HB = pl.BlockSpec(memory_space=pltpu.HBM)
S_DECAY, S_K, S_V, S_ATT, S_CP, S_X, S_BC, S_T, S_S1, S_S2, S_Y, S_PART = 1, 4, 6, 8, 12, 13, 16, 19, 20, 21, 22, 25
PIECES = 5
S_OFF, S_ON = 30, 32
CHUNKS = 2
LIMIT = 63 * 1024 * 1024
F32 = jnp.float32
BF16 = jnp.bfloat16
NT = (((1,), (1,)), ((), ()))
TN = (((0,), (0,)), ((), ()))


def dot(a, b, dims=(((1,), (0,)), ((), ())), precision=None):
    return lax.dot_general(a, b, dims, precision=precision, preferred_element_type=F32)


def iota(shape, dim):
    return lax.broadcasted_iota(jnp.int32, shape, dim)


def fused_kernel(
    nt,
    frames_hbm, ids_hbm, lng_hbm, lnb_hbm, qkv_hbm, out_hbm, ob_hbm, ad_hbm, rms_hbm, x_hbm, bc_hbm, decay_hbm, skip_hbm,
    enc_o, mix_o,
    wqkv, wout, wad, wx, wbc, ids, ln_gain, ln_bias, out_bias, rms_gain, skip, wsem,
    fb, ob, nb, qb, kb, vb, mk, acc, mb, lb, att, pf, ps, pr, sc, cp, xin, xq, xb, bcb, db,
    sm, pm, s1, s2, tp, tn, wgt, dx, skx, yacc, yb, yr, send, recv,
):
    tm = lax.axis_index("tm")
    hy = lax.axis_index("head")
    z = tm // PLANE
    q = tm % PLANE
    planes = nt // PLANE
    rows = frames_hbm.shape[0]
    toks = decay_hbm.shape[1]
    span = PLANE * toks
    width = qb.shape[1]
    pairs = width // 128
    qw = xb.shape[2]
    qheads = qw // HDIM
    heads = decay_hbm.shape[0]

    loads = [
        pltpu.make_async_copy(src, dst, wsem.at[i])
        for i, (src, dst) in enumerate(
            [
                (qkv_hbm.at[1], wqkv.at[1]),
                (qkv_hbm.at[2], wqkv.at[2]),
                (qkv_hbm.at[0], wqkv.at[0]),
                (out_hbm, wout),
                (ad_hbm, wad),
                (bc_hbm, wbc),
                (x_hbm, wx),
                (frames_hbm, fb.at[hy]),
                (decay_hbm, db.at[q]),
                (ids_hbm, ids),
                (lng_hbm, ln_gain),
                (lnb_hbm, ln_bias),
                (ob_hbm, out_bias),
                (rms_hbm, rms_gain),
                (skip_hbm, skip),
            ]
        )
    ]

    def remote(src, dst, sem, device):
        return pltpu.make_async_remote_copy(
            src_ref=src, dst_ref=dst, send_sem=send.at[sem], recv_sem=recv.at[sem],
            device_id=device, device_id_type=MESH,
        )

    partner = {"head": 1 - hy}
    peers = [{"tm": z * PLANE + (q + k) % PLANE} for k in range(1, PLANE)]
    side = tm % 2
    off_at = (tm + nt - 1 + 2 * side) % nt
    on_at = tm + 1 - 2 * side
    off = {"tm": off_at}
    on = {"tm": on_at}
    has_off = jnp.logical_and(tm > 0, tm < nt - 1)
    bar = pltpu.get_barrier_semaphore()

    def greet(device):
        pl.semaphore_signal(bar, inc=1, device_id=device, device_id_type=MESH)

    greet(partner)
    for peer in peers:
        greet(peer)
    for dz in range(1, planes):
        greet({"tm": (tm + dz * PLANE) % nt})
    far = jnp.logical_and(has_off, jnp.logical_or(q == 0, q == PLANE - 1))

    @pl.when(far)
    def _():
        greet(off)

    for load in loads[7:]:
        load.start()
    for load in loads[:3]:
        load.start()
    loads[7].wait()
    loads[8].wait()
    pl.semaphore_wait(bar, PLANE + planes - 1 + far.astype(jnp.int32))

    c_decay = [remote(db.at[q], db.at[q], S_DECAY + k, peer) for k, peer in enumerate(peers)]
    for c in c_decay:
        c.start()
    c_frames = remote(fb.at[hy], fb.at[hy], 0, partner)
    c_frames.start()
    step = rows // CHUNKS

    def off_copy(i):
        part = pl.ds(i * step, step)
        return remote(fb.at[hy, part, :], ob.at[hy, part, :], S_OFF + i, off)

    def on_copy(i):
        part = pl.ds(i * step, step)
        return remote(ob.at[hy, part, :], ob.at[hy, part, :], S_ON + i, partner)

    def hand_on(i):
        @pl.when(has_off)
        def _():
            off_copy(i).wait_recv()
            on_copy(i).start()

    @pl.when(has_off)
    def _():
        for i in range(CHUNKS):
            off_copy(i).start()

    for load in loads[9:]:
        load.wait()

    def id_row(at):
        return ids[pl.ds(pl.multiple_of(at * rows, rows), rows)].reshape(1, rows).astype(F32)

    own = id_row(tm)
    beside = id_row(on_at)
    beyond = jnp.where(has_off, id_row(off_at), -1.0)
    own_col = jnp.transpose(jnp.broadcast_to(own, (128, rows)))[:, :1]
    for i, row in enumerate((own, beside, beyond)):
        mk[:, i * rows : (i + 1) * rows] = jnp.where(own_col == row, 0.0, -1e30)

    def normalize(buf):
        both = jnp.concatenate([buf[0], buf[1]], axis=1).astype(F32)
        center = jnp.mean(both, axis=-1, keepdims=True)
        moved = both - center
        spread = jnp.mean(jnp.square(moved), axis=-1, keepdims=True)
        scale = ln_gain[...].reshape(1, -1)
        nb[...] = (moved * lax.rsqrt(spread + EPSILON) * scale + ln_bias[...].reshape(1, -1)).astype(BF16)

    is_low = iota((1, 128), 1) < EHEAD_DIM

    for c in c_decay:
        c.wait()
    blocks = []
    for j in range(PLANE):
        block = db[j]
        mine = block[:qheads, :]
        for i in range(1, PLANE):
            mine = jnp.where(q == i, block[i * qheads : (i + 1) * qheads, :], mine)
        blocks.append(mine)
    dec_row = jnp.concatenate(blocks, axis=1)
    dec_row = jnp.concatenate([dec_row, jnp.ones((8 - qheads, span), F32)], axis=0)
    logs = jnp.log(jnp.maximum(dec_row, 1e-37))
    l0 = logs.astype(BF16).astype(F32)
    l1 = (logs - l0).astype(BF16).astype(F32)
    l2 = logs - l0 - l1
    upto = jnp.where(iota((span, span), 0) <= iota((span, span), 1), 1.0, 0.0).astype(BF16)
    summed = dot(jnp.concatenate([l0, l1, l2, jnp.zeros((8, span), F32)], axis=0).astype(BF16), upto)
    cum_row = summed[:8] + summed[8:16] + summed[16:24]
    cols = jnp.transpose(jnp.concatenate([cum_row, dec_row, jnp.zeros((112, span), F32)], axis=0))
    cum_col = cols[:, :8]
    rest = 1.0 - cols[:, 8:16]
    grow = jnp.exp(cum_col)
    tail = jnp.exp(cum_col[span - 1 :, :] - cum_col) * rest

    def widen(narrow, dst):
        for h in range(0, qheads, 2):
            first = jnp.broadcast_to(narrow[:, h : h + 1], (narrow.shape[0], 128))
            if h + 1 < qheads:
                second = jnp.broadcast_to(narrow[:, h + 1 : h + 2], (narrow.shape[0], 128))
                dst[:, h * HDIM : (h + 2) * HDIM] = jnp.where(is_low, first, second)
            else:
                dst[:, h * HDIM : (h + 1) * HDIM] = first[:, :HDIM]

    widen(grow, dx.at[0])
    widen(tail, dx.at[1])
    widen(rest, dx.at[2])
    gains = skip[...].reshape(1, -1)
    own_gain = gains[:, :qheads]
    for i in range(1, PLANE):
        own_gain = jnp.where(q == i, gains[:, i * qheads : (i + 1) * qheads], own_gain)
    widen(jnp.broadcast_to(own_gain, (8, qheads)), skx)
    causal = iota((span, span), 0) >= iota((span, span), 1)
    for h in range(qheads):
        gap = cum_col[:, h : h + 1] - cum_row[h : h + 1, :]
        wgt[h] = jnp.exp(jnp.where(causal, gap, -1e30))
    total = dx[0, span - 1 :, :]
    tp[...] = jnp.broadcast_to(total, (8, qw))
    later = {"tm": (tm + PLANE) % nt}
    latest = {"tm": (tm + 2 * PLANE) % nt}
    c_t = remote(tp, tn, S_T, later)
    c_s1 = remote(sm, s1, S_S1, later)
    c_s2 = remote(sm, s2, S_S2, latest)
    c_p = remote(pm, s2, S_S2, latest)

    @pl.when(z < planes - 1)
    def _():
        c_t.start()

    c_frames.wait()
    for load in loads[3:7]:
        load.start()
    normalize(fb)

    def project(which, dst, scale):
        def tile(j, carry):
            cols = pl.ds(pl.multiple_of(j * 256, 256), 256)
            part = dot(nb[...], wqkv[which, :, cols]).astype(BF16)
            dst[:, cols] = part * scale if scale is not None else part
            return carry

        lax.fori_loop(0, width // 256, tile, 0, unroll=True)

    loads[0].wait()
    project(1, kb.at[0], None)
    c_k = remote(kb.at[0], kb.at[1], S_K, on)
    c_k.start()
    hand_on(0)
    loads[1].wait()
    project(2, vb.at[0], None)
    c_v = remote(vb.at[0], vb.at[1], S_V, on)
    c_v.start()
    hand_on(1)
    loads[2].wait()
    project(0, qb, jnp.asarray(EHEAD_DIM ** (-0.5), BF16))

    sides = (jnp.where(is_low, 1.0, 0.0).astype(BF16), jnp.where(is_low, 0.0, 1.0).astype(BF16))

    def row_sums(got):
        crossed = jnp.where(is_low, got[1][0], got[0][0])
        return jnp.concatenate([crossed[:, EHEAD_DIM:], crossed[:, :EHEAD_DIM]], axis=1)

    def within_chip(p, carry):
        cols = pl.ds(pl.multiple_of(p * 128, 128), 128)
        qp = qb[:, cols]
        kp = kb[:2, :, cols].reshape(2 * rows, 128)
        vp = vb[:2, :, cols].reshape(2 * rows, 128)
        got = []
        for side in sides:
            s = dot(qp * side, kp, NT) + mk[:, : 2 * rows]
            m = jnp.max(s, axis=-1, keepdims=True)
            e = jnp.exp(s - m)
            got.append((dot(e.astype(BF16), vp * side + (1 - side)), m))
        acc[p] = jnp.where(is_low, got[0][0], got[1][0])
        mb[p] = jnp.where(is_low, got[0][1], got[1][1])
        lb[p] = row_sums(got)
        return carry

    c_k.wait()
    c_v.wait()
    lax.fori_loop(0, pairs, within_chip, 0, unroll=2)

    @pl.when(has_off)
    def _():
        for i in range(CHUNKS):
            on_copy(i).wait()
            off_copy(i).wait_send()
        normalize(ob)
        project(1, kb.at[2], None)
        project(2, vb.at[2], None)

    @pl.when(jnp.logical_not(has_off))
    def _():
        kb[2] = jnp.zeros((rows, width), BF16)
        vb[2] = jnp.zeros((rows, width), BF16)

    def att_copy(p):
        cols = pl.ds(pl.multiple_of(hy * width + p * 128, 128), 128)
        return remote(att.at[:, cols], att.at[:, cols], S_ATT + p, partner)

    def beyond_chip(p, carry):
        cols = pl.ds(pl.multiple_of(p * 128, 128), 128)
        qp = qb[:, cols]
        kp, vp = kb[2, :, cols], vb[2, :, cols]
        old_m, old_l = mb[p], lb[p]
        got = []
        for i, side in enumerate(sides):
            s = dot(qp * side, kp, NT) + mk[:, 2 * rows :]
            m1 = old_m[:, i * EHEAD_DIM : i * EHEAD_DIM + 1]
            m = jnp.maximum(jnp.max(s, axis=-1, keepdims=True), m1)
            e = jnp.exp(s - m)
            got.append((dot(e.astype(BF16), vp * side + (1 - side)), m))
        fade = jnp.exp(old_m - jnp.where(is_low, got[0][1], got[1][1]))
        total = old_l * fade + row_sums(got)
        blended = acc[p] * fade + jnp.where(is_low, got[0][0], got[1][0])
        att[:, pl.ds(pl.multiple_of(hy * width + p * 128, 128), 128)] = (blended / total).astype(BF16)
        att_copy(p).start()
        return carry

    lax.fori_loop(0, pairs, beyond_chip, 0, unroll=2)
    for p in range(pairs):
        att_copy(p).wait()

    loads[3].wait()
    encoded = (fb[hy].astype(F32) + dot(att[...], wout[...]) + out_bias[...].reshape(1, -1)).astype(BF16)
    enc_o[...] = encoded
    rr, cc = iota((toks, rows), 0) * 4, iota((toks, rows), 1)
    pool = jnp.where(jnp.logical_and(cc >= rr, cc < rr + 4), 0.25, 0.0).astype(BF16)
    pooled = dot(pool, encoded).astype(BF16)

    loads[4].wait()

    piece = wad.shape[1] // PIECES

    def part_copy(j):
        cols = pl.ds(pl.multiple_of(j * piece, piece), piece)
        return remote(ps.at[:, cols], pr.at[:, cols], S_PART + j, partner)

    def adapt(j, carry):
        cols = pl.ds(pl.multiple_of(j * piece, piece), piece)
        part = dot(pooled, wad[:, cols])
        pf[:, cols] = part
        ps[:, cols] = part.astype(BF16)
        part_copy(j).start()
        return carry

    lax.fori_loop(0, PIECES, adapt, 0)

    for j in range(PIECES):
        part_copy(j).wait()
    proj = pf[...] + pr[...].astype(F32)
    square = jnp.mean(jnp.square(proj), axis=-1, keepdims=True)
    sc[...] = (proj * lax.rsqrt(square + EPSILON) * rms_gain[...].reshape(1, -1)).astype(BF16)

    def silu(v):
        return v / (1.0 + jnp.exp(-v))

    loads[5].wait()
    cp[hy] = silu(dot(sc[...], wbc[...])).astype(BF16)
    c_cp = remote(cp.at[hy], cp.at[hy], S_CP, partner)
    c_cp.start()
    loads[6].wait()

    def drive_in(j, carry):
        cols = pl.ds(pl.multiple_of(j * 256, 256), 256)
        xin[:, cols] = silu(dot(sc[...], wx[:, cols]))
        return carry

    tiles = wx.shape[1] // 256
    lax.fori_loop(0, tiles // 2 + 1, drive_in, 0, unroll=True)
    c_cp.wait()
    c_bc = [remote(cp, bcb.at[:, q], S_BC + k - 1, peers[k - 1]) for k in range(1, PLANE)]
    for c in c_bc:
        c.start()
    bcb[:, q] = cp[...]
    lax.fori_loop(tiles // 2 + 1, tiles, drive_in, 0, unroll=True)
    for j in range(PLANE):
        xq[j] = xin[:, j * qw : (j + 1) * qw].astype(BF16)
    c_x = [remote(xq.at[(q + k) % PLANE], xb.at[q], S_X + k - 1, peers[k - 1]) for k in range(1, PLANE)]
    for c in c_x:
        c.start()
    xb[q] = xq[q]
    for c in c_x:
        c.wait()
    for c in c_bc:
        c.wait()

    x_all = xb[...].reshape(span, qw).astype(F32)
    b_all = bcb[0].reshape(span, NSTATE)
    c_all = bcb[1].reshape(span, NSTATE)
    state = dot(b_all, (x_all * dx[1]).astype(BF16), TN)
    sm[...] = state.astype(BF16)

    @pl.when(z < planes - 1)
    def _():
        c_s1.start()

    @pl.when(z == 0)
    def _():
        c_s2.start()

    affinity = dot(c_all, b_all, NT)
    driven = (x_all * dx[2]).astype(BF16)

    def head_out(h, cols):
        return dot((affinity * wgt[h]).astype(BF16), cols)

    for h in range(0, qheads, 2):
        if h + 1 < qheads:
            cols = driven[:, h * HDIM : (h + 2) * HDIM]
            yacc[:, h * HDIM : (h + 2) * HDIM] = jnp.where(is_low, head_out(h, cols), head_out(h + 1, cols))
        else:
            yacc[:, h * HDIM : (h + 1) * HDIM] = head_out(h, driven[:, h * HDIM : (h + 1) * HDIM])
    yacc[...] = yacc[...] + skx[:1, :] * x_all

    @pl.when(z > 0)
    def _():
        c_t.wait_recv()
        c_s1.wait_recv()

    @pl.when(z == 1)
    def _():
        pm[...] = (sm[...].astype(F32) + tp[:1, :] * s1[...].astype(F32)).astype(BF16)
        c_p.start()

    @pl.when(z > 1)
    def _():
        c_s2.wait_recv()
        s1[...] = (s1[...].astype(F32) + tn[:1, :] * s2[...].astype(F32)).astype(BF16)

    @pl.when(z == 0)
    def _():
        s1[...] = jnp.zeros(s1.shape, BF16)

    y = yacc[...] + dx[0] * dot(c_all, s1[...])
    yb[...] = y.astype(BF16).reshape(PLANE, toks, qw)
    c_y = [remote(yb.at[(q + k) % PLANE], yr.at[q], S_Y + k - 1, peers[k - 1]) for k in range(1, PLANE)]
    for c in c_y:
        c.start()
    yr[q] = yb[q]
    @pl.when(z < planes - 1)
    def _():
        c_t.wait_send()
        c_s1.wait_send()

    @pl.when(z < planes - 2)
    def _():
        c_s2.wait_send()

    for c in c_y:
        c.wait()
    for j in range(PLANE):
        mix_o[:, j * qw : (j + 1) * qw] = yr[j]


def place_kernel(a, b, a_out, b_out):
    a_out[...] = a[...]
    b_out[...] = b[...]


def fused(nt):
    def per_device(frames, segment_ids, ln_gain, ln_bias, qkv_weight, out_weight, out_bias, adapter, rms_gain,
                   x_weight, bc_weight, decay, skip_gain):
        rows, half = frames.shape
        width = qkv_weight.shape[2]
        toks, heads = decay.shape
        dm = adapter.shape[1]
        xw = x_weight.shape[1]
        qw = xw // PLANE
        planes = nt // PLANE
        span = PLANE * toks
        pairs = width // 128
        sems = S_ON + CHUNKS
        v = pltpu.VMEM
        encoded, mixed = pl.pallas_call(
            functools.partial(fused_kernel, nt),
            out_shape=(
                jax.ShapeDtypeStruct((rows, half), BF16),
                jax.ShapeDtypeStruct((toks, xw), BF16),
            ),
            in_specs=[HB] * 13,
            out_specs=(VM, VM),
            scratch_shapes=[
                v(qkv_weight.shape, BF16),
                v(out_weight.shape, BF16),
                v(adapter.shape, BF16),
                v(x_weight.shape, BF16),
                v(bc_weight.shape, BF16),
                v(segment_ids.shape, jnp.int32),
                v(ln_gain.shape, F32),
                v(ln_bias.shape, F32),
                v(out_bias.shape, F32),
                v(rms_gain.shape, F32),
                v(skip_gain.shape, F32),
                pltpu.SemaphoreType.DMA((15,)),
                v((2, rows, half), BF16),
                v((2, rows, half), BF16),
                v((rows, 2 * half), BF16),
                v((rows, width), BF16),
                v((3, rows, width), BF16),
                v((3, rows, width), BF16),
                v((rows, 3 * rows), F32),
                v((pairs, rows, 128), F32),
                v((pairs, rows, 128), F32),
                v((pairs, rows, 128), F32),
                v((rows, 2 * width), BF16),
                v((toks, dm), F32),
                v((toks, dm), BF16),
                v((toks, dm), BF16),
                v((toks, dm), BF16),
                v((2, toks, NSTATE), BF16),
                v((toks, xw), F32),
                v((PLANE, toks, qw), BF16),
                v((PLANE, toks, qw), BF16),
                v((2, PLANE, toks, NSTATE), BF16),
                v((PLANE, heads, toks), F32),
                v((NSTATE, qw), BF16),
                v((NSTATE, qw), BF16),
                v((NSTATE, qw), BF16),
                v((NSTATE, qw), BF16),
                v((8, qw), F32),
                v((8, qw), F32),
                v((qw // HDIM, span, span), F32),
                v((3, span, qw), F32),
                v((8, qw), F32),
                v((span, qw), F32),
                v((PLANE, toks, qw), BF16),
                v((PLANE, toks, qw), BF16),
                pltpu.SemaphoreType.DMA((sems,)),
                pltpu.SemaphoreType.DMA((sems,)),
            ],
            compiler_params=pltpu.CompilerParams(
                collective_id=0, has_side_effects=True, vmem_limit_bytes=LIMIT
            ),
        )(
            frames, segment_ids, ln_gain, ln_bias, qkv_weight, out_weight, out_bias, adapter, rms_gain, x_weight,
            bc_weight, jnp.transpose(decay), skip_gain,
        )
        return pl.pallas_call(
            place_kernel,
            out_shape=(jax.ShapeDtypeStruct(encoded.shape, BF16), jax.ShapeDtypeStruct(mixed.shape, BF16)),
            in_specs=[VM, VM],
            out_specs=(VM, VM),
        )(encoded, mixed)

    return per_device


def solution(mesh):
    placed = (
        P("tm", "head"),
        P(),
        P(),
        P(),
        P(None, None, "head"),
        P(None, "head"),
        P("head"),
        P("head", None),
        P(),
        P(None, "head"),
        P(None, "head"),
        P("tm", "head"),
        P("head"),
    )
    nt = mesh.shape["tm"]
    body = fused(nt) if mesh.shape["head"] == 2 and nt == 4 * PLANE else per_device
    return jax.shard_map(
        body,
        mesh=mesh,
        in_specs=placed,
        out_specs=(P("tm", "head"), P("tm", "head")),
        check_vma=False,
    )
```
